256 devices in a mesh: facet: 8 (over y, z_hi), tile: 32 (over x, z_lo, core).
Axes of the slice: x: 4, y: 4, z: 8 (z_hi: 2, z_lo: 4; z = z_hi * 4 + z_lo), core: 2. Of those that a mesh axis runs over, the one named last changes fastest.
Arguments:
- sectioned_rows: bfloat16 [8, 512, 2048], P('facet', 'tile'), may hold values from -6 to 6
- reader: int32 [32, 8], P('tile'), may hold values from 0 to 7, each once within a row
- baseline_coords: float32 [8, 2, 512], P(None, None, 'tile'), may hold values from -8 to 8
- subgrid_index: int32 [8, 512], P(None, 'tile'), may hold values from 0 to 127
- stations: int32 [8, 2, 512], P(None, None, 'tile'), may hold values from 0 to 511
- plane_index: int32 [8, 512], P(None, 'tile'), may hold values from 0 to 31
- model_grid: bfloat16 [8, 128, 2048], P('facet', 'tile'), may hold values from -0.1875 to 0.1875
- beam_screens: bfloat16 [8, 512, 2048], P('facet'), may hold values from -3.5 to 3.5
- plane_phase: float32 [32, 1024], replicated, may hold values from -3.140625 to 3.140625
- channel_freq: float32 [1024], replicated, may hold values from 0.25 to 1.75
Outputs:
- residual: float32 [8, 512, 2048], P('facet', 'tile')
- dirty_grid: float32 [8, 128, 2048], P('facet', 'tile')
The draws below stay inside these ranges and needn't reach their ends.
Inputs may be any that keep to these rules, and one draw needn't show every extreme that they name: `reader`: for each run of baselines, each facet group read exactly one block.
All inputs are finite; a program needn't handle non-finite values.
Results may differ from the reference program's by a relative error of at most 0.0033.
Values may be sent and summed in bfloat16 or wider, within the bound.
No kernel may reach another device: no remote copies, remote signals or barrier semaphores. Data moves between devices by JAX's collectives and lax.ppermute only.
A program may use at most 128 MiB of HBM per device.

```python
import math
import jax
import jax.numpy as jnp
import numpy as np
from jax import lax

EDGE = 32
PIXELS = 1024
CHANNELS = 1024
STATIONS = 512
PLANES = 32
ROW_DEV = 16
BLOCKS = 8
FACETS = 8
ROWS = 512
SUBGRIDS = 128
N_TILE = 32


def corner_factor():
    cell_ids = jnp.arange(PIXELS, dtype=jnp.int32)
    row_offset = cell_ids // EDGE - EDGE // 2
    col_offset = cell_ids % EDGE - EDGE // 2
    distance = jnp.abs(row_offset) + jnp.abs(col_offset)
    return jnp.where(distance >= 3 * EDGE // 4, 1.0, 0.25).astype(jnp.float32)


def draw_beam_screens(key, part):
    key = jax.random.fold_in(key, 11)
    factor = corner_factor()
    factor = jnp.concatenate([factor, factor])
    values = jnp.clip(0.7 * jax.random.normal(key, (FACETS, STATIONS, 2 * PIXELS), jnp.float32), -3.5, 3.5)
    return (values * factor[None, None, :]).astype(jnp.bfloat16)


def draw_baseline_coords(key, part):
    key = jax.random.fold_in(key, 7)
    sign_key, size_key = jax.random.split(key)
    sign_pick = (2 * jax.random.randint(sign_key, (BLOCKS, 2, ROWS), 0, 2) - 1).astype(jnp.float32)
    magnitude = jax.random.uniform(size_key, (BLOCKS, 2, ROWS), jnp.float32, 6.0, 8.0)
    return (sign_pick * magnitude).astype(jnp.float32)


def set_ends(drawn, rng, least, top_value):
    dims = drawn.shape
    index_at = [jax.random.randint(jax.random.fold_in(rng, axis), (), 0, dims[axis]) for axis in range(len(dims))]
    drawn = drawn.at[tuple(index_at)].set(least)
    longest = dims.index(max(dims))
    index_at[longest] = (index_at[longest] + 1) % dims[longest]
    return drawn.at[tuple(index_at)].set(top_value)


def shard_levels(stream_key, extent, cuts, smallest, top_value):
    gain, own = 1.0, jax.random.fold_in(stream_key, 6)
    for axis_at, shards_of in cuts:
        heights = jnp.exp(jax.random.uniform(jax.random.fold_in(own, axis_at), (shards_of,), jnp.float32, smallest / len(cuts), top_value / len(cuts)))
        gain = gain * jnp.repeat(heights, extent[axis_at] // shards_of).reshape([-1 if axis == axis_at else 1 for axis in range(len(extent))])
    return gain


def cumulative_ranks(amount, slope):
    portions = [(1 << 20) // math.isqrt(standing ** slope) + 1 for standing in range(1, amount + 1)]
    scale = 1 + sum(portions) // (1 << 30)
    return np.cumsum(np.array([max(1, weight // scale) for weight in portions]))


def skewed_ids(rng, shape, amount, slope):
    grid = cumulative_ranks(amount, slope)
    ticket = jax.random.randint(jax.random.fold_in(rng, 1), shape, 0, int(grid[amount - 1]))
    standing = jnp.searchsorted(jnp.asarray(grid, jnp.int32), ticket, side="right")
    return jax.random.permutation(jax.random.fold_in(rng, 2), amount)[standing].astype(jnp.int32)


def scatter_about(rng, shape, width, most, cuts=(), held_as=jnp.bfloat16):
    level = shard_levels(rng, shape, cuts, -0.22, 0.18) if cuts else 1.0
    values = jax.random.normal(rng, shape, jnp.float32) * width * level
    return jnp.minimum(jnp.maximum(values, -most), most).astype(held_as)


def setup_inputs(seed: int = 0) -> dict:
    key_list = jax.random.split(jax.random.key(seed), 11)
    return {
        "sectioned_rows": scatter_about(key_list[0], (BLOCKS, ROWS, 2 * CHANNELS), 1.0, 6.0, ((0, 8), (1, 32))),
        "reader": jax.vmap(lambda own: jax.random.permutation(own, BLOCKS))(jax.random.split(key_list[1], N_TILE)).reshape((N_TILE, BLOCKS)).astype(jnp.int32),
        "baseline_coords": draw_baseline_coords(jax.random.fold_in(key_list[10], 71), 0),
        "subgrid_index": set_ends(skewed_ids(key_list[3], (BLOCKS, ROWS), SUBGRIDS, 2), jax.random.fold_in(key_list[3], 3), 0, SUBGRIDS - 1).astype(jnp.int32),
        "stations": set_ends(jax.random.randint(key_list[4], (BLOCKS, 2, ROWS), 0, STATIONS), jax.random.fold_in(key_list[4], 1), 0, STATIONS - 1).astype(jnp.int32),
        "plane_index": set_ends(jax.random.randint(key_list[5], (BLOCKS, ROWS), 0, PLANES), jax.random.fold_in(key_list[5], 1), 0, PLANES - 1).astype(jnp.int32),
        "model_grid": scatter_about(key_list[6], (FACETS, SUBGRIDS, 2 * PIXELS), PIXELS ** -0.5, 0.1875, ((0, 8), (1, 32))),
        "beam_screens": draw_beam_screens(jax.random.fold_in(key_list[10], 71), 0),
        "plane_phase": jnp.clip(jax.random.uniform(key_list[8], (PLANES, PIXELS), jnp.float32, -3.140625, 3.140625), -3.140625, 3.140625),
        "channel_freq": jnp.clip(jax.random.uniform(key_list[9], (CHANNELS,), jnp.float32, 0.25, 1.75), 0.25, 1.75),
    }


TWO_PI = 2.0 * math.pi

def phasor_tables(coords, channel_freq, edge_cells):
    offsets = (jnp.arange(edge_cells, dtype=jnp.float32) - edge_cells // 2) / edge_cells
    angles = TWO_PI * coords[:, None, None] * offsets[None, :, None] * channel_freq[None, None, :]
    return (jnp.cos(angles).astype(jnp.bfloat16), jnp.sin(angles).astype(jnp.bfloat16))

def north_matrix(north_cos, north_sin):
    upper_half = jnp.concatenate([north_cos, north_sin], axis=2)
    lower_half = jnp.concatenate([-north_sin, north_cos], axis=2)
    return jnp.concatenate([upper_half, lower_half], axis=1)

def screen_parts(screens, station_pair, plane_rows, plane_phase):
    pixels = plane_phase.shape[1]
    station_one = screens[station_pair[0]].astype(jnp.float32)
    station_two = screens[station_pair[1]].astype(jnp.float32)
    one_re, one_im = (station_one[:, :pixels], station_one[:, pixels:])
    two_re, two_im = (station_two[:, :pixels], station_two[:, pixels:])
    pair_re = one_re * two_re + one_im * two_im
    pair_im = one_im * two_re - one_re * two_im
    angles = plane_phase[plane_rows]
    wave_re, wave_im = (jnp.cos(angles), jnp.sin(angles))
    return (pair_re * wave_re - pair_im * wave_im, pair_re * wave_im + pair_im * wave_re)

def degrid_rows(model_rows, screen_re, screen_im, east_cos, east_sin, north_mat):
    row_count = model_rows.shape[0]
    pixels = model_rows.shape[1] // 2
    edge_cells = east_cos.shape[1]
    channels = east_cos.shape[2]
    model_f = model_rows.astype(jnp.float32)
    model_re, model_im = (model_f[:, :pixels], model_f[:, pixels:])
    image_re = screen_re * model_re - screen_im * model_im
    image_im = screen_re * model_im + screen_im * model_re
    operand = jnp.concatenate([image_re.reshape(row_count, edge_cells, edge_cells), image_im.reshape(row_count, edge_cells, edge_cells)], axis=2).astype(jnp.bfloat16)
    inner_sum = jnp.einsum('rxy,ryc->rxc', operand.astype(jnp.float32), north_mat.astype(jnp.float32))
    inner_re, inner_im = (inner_sum[:, :, :channels], inner_sum[:, :, channels:])
    cos_f, sin_f = (east_cos.astype(jnp.float32), east_sin.astype(jnp.float32))
    vis_re = lax.optimization_barrier(jnp.sum(cos_f * inner_re - sin_f * inner_im, axis=1))
    vis_im = lax.optimization_barrier(jnp.sum(cos_f * inner_im + sin_f * inner_re, axis=1))
    return jnp.concatenate([vis_re, vis_im], axis=1)

def grid_rows(resid_rows, screen_re, screen_im, east_cos, east_sin, north_mat, grid_scale):
    row_count = resid_rows.shape[0]
    edge_cells = east_cos.shape[1]
    channels = east_cos.shape[2]
    resid_f = resid_rows.astype(jnp.float32)
    resid_re, resid_im = (resid_f[:, None, :channels], resid_f[:, None, channels:])
    cos_f, sin_f = (east_cos.astype(jnp.float32), east_sin.astype(jnp.float32))
    weighted_re = cos_f * resid_re + sin_f * resid_im
    weighted_im = cos_f * resid_im - sin_f * resid_re
    operand = jnp.concatenate([weighted_re, weighted_im], axis=2).astype(jnp.bfloat16)
    gridded = jnp.einsum('rxc,ryc->rxy', operand.astype(jnp.float32), north_mat.astype(jnp.float32))
    grid_re = gridded[:, :, :edge_cells].reshape(row_count, edge_cells * edge_cells)
    grid_im = gridded[:, :, edge_cells:].reshape(row_count, edge_cells * edge_cells)
    out_re = (screen_re * grid_re + screen_im * grid_im) * grid_scale
    out_im = (screen_re * grid_im - screen_im * grid_re) * grid_scale
    return jnp.concatenate([out_re, out_im], axis=1).astype(jnp.bfloat16)

def reference(sectioned_rows, reader, baseline_coords, subgrid_index, stations, plane_index, model_grid, beam_screens, plane_phase, channel_freq):
    sectioned_runs = sectioned_rows.reshape(BLOCKS, N_TILE, ROW_DEV, 2 * CHANNELS)
    run_ids = jnp.arange(N_TILE, dtype=jnp.int32)
    visible = sectioned_runs[reader.T, run_ids[None, :]].reshape(BLOCKS, ROWS, 2 * CHANNELS)
    grid_scale = 1.0 / math.sqrt(CHANNELS * BLOCKS * ROWS / SUBGRIDS)
    targets = jnp.arange(SUBGRIDS, dtype=jnp.int32)

    def per_block(block_id):
        east_cos, east_sin = phasor_tables(baseline_coords[block_id, 0], channel_freq, EDGE)
        north_cos, north_sin = phasor_tables(baseline_coords[block_id, 1], channel_freq, EDGE)
        north_mat = north_matrix(north_cos, north_sin)
        rows_sub = subgrid_index[block_id]
        screens_all = [screen_parts(beam_screens[facet_id], stations[block_id], plane_index[block_id], plane_phase) for facet_id in range(FACETS)]
        predicted = jnp.zeros((ROWS, 2 * CHANNELS), jnp.float32)
        for facet_id in range(FACETS):
            screen_re, screen_im = screens_all[facet_id]
            predicted = predicted + degrid_rows(model_grid[facet_id][rows_sub], screen_re, screen_im, east_cos, east_sin, north_mat)
        resid_block = visible[block_id].astype(jnp.float32) - predicted
        onehot = (targets[:, None] == rows_sub[None, :]).astype(jnp.bfloat16)
        partials = []
        for facet_id in range(FACETS):
            screen_re, screen_im = screens_all[facet_id]
            regridded = grid_rows(resid_block, screen_re, screen_im, east_cos, east_sin, north_mat, grid_scale)
            partials.append(jnp.dot(onehot, regridded, preferred_element_type=jnp.float32))
        return (resid_block, jnp.stack(partials))
    residual, partials = lax.map(per_block, jnp.arange(BLOCKS, dtype=jnp.int32))
    return (residual, lax.optimization_barrier(jnp.sum(partials, axis=0)))
```

```python
import math

import jax
import jax.numpy as jnp
from jax import lax
from jax.experimental import pallas as pl
from jax.experimental.pallas import tpu as pltpu
from jax.sharding import Mesh
from jax.sharding import PartitionSpec as P

TWO_PI = 2.0 * math.pi
F32 = jnp.float32
BF16 = jnp.bfloat16
FACET = ("y", "h")
TILE = ("x", "z", "c")
VMEM = pl.BlockSpec(memory_space=pltpu.VMEM)


def params(mib):
    return pltpu.CompilerParams(vmem_limit_bytes=mib << 20)


def cmul(a, b):
    return (a[0] * b[0] - a[1] * b[1], a[0] * b[1] + a[1] * b[0])


def conj(a):
    return (a[0], -a[1])


def onehot_rows(column, count):
    lanes = lax.broadcasted_iota(jnp.int32, (column.shape[0], count), 1)
    return jnp.where(column == lanes, 1.0, 0.0).astype(BF16)


def screen_kernel(index_ref, phase_ref, beam_ref, screen_ref):
    stations = beam_ref.shape[0]
    planes, pixels = phase_ref.shape
    one = onehot_rows(index_ref[:, 0:1], stations)
    two = onehot_rows(index_ref[:, 1:2], stations)
    plane = onehot_rows(index_ref[:, 2:3], planes).astype(F32)
    width = 256
    for at in range(0, pixels, width):
        re, im = pl.ds(at, width), pl.ds(pixels + at, width)
        one_re = jnp.dot(one, beam_ref[:, re], preferred_element_type=F32)
        one_im = jnp.dot(one, beam_ref[:, im], preferred_element_type=F32)
        two_re = jnp.dot(two, beam_ref[:, re], preferred_element_type=F32)
        two_im = jnp.dot(two, beam_ref[:, im], preferred_element_type=F32)
        pair_re = one_re * two_re + one_im * two_im
        pair_im = one_im * two_re - one_re * two_im
        phase = phase_ref[:, re]
        exact = lax.Precision.HIGHEST
        wave_re = jnp.dot(plane, jnp.cos(phase), precision=exact, preferred_element_type=F32)
        wave_im = jnp.dot(plane, jnp.sin(phase), precision=exact, preferred_element_type=F32)
        screen_ref[:, re] = pair_re * wave_re - pair_im * wave_im
        screen_ref[:, im] = pair_re * wave_im + pair_im * wave_re


def table_kernel(coords_ref, freq_ref, east_ref, north_re_ref, north_im_ref, *powers):
    rows = coords_ref.shape[0] // 2
    angle = (TWO_PI * coords_ref[...]) * (1.0 / 32.0) * freq_ref[...]
    z1 = (jnp.cos(angle), jnp.sin(angle))
    z2 = cmul(z1, z1)
    z4 = cmul(z2, z2)
    z8 = cmul(z4, z4)
    z16 = cmul(z8, z8)
    low16 = conj(z16)
    for at, value in enumerate((z1, z2, z4, z8, z16)):
        powers[0][2 * at] = value[0]
        powers[0][2 * at + 1] = value[1]
    for at, value in enumerate((low16, cmul(low16, z1), cmul(low16, z2), cmul(low16, cmul(z1, z2)))):
        powers[1][2 * at] = value[0]
        powers[1][2 * at + 1] = value[1]
    sub = lax.broadcasted_iota(jnp.int32, (8, angle.shape[1]), 0)

    def row_of(ref, at, row):
        return (ref[2 * at, pl.ds(row, 1), :], ref[2 * at + 1, pl.ds(row, 1), :])

    def picked(factor, bit):
        on = (sub & bit) != 0
        return (jnp.where(on, factor[0], 1.0), jnp.where(on, factor[1], 0.0))

    def bits(factors):
        return cmul(cmul(picked(factors[0], 1), picked(factors[1], 2)), picked(factors[2], 4))

    def body(b, carry):
        base = bits([row_of(powers[0], at, b) for at in (2, 3, 4)])
        parts = [cmul(base, row_of(powers[1], at, b)) for at in range(4)]
        cos = jnp.concatenate([part[0] for part in parts], axis=0)
        sin = jnp.concatenate([part[1] for part in parts], axis=0)
        east_ref[b] = jnp.concatenate([cos, sin], axis=0).astype(BF16)
        row = b + rows
        base = bits([row_of(powers[0], at, row) for at in (0, 1, 2)])
        up8 = row_of(powers[0], 3, row)
        parts = [cmul(base, row_of(powers[1], 0, row)), cmul(base, conj(up8)), base, cmul(base, up8)]
        cos = jnp.concatenate([part[0] for part in parts], axis=0)
        sin = jnp.concatenate([part[1] for part in parts], axis=0)
        north_re_ref[b] = jnp.concatenate([cos, -sin], axis=0).astype(BF16)
        north_im_ref[b] = jnp.concatenate([sin, cos], axis=0).astype(BF16)
        return carry

    lax.fori_loop(0, rows, body, 0)


def image_kernel(index_ref, near_ref, far_ref, screen_ref, image_ref):
    half = near_ref.shape[0]
    pixels = screen_ref.shape[1] // 2
    blocks = image_ref.shape[0]
    slots = onehot_rows(index_ref[:, 3:4], 2 * half)
    near, far = (slots[:, :half], slots[:, half:])
    tiles = pixels // 128
    width = 256

    def rows_of(cells):
        return jnp.dot(near, near_ref[:, cells], preferred_element_type=F32) + jnp.dot(
            far, far_ref[:, cells], preferred_element_type=F32
        )

    for at in range(0, pixels, width):
        re, im = pl.ds(at, width), pl.ds(pixels + at, width)
        model_re, model_im = (rows_of(re), rows_of(im))
        screen_re, screen_im = (screen_ref[:, re], screen_ref[:, im])
        image_re = (screen_re * model_re - screen_im * model_im).astype(BF16)
        image_im = (screen_re * model_im + screen_im * model_re).astype(BF16)
        for off in range(0, width, 128):
            q = (at + off) // 128
            image_ref[:, 16 * q : 16 * q + 16, :] = image_re[:, off : off + 128].reshape(blocks, 16, 128)
            q = q + tiles
            image_ref[:, 16 * q : 16 * q + 16, :] = image_im[:, off : off + 128].reshape(blocks, 16, 128)


def visibility_kernel(
    images_ref, visible_ref, east_ref, north_re_ref, north_im_ref, resid_ref, grid_ref, cells_ref, out_ref
):
    rows, channels = (resid_ref.shape[0], resid_ref.shape[1] // 2)
    facets = images_ref.shape[0]
    total = images_ref[0].astype(F32)
    for at in range(1, facets):
        total = total + images_ref[at].astype(F32)
    cells_ref[...] = total
    resid_ref[...] = visible_ref[...].astype(F32)
    width = 256

    def degrid(b, carry):
        cells = cells_ref[pl.ds(b, 16, stride=16), :]
        pieces = [
            jnp.concatenate(
                [cells[0:8, 32 * p : 32 * p + 32], cells[8:16, 32 * p : 32 * p + 32]], axis=1
            )
            for p in range(4)
        ]
        image = jnp.concatenate(pieces, axis=0)
        high = image.astype(BF16)
        low = (image - high.astype(F32)).astype(BF16)
        operand = jnp.concatenate([high, low], axis=0)
        for at in range(0, channels, width):
            chans = pl.ds(at, width)
            inner_re = jnp.dot(operand, north_re_ref[b, :, chans], preferred_element_type=F32)
            inner_im = jnp.dot(operand, north_im_ref[b, :, chans], preferred_element_type=F32)
            inner_re = inner_re[:32] + inner_re[32:]
            inner_im = inner_im[:32] + inner_im[32:]
            east = east_ref[b, :, chans].astype(F32)
            cos, sin = (east[:32], east[32:])
            vis_re = jnp.sum(cos * inner_re - sin * inner_im, axis=0, keepdims=True)
            vis_im = jnp.sum(cos * inner_im + sin * inner_re, axis=0, keepdims=True)
            row = pl.ds(b, 1)
            late = pl.ds(channels + at, width)
            resid_ref[row, chans] = resid_ref[row, chans] - vis_re
            resid_ref[row, late] = resid_ref[row, late] - vis_im
        return carry

    def grid(b, carry):
        gridded = jnp.zeros((32, 64), F32)
        over = (((1,), (1,)), ((), ()))
        for at in range(0, channels, width):
            chans, late = (pl.ds(at, width), pl.ds(channels + at, width))
            resid_re, resid_im = (resid_ref[pl.ds(b, 1), chans], resid_ref[pl.ds(b, 1), late])
            east = east_ref[b, :, chans].astype(F32)
            cos, sin = (east[:32], east[32:])
            weighted_re = (cos * resid_re + sin * resid_im).astype(BF16)
            weighted_im = (cos * resid_im - sin * resid_re).astype(BF16)
            gridded = gridded + lax.dot_general(
                weighted_re, north_re_ref[b, :, chans], over, preferred_element_type=F32
            )
            gridded = gridded + lax.dot_general(
                weighted_im, north_im_ref[b, :, chans], over, preferred_element_type=F32
            )
        halves = [
            jnp.concatenate([gridded[8 * p : 8 * p + 8, at : at + 32] for p in range(4)], axis=1)
            for at in (0, 32)
        ]
        out_ref[pl.ds(b, 16, stride=16), :] = jnp.concatenate(halves, axis=0)
        return carry

    lax.fori_loop(0, rows, degrid, 0, unroll=4)
    lax.fori_loop(0, rows, grid, 0, unroll=4)
    packed = out_ref[...].astype(BF16)
    for at in range(facets):
        grid_ref[at] = packed


def regrid_kernel(scale, target_ref, grid_ref, screen_ref, near_ref, far_ref):
    half = near_ref.shape[0]
    pixels = screen_ref.shape[1] // 2
    tiles = pixels // 128
    count = screen_ref.shape[0]
    subs = lax.broadcasted_iota(jnp.int32, (2 * half, count), 0)
    onehot = jnp.where(target_ref[...] == subs, 1.0, 0.0).astype(BF16)
    near, far = (onehot[:half], onehot[half:])
    for q in range(tiles):
        re, im = pl.ds(128 * q, 128), pl.ds(pixels + 128 * q, 128)
        grid_re = grid_ref[:, 16 * q : 16 * q + 16, :].reshape(count, 128).astype(F32)
        grid_im = grid_ref[:, 16 * (q + tiles) : 16 * (q + tiles) + 16, :].reshape(count, 128).astype(F32)
        screen_re, screen_im = (screen_ref[:, re], screen_ref[:, im])
        out_re = (screen_re * grid_re + screen_im * grid_im) * scale
        out_im = (screen_re * grid_im - screen_im * grid_re) * scale
        for cells, value in ((re, out_re), (im, out_im)):
            high = value.astype(BF16)
            low = (value - high.astype(F32)).astype(BF16)
            near_ref[:, cells] = jnp.dot(near, high, preferred_element_type=F32) + jnp.dot(
                near, low, preferred_element_type=F32
            )
            far_ref[:, cells] = jnp.dot(far, high, preferred_element_type=F32) + jnp.dot(
                far, low, preferred_element_type=F32
            )


def shift(value, axis, by):
    size = lax.axis_size(axis)
    return lax.ppermute(value, axis, [(i, (i + by) % size) for i in range(size)])


def local(
    sectioned_rows,
    reader,
    baseline_coords,
    subgrid_index,
    stations,
    plane_index,
    model_grid,
    beam_screens,
    plane_phase,
    channel_freq,
):
    n_y, n_h, n_x, n_z, n_c = (lax.axis_size(axis) for axis in FACET + TILE)
    at_y, at_h, at_x, at_z, at_c = (lax.axis_index(axis) for axis in FACET + TILE)
    n_facet = n_y * n_h
    facet_id = at_y * n_h + at_h
    channels = channel_freq.shape[0]
    planes, pixels = plane_phase.shape
    row_block = sectioned_rows.shape[1]
    count = n_facet * row_block
    owned = model_grid.shape[1]
    subgrid_count = owned * n_x * n_z * n_c
    grid_scale = 1.0 / math.sqrt(channels * n_facet * (row_block * n_x * n_z * n_c) / subgrid_count)

    with jax.named_scope("model_gather"):
        own = model_grid[0]
        column = jnp.concatenate([own] + [shift(own, "z", by) for by in range(1, n_z)], axis=0)
        near = jnp.concatenate([column] + [shift(column, "x", by) for by in range(1, n_x)], axis=0)
        far = shift(near, "c", 1)

    with jax.named_scope("visible_route"):
        rows = sectioned_rows[0]
        other = shift(rows, "h", 1)
        read_by = reader[0]
        block_of = jnp.sum(
            jnp.where(
                read_by[None, :] == jnp.arange(n_facet, dtype=jnp.int32)[:, None],
                jnp.arange(n_facet, dtype=jnp.int32)[None, :],
                0,
            ),
            axis=1,
        )
        mine_to = block_of[facet_id]
        source = read_by[facet_id]
        visible = jnp.where(source // n_h == at_y, jnp.where(source % n_h == at_h, rows, other), 0)
        for by in range(1, n_y):
            to = ((at_y + by) % n_y) * n_h + at_h
            came = shift(jnp.where(mine_to == to, rows, other), "y", by)
            visible = jnp.where((source // n_h + by) % n_y == at_y, came, visible)

    sub = subgrid_index.reshape(count)
    sub_row, sub_c = (sub % owned, (sub // owned) % n_c)
    sub_z, sub_x = ((sub // (owned * n_c)) % n_z, sub // (owned * n_c * n_z))
    core = (sub_c - at_c) % n_c
    slot = ((core * n_x + (at_x - sub_x) % n_x) * n_z + (at_z - sub_z) % n_z) * owned + sub_row
    target = ((core * n_x + sub_x) * n_z + sub_z) * owned + sub_row
    index = jnp.stack(
        [stations[:, 0].reshape(count), stations[:, 1].reshape(count), plane_index.reshape(count), slot], axis=1
    )

    screen = pl.pallas_call(
        screen_kernel,
        out_shape=jax.ShapeDtypeStruct((count, 2 * pixels), F32),
        in_specs=[VMEM] * 3,
        out_specs=VMEM,
        compiler_params=params(32),
        cost_estimate=pl.CostEstimate(flops=10**9, bytes_accessed=4 << 20, transcendentals=1 << 16),
        name="screens",
    )(index, plane_phase, beam_screens[0])

    coords = lax.dynamic_index_in_dim(baseline_coords, facet_id, 0, keepdims=False).reshape(2 * row_block, 1)
    east, north_re, north_im = pl.pallas_call(
        table_kernel,
        out_shape=[jax.ShapeDtypeStruct((row_block, 64, channels), BF16)] * 3,
        in_specs=[VMEM] * 2,
        out_specs=[VMEM] * 3,
        scratch_shapes=[
            pltpu.VMEM((10, 2 * row_block, channels), F32),
            pltpu.VMEM((8, 2 * row_block, channels), F32),
        ],
        compiler_params=params(32),
        cost_estimate=pl.CostEstimate(flops=10**8, bytes_accessed=6 << 20, transcendentals=1 << 16),
        name="tables",
    )(coords, channel_freq.reshape(1, channels))

    images = pl.pallas_call(
        image_kernel,
        out_shape=jax.ShapeDtypeStruct((n_facet, 2 * pixels // 128 * row_block, 128), BF16),
        in_specs=[VMEM] * 4,
        out_specs=VMEM,
        compiler_params=params(32),
        cost_estimate=pl.CostEstimate(flops=10**8, bytes_accessed=2 << 20, transcendentals=0),
        name="images",
    )(index, near, far, screen)

    arrived = lax.all_to_all(images, FACET, split_axis=0, concat_axis=0, tiled=True)

    cell_rows = 2 * pixels // 128 * row_block
    residual, gridded = pl.pallas_call(
        visibility_kernel,
        out_shape=[
            jax.ShapeDtypeStruct((row_block, 2 * channels), F32),
            jax.ShapeDtypeStruct((n_facet, cell_rows, 128), BF16),
        ],
        in_specs=[VMEM] * 5,
        out_specs=[VMEM] * 2,
        scratch_shapes=[pltpu.VMEM((cell_rows, 128), F32), pltpu.VMEM((cell_rows, 128), F32)],
        compiler_params=params(48),
        cost_estimate=pl.CostEstimate(flops=10**9, bytes_accessed=8 << 20, transcendentals=0),
        name="visibilities",
    )(arrived, visible, east, north_re, north_im)

    gathered = lax.all_to_all(gridded, FACET, split_axis=0, concat_axis=0, tiled=True)

    half = subgrid_count // n_c
    near_sum, far_sum = pl.pallas_call(
        lambda *refs: regrid_kernel(grid_scale, *refs),
        out_shape=[jax.ShapeDtypeStruct((half, 2 * pixels), F32)] * 2,
        in_specs=[VMEM] * 3,
        out_specs=[VMEM] * 2,
        compiler_params=params(32),
        cost_estimate=pl.CostEstimate(flops=10**8, bytes_accessed=3 << 20, transcendentals=0),
        name="regrid",
    )(target.reshape(1, count), gathered, screen)

    with jax.named_scope("dirty_scatter"):
        chip_sum = (near_sum + shift(far_sum, "c", 1)).astype(BF16).reshape(n_x * n_z, owned, 2 * pixels)
        chips = lax.all_to_all(chip_sum, ("x", "z"), split_axis=0, concat_axis=0, tiled=True)
        dirty = jnp.sum(chips.astype(F32), axis=0)
    return (residual[None], dirty[None])


def solution(mesh):
    split = Mesh(mesh.devices.reshape(4, 2, 4, 4, 2), FACET + TILE)
    return jax.shard_map(
        local,
        mesh=split,
        in_specs=(
            P(FACET, TILE, None),
            P(TILE, None),
            P(None, None, TILE),
            P(None, TILE),
            P(None, None, TILE),
            P(None, TILE),
            P(FACET, TILE, None),
            P(FACET, None, None),
            P(),
            P(),
        ),
        out_specs=(P(FACET, TILE, None), P(FACET, TILE, None)),
        check_vma=False,
    )
```

```python
import functools
import math

import jax
import jax.numpy as jnp
from jax import lax
from jax.experimental import pallas as pl
from jax.experimental.pallas import tpu as pltpu
from jax.sharding import Mesh
from jax.sharding import PartitionSpec as P

TWO_PI = 2.0 * math.pi
F32 = jnp.float32
BF16 = jnp.bfloat16
FACET = ("y", "h")
TILE = ("x", "z", "c")
VMEM = pl.BlockSpec(memory_space=pltpu.VMEM)
SMEM = pl.BlockSpec(memory_space=pltpu.SMEM)


def params(mib):
    return pltpu.CompilerParams(vmem_limit_bytes=mib << 20)


def cmul(a, b):
    return (a[0] * b[0] - a[1] * b[1], a[0] * b[1] + a[1] * b[0])


def conj(a):
    return (a[0], -a[1])


def row_of_blocks(values):
    return jnp.concatenate([values[at : at + 1, :] for at in range(values.shape[0])], axis=1)


def down(row):
    return jnp.broadcast_to(row, (128, 128)).T


def onehot(column, first, count):
    lanes = lax.broadcasted_iota(jnp.int32, (128, 128), 1)
    width = min(count, 128)
    parts = [
        jnp.where(column == lanes + (first + at), 1.0, 0.0).astype(BF16)[:, :width] for at in range(0, count, 128)
    ]
    return parts[0] if len(parts) == 1 else jnp.concatenate(parts, axis=1)


def slot_of(subgrid, core, cores, owned):
    held = lax.rem(lax.div(subgrid, owned) + (cores - core), cores)
    return (held * (128 // cores)) + lax.div(subgrid, owned * cores) * owned + lax.rem(subgrid, owned)


def screen_kernel(stations_ref, plane_ref, phase_ref, beam_ref, screen_ref):
    stations = beam_ref.shape[0]
    planes, pixels = phase_ref.shape
    one = onehot(down(row_of_blocks(stations_ref[:, 0, :])), 0, stations)
    two = onehot(down(row_of_blocks(stations_ref[:, 1, :])), 0, stations)
    plane = onehot(down(row_of_blocks(plane_ref[...])), 0, planes).astype(F32)
    width = 256
    for at in range(0, pixels, width):
        re, im = pl.ds(at, width), pl.ds(pixels + at, width)
        one_re = jnp.dot(one, beam_ref[:, re], preferred_element_type=F32)
        one_im = jnp.dot(one, beam_ref[:, im], preferred_element_type=F32)
        two_re = jnp.dot(two, beam_ref[:, re], preferred_element_type=F32)
        two_im = jnp.dot(two, beam_ref[:, im], preferred_element_type=F32)
        pair_re = one_re * two_re + one_im * two_im
        pair_im = one_im * two_re - one_re * two_im
        phase = phase_ref[:, re]
        exact = lax.Precision.HIGHEST
        wave_re = jnp.dot(plane, jnp.cos(phase), precision=exact, preferred_element_type=F32)
        wave_im = jnp.dot(plane, jnp.sin(phase), precision=exact, preferred_element_type=F32)
        screen_ref[:, re] = pair_re * wave_re - pair_im * wave_im
        screen_ref[:, im] = pair_re * wave_im + pair_im * wave_re


def table_kernel(place_ref, coords_ref, freq_ref, east_ref, north_re_ref, north_im_ref, *powers):
    rows = coords_ref.shape[2]
    coords = coords_ref[place_ref[0]]
    row = jnp.concatenate([coords[0:1], coords[1:2], jnp.zeros((1, 128 - 2 * rows), F32)], axis=1)
    column = (TWO_PI * down(row)[: 2 * rows]) * (1.0 / 32.0)
    angle = jnp.concatenate([column] * (freq_ref.shape[1] // 128), axis=1) * freq_ref[...]
    z1 = (jnp.cos(angle), jnp.sin(angle))
    z2 = cmul(z1, z1)
    z4 = cmul(z2, z2)
    z8 = cmul(z4, z4)
    z16 = cmul(z8, z8)
    low16 = conj(z16)
    for at, value in enumerate((z1, z2, z4, z8, z16)):
        powers[0][2 * at] = value[0]
        powers[0][2 * at + 1] = value[1]
    for at, value in enumerate((low16, cmul(low16, z1), cmul(low16, z2), cmul(low16, cmul(z1, z2)))):
        powers[1][2 * at] = value[0]
        powers[1][2 * at + 1] = value[1]
    sub = lax.broadcasted_iota(jnp.int32, (8, angle.shape[1]), 0)

    def row_of(ref, at, row):
        return (ref[2 * at, pl.ds(row, 1), :], ref[2 * at + 1, pl.ds(row, 1), :])

    def picked(factor, bit):
        on = (sub & bit) != 0
        return (jnp.where(on, factor[0], 1.0), jnp.where(on, factor[1], 0.0))

    def bits(factors):
        return cmul(cmul(picked(factors[0], 1), picked(factors[1], 2)), picked(factors[2], 4))

    def body(b, carry):
        base = bits([row_of(powers[0], at, b) for at in (2, 3, 4)])
        parts = [cmul(base, row_of(powers[1], at, b)) for at in range(4)]
        cos = jnp.concatenate([part[0] for part in parts], axis=0)
        sin = jnp.concatenate([part[1] for part in parts], axis=0)
        east_ref[b] = jnp.concatenate([cos, sin], axis=0).astype(BF16)
        row = b + rows
        base = bits([row_of(powers[0], at, row) for at in (0, 1, 2)])
        up8 = row_of(powers[0], 3, row)
        parts = [cmul(base, row_of(powers[1], 0, row)), cmul(base, conj(up8)), base, cmul(base, up8)]
        cos = jnp.concatenate([part[0] for part in parts], axis=0)
        sin = jnp.concatenate([part[1] for part in parts], axis=0)
        north_re_ref[b] = jnp.concatenate([cos, -sin], axis=0).astype(BF16)
        north_im_ref[b] = jnp.concatenate([sin, cos], axis=0).astype(BF16)
        return carry

    lax.fori_loop(0, rows, body, 0)


def image_kernel(cores, owned, place_ref, subgrid_ref, near_ref, far_ref, screen_ref, image_ref):
    half = near_ref.shape[0]
    pixels = screen_ref.shape[1] // 2
    blocks = image_ref.shape[0]
    slots = down(slot_of(row_of_blocks(subgrid_ref[...]), place_ref[3], cores, owned))
    near, far = (onehot(slots, 0, half), onehot(slots, half, half))
    tiles = pixels // 128
    width = 256

    def rows_of(cells):
        return jnp.dot(near, near_ref[:, cells], preferred_element_type=F32) + jnp.dot(
            far, far_ref[:, cells], preferred_element_type=F32
        )

    for at in range(0, pixels, width):
        re, im = pl.ds(at, width), pl.ds(pixels + at, width)
        model_re, model_im = (rows_of(re), rows_of(im))
        screen_re, screen_im = (screen_ref[:, re], screen_ref[:, im])
        image_re = (screen_re * model_re - screen_im * model_im).astype(BF16)
        image_im = (screen_re * model_im + screen_im * model_re).astype(BF16)
        for off in range(0, width, 128):
            q = (at + off) // 128
            image_ref[:, 16 * q : 16 * q + 16, :] = image_re[:, off : off + 128].reshape(blocks, 16, 128)
            q = q + tiles
            image_ref[:, 16 * q : 16 * q + 16, :] = image_im[:, off : off + 128].reshape(blocks, 16, 128)


def route_kernel(n_y, n_h, place_ref, reader_ref, rows_ref, other_ref, *out_refs):
    block = jnp.int32(0)
    for at in range(n_y * n_h):
        block = jnp.where(reader_ref[0, at] == place_ref[0], at, block)
    for by, out_ref in enumerate(out_refs, 1):
        to = lax.rem(place_ref[1] + by, n_y) * n_h + place_ref[2]

        @pl.when(block == to)
        def _():
            out_ref[...] = rows_ref[...]

        @pl.when(block != to)
        def _():
            out_ref[...] = other_ref[...]


def visibility_kernel(
    n_y,
    n_h,
    place_ref,
    reader_ref,
    images_ref,
    rows_ref,
    other_ref,
    came_1_ref,
    came_2_ref,
    came_3_ref,
    east_ref,
    north_re_ref,
    north_im_ref,
    resid_ref,
    grid_ref,
    cells_ref,
    out_ref,
):
    rows, channels = (resid_ref.shape[0], resid_ref.shape[1] // 2)
    facets = images_ref.shape[0]
    total = images_ref[0].astype(F32)
    for at in range(1, facets):
        total = total + images_ref[at].astype(F32)
    cells_ref[...] = total
    source = reader_ref[0, place_ref[0]]
    steps = lax.rem(place_ref[1] + n_y - lax.div(source, n_h), n_y)
    here = jnp.where(lax.rem(source, n_h) == place_ref[2], 0, 1)
    pick = jnp.where(steps == 0, here, steps + 1)
    for at, ref in enumerate((rows_ref, other_ref, came_1_ref, came_2_ref, came_3_ref)):

        @pl.when(pick == at)
        def _():
            resid_ref[...] = ref[...].astype(F32)

    width = 256

    def degrid(b, carry):
        cells = cells_ref[pl.ds(b, 16, stride=16), :]
        pieces = [
            jnp.concatenate(
                [cells[0:8, 32 * p : 32 * p + 32], cells[8:16, 32 * p : 32 * p + 32]], axis=1
            )
            for p in range(4)
        ]
        image = jnp.concatenate(pieces, axis=0)
        high = image.astype(BF16)
        low = (image - high.astype(F32)).astype(BF16)
        operand = jnp.concatenate([high, low], axis=0)
        for at in range(0, channels, width):
            chans = pl.ds(at, width)
            inner_re = jnp.dot(operand, north_re_ref[b, :, chans], preferred_element_type=F32)
            inner_im = jnp.dot(operand, north_im_ref[b, :, chans], preferred_element_type=F32)
            inner_re = inner_re[:32] + inner_re[32:]
            inner_im = inner_im[:32] + inner_im[32:]
            east = east_ref[b, :, chans].astype(F32)
            cos, sin = (east[:32], east[32:])
            vis_re = jnp.sum(cos * inner_re - sin * inner_im, axis=0, keepdims=True)
            vis_im = jnp.sum(cos * inner_im + sin * inner_re, axis=0, keepdims=True)
            row = pl.ds(b, 1)
            late = pl.ds(channels + at, width)
            resid_ref[row, chans] = resid_ref[row, chans] - vis_re
            resid_ref[row, late] = resid_ref[row, late] - vis_im
        return carry

    def grid(b, carry):
        gridded = jnp.zeros((32, 64), F32)
        over = (((1,), (1,)), ((), ()))
        for at in range(0, channels, width):
            chans, late = (pl.ds(at, width), pl.ds(channels + at, width))
            resid_re, resid_im = (resid_ref[pl.ds(b, 1), chans], resid_ref[pl.ds(b, 1), late])
            east = east_ref[b, :, chans].astype(F32)
            cos, sin = (east[:32], east[32:])
            weighted_re = (cos * resid_re + sin * resid_im).astype(BF16)
            weighted_im = (cos * resid_im - sin * resid_re).astype(BF16)
            gridded = gridded + lax.dot_general(
                weighted_re, north_re_ref[b, :, chans], over, preferred_element_type=F32
            )
            gridded = gridded + lax.dot_general(
                weighted_im, north_im_ref[b, :, chans], over, preferred_element_type=F32
            )
        halves = [
            jnp.concatenate([gridded[8 * p : 8 * p + 8, at : at + 32] for p in range(4)], axis=1)
            for at in (0, 32)
        ]
        out_ref[pl.ds(b, 16, stride=16), :] = jnp.concatenate(halves, axis=0)
        return carry

    lax.fori_loop(0, rows, degrid, 0, unroll=4)
    lax.fori_loop(0, rows, grid, 0, unroll=4)
    grid_ref[...] = out_ref[...].astype(BF16)


def regrid_kernel(scale, n_y, n_h, cores, owned, place_ref, subgrid_ref, screen_ref, *refs):
    grids, (near_ref, far_ref, grid_ref) = (refs[:-3], refs[-3:])
    for at, ref in enumerate(grids):
        by, flip = divmod(at, n_h)
        block = lax.rem(place_ref[1] + (n_y - by), n_y) * n_h + lax.rem(place_ref[2] + flip, n_h)
        grid_ref[block] = ref[...]
    half = near_ref.shape[0]
    pixels = screen_ref.shape[1] // 2
    tiles = pixels // 128
    count = screen_ref.shape[0]
    subs = lax.broadcasted_iota(jnp.int32, (2 * half, count), 0)
    target = slot_of(row_of_blocks(subgrid_ref[...]), place_ref[3], cores, owned)
    sums = jnp.where(target == subs, 1.0, 0.0).astype(BF16)
    near, far = (sums[:half], sums[half:])
    for q in range(tiles):
        re, im = pl.ds(128 * q, 128), pl.ds(pixels + 128 * q, 128)
        grid_re = grid_ref[:, 16 * q : 16 * q + 16, :].reshape(count, 128).astype(F32)
        grid_im = grid_ref[:, 16 * (q + tiles) : 16 * (q + tiles) + 16, :].reshape(count, 128).astype(F32)
        screen_re, screen_im = (screen_ref[:, re], screen_ref[:, im])
        out_re = (screen_re * grid_re + screen_im * grid_im) * scale
        out_im = (screen_re * grid_im - screen_im * grid_re) * scale
        for cells, value in ((re, out_re), (im, out_im)):
            high = value.astype(BF16)
            low = (value - high.astype(F32)).astype(BF16)
            near_ref[:, cells] = jnp.dot(near, high, preferred_element_type=F32) + jnp.dot(
                near, low, preferred_element_type=F32
            )
            far_ref[:, cells] = jnp.dot(far, high, preferred_element_type=F32) + jnp.dot(
                far, low, preferred_element_type=F32
            )


def shift(value, axis, by):
    size = lax.axis_size(axis)
    return lax.ppermute(value, axis, [(i, (i + by) % size) for i in range(size)])


def local(
    sectioned_rows,
    reader,
    baseline_coords,
    subgrid_index,
    stations,
    plane_index,
    model_grid,
    beam_screens,
    plane_phase,
    channel_freq,
):
    n_y, n_h, n_x, n_z, n_c = (lax.axis_size(axis) for axis in FACET + TILE)
    at_y, at_h, at_x, at_z, at_c = (lax.axis_index(axis) for axis in FACET + TILE)
    n_facet = n_y * n_h
    channels = channel_freq.shape[0]
    pixels = plane_phase.shape[1]
    row_block = sectioned_rows.shape[1]
    count = n_facet * row_block
    owned = model_grid.shape[1]
    subgrid_count = owned * n_x * n_z * n_c
    cell_rows = 2 * pixels // 128 * row_block
    grid_scale = 1.0 / math.sqrt(channels * n_facet * (row_block * n_x * n_z * n_c) / subgrid_count)
    ids = jnp.arange(4, dtype=jnp.int32)
    place = jnp.where(
        ids == 0, at_y * n_h + at_h, jnp.where(ids == 1, at_y, jnp.where(ids == 2, at_h, at_c))
    ).astype(jnp.int32)

    with jax.named_scope("model_gather"):
        copies = jnp.broadcast_to(model_grid, (n_x * n_z, owned, 2 * pixels))
        near = lax.all_to_all(copies, ("x", "z"), split_axis=0, concat_axis=0, tiled=True)
        near = near.reshape(n_x * n_z * owned, 2 * pixels)
        far = shift(near, "c", 1)

    screen = pl.pallas_call(
        screen_kernel,
        out_shape=jax.ShapeDtypeStruct((count, 2 * pixels), F32),
        in_specs=[VMEM] * 4,
        out_specs=VMEM,
        compiler_params=params(16),
        cost_estimate=pl.CostEstimate(flops=10**9, bytes_accessed=4 << 20, transcendentals=1 << 16),
        name="screens",
    )(stations, plane_index, plane_phase, beam_screens[0])

    east, north_re, north_im = pl.pallas_call(
        table_kernel,
        out_shape=[jax.ShapeDtypeStruct((row_block, 64, channels), BF16)] * 3,
        in_specs=[SMEM, VMEM, VMEM],
        out_specs=[VMEM] * 3,
        scratch_shapes=[
            pltpu.VMEM((10, 2 * row_block, channels), F32),
            pltpu.VMEM((8, 2 * row_block, channels), F32),
        ],
        compiler_params=params(16),
        cost_estimate=pl.CostEstimate(flops=10**8, bytes_accessed=6 << 20, transcendentals=1 << 16),
        name="tables",
    )(place, baseline_coords, channel_freq.reshape(1, channels))

    with jax.named_scope("visible_route"):
        rows, east = lax.optimization_barrier((sectioned_rows[0], east))
        other = shift(rows, "h", 1)
        sent = pl.pallas_call(
            functools.partial(route_kernel, n_y, n_h),
            out_shape=[jax.ShapeDtypeStruct(rows.shape, BF16)] * (n_y - 1),
            in_specs=[SMEM, SMEM, VMEM, VMEM],
            out_specs=[VMEM] * (n_y - 1),
            compiler_params=params(4),
            cost_estimate=pl.CostEstimate(flops=10**6, bytes_accessed=1 << 18, transcendentals=0),
            name="route",
        )(place, reader, rows, other)

    near, far, screen, east = lax.optimization_barrier((near, far, screen, east))
    images = pl.pallas_call(
        functools.partial(image_kernel, n_c, owned),
        out_shape=jax.ShapeDtypeStruct((n_facet, cell_rows, 128), BF16),
        in_specs=[SMEM] + [VMEM] * 4,
        out_specs=VMEM,
        compiler_params=params(8),
        cost_estimate=pl.CostEstimate(flops=10**8, bytes_accessed=2 << 20, transcendentals=0),
        name="images",
    )(place, subgrid_index, near, far, screen)

    arrived = lax.all_to_all(images, FACET, split_axis=0, concat_axis=0, tiled=True)
    came = [shift(value, "y", by) for by, value in enumerate(sent, 1)]

    residual, gridded = pl.pallas_call(
        functools.partial(visibility_kernel, n_y, n_h),
        out_shape=[
            jax.ShapeDtypeStruct((row_block, 2 * channels), F32),
            jax.ShapeDtypeStruct((cell_rows, 128), BF16),
        ],
        in_specs=[SMEM] * 2 + [VMEM] * 9,
        out_specs=[VMEM] * 2,
        scratch_shapes=[pltpu.VMEM((cell_rows, 128), F32), pltpu.VMEM((cell_rows, 128), F32)],
        compiler_params=params(16),
        cost_estimate=pl.CostEstimate(flops=10**9, bytes_accessed=8 << 20, transcendentals=0),
        name="visibilities",
    )(place, reader, arrived, rows, other, *came, east, north_re, north_im)

    with jax.named_scope("grid_gather"):
        beside = shift(gridded, "h", 1)
        grids = [gridded, beside]
        for by in range(1, n_y):
            grids += [shift(gridded, "y", by), shift(beside, "y", by)]

    half = subgrid_count // n_c
    near_sum, far_sum = pl.pallas_call(
        functools.partial(regrid_kernel, grid_scale, n_y, n_h, n_c, owned),
        out_shape=[jax.ShapeDtypeStruct((half, 2 * pixels), F32)] * 2,
        in_specs=[SMEM] + [VMEM] * (2 + n_facet),
        out_specs=[VMEM] * 2,
        scratch_shapes=[pltpu.VMEM((n_facet, cell_rows, 128), BF16)],
        compiler_params=params(8),
        cost_estimate=pl.CostEstimate(flops=10**8, bytes_accessed=3 << 20, transcendentals=0),
        name="regrid",
    )(place, subgrid_index, screen, *grids)

    with jax.named_scope("dirty_scatter"):
        chip_sum = (near_sum + shift(far_sum, "c", 1)).astype(BF16).reshape(n_x * n_z, owned, 2 * pixels)
        chips = lax.all_to_all(chip_sum, ("x", "z"), split_axis=0, concat_axis=0, tiled=True)
        dirty = jnp.sum(chips.astype(F32), axis=0)
    return (residual[None], dirty[None])


def solution(mesh):
    split = Mesh(mesh.devices.reshape(4, 2, 4, 4, 2), FACET + TILE)
    return jax.shard_map(
        local,
        mesh=split,
        in_specs=(
            P(FACET, TILE, None),
            P(TILE, None),
            P(None, None, TILE),
            P(None, TILE),
            P(None, None, TILE),
            P(None, TILE),
            P(FACET, TILE, None),
            P(FACET, None, None),
            P(),
            P(),
        ),
        out_specs=(P(FACET, TILE, None), P(FACET, TILE, None)),
        check_vma=False,
    )
```

```python
import functools
import math

import jax
import jax.numpy as jnp
from jax import lax
from jax.experimental import pallas as pl
from jax.experimental.pallas import tpu as pltpu
from jax.sharding import Mesh
from jax.sharding import PartitionSpec as P

TWO_PI = 2.0 * math.pi
F32 = jnp.float32
BF16 = jnp.bfloat16
FACET = ("y", "h")
TILE = ("x", "z", "c")
VMEM = pl.BlockSpec(memory_space=pltpu.VMEM)
SMEM = pl.BlockSpec(memory_space=pltpu.SMEM)
ANY = pl.BlockSpec(memory_space=pl.ANY)


def params(mib):
    return pltpu.CompilerParams(vmem_limit_bytes=mib << 20)


def cmul(a, b):
    return (a[0] * b[0] - a[1] * b[1], a[0] * b[1] + a[1] * b[0])


def conj(a):
    return (a[0], -a[1])


def row_of_blocks(values):
    return jnp.concatenate([values[at : at + 1, :] for at in range(values.shape[0])], axis=1)


def down(row):
    return jnp.broadcast_to(row, (128, 128)).T


def onehot(column, first, count):
    lanes = lax.broadcasted_iota(jnp.int32, (128, 128), 1)
    width = min(count, 128)
    parts = [
        jnp.where(column == lanes + (first + at), 1.0, 0.0).astype(BF16)[:, :width] for at in range(0, count, 128)
    ]
    return parts[0] if len(parts) == 1 else jnp.concatenate(parts, axis=1)


def slot_of(subgrid, core, cores, owned):
    held = lax.rem(lax.div(subgrid, owned) + (cores - core), cores)
    return (held * (128 // cores)) + lax.div(subgrid, owned * cores) * owned + lax.rem(subgrid, owned)


def prepare_kernel(place_ref, *refs):
    sources, (east_to, north_to, screen_ref) = (refs[:6], refs[6:9])
    east_ref, north_ref, powers, groups, sems, out_sems = refs[15:]
    copies = [pltpu.make_async_copy(src, dst, sems.at[at]) for at, (src, dst) in enumerate(zip(sources, refs[9:15]))]
    for copy in copies:
        copy.start()
    coords_ref, freq_ref, stations_ref, plane_ref, phase_ref, beam_ref = refs[9:15]
    copies[0].wait()
    copies[1].wait()
    rows = coords_ref.shape[2]
    coords = coords_ref[place_ref[0]]
    row = jnp.concatenate([coords[0:1], coords[1:2], jnp.zeros((1, 128 - 2 * rows), F32)], axis=1)
    column = (TWO_PI * down(row)[: 2 * rows]) * (1.0 / 32.0)
    angle = jnp.concatenate([column] * (freq_ref.shape[1] // 128), axis=1) * freq_ref[...]
    z1 = (jnp.cos(angle), jnp.sin(angle))
    z2 = cmul(z1, z1)
    z4 = cmul(z2, z2)
    z8 = cmul(z4, z4)
    z16 = cmul(z8, z8)
    low16 = conj(z16)
    for at, value in enumerate((z1, z2, z4, z8, z16)):
        powers[2 * at] = value[0]
        powers[2 * at + 1] = value[1]
    for at, value in enumerate((low16, cmul(low16, z1), cmul(low16, z2), cmul(low16, cmul(z1, z2)))):
        groups[2 * at] = value[0]
        groups[2 * at + 1] = value[1]
    sub = lax.broadcasted_iota(jnp.int32, (8, angle.shape[1]), 0)

    def row_of(ref, at, row):
        return (ref[2 * at, pl.ds(row, 1), :], ref[2 * at + 1, pl.ds(row, 1), :])

    def picked(factor, bit):
        on = (sub & bit) != 0
        return (jnp.where(on, factor[0], 1.0), jnp.where(on, factor[1], 0.0))

    def bits(factors):
        return cmul(cmul(picked(factors[0], 1), picked(factors[1], 2)), picked(factors[2], 4))

    def stacked(parts):
        return jnp.concatenate([part[0] for part in parts] + [part[1] for part in parts], axis=0).astype(BF16)

    def body(b, carry):
        base = bits([row_of(powers, at, b) for at in (2, 3, 4)])
        east_ref[b] = stacked([cmul(base, row_of(groups, at, b)) for at in range(4)])
        row = b + rows
        base = bits([row_of(powers, at, row) for at in (0, 1, 2)])
        up8 = row_of(powers, 3, row)
        north_ref[b] = stacked([cmul(base, row_of(groups, 0, row)), cmul(base, conj(up8)), base, cmul(base, up8)])
        return carry

    lax.fori_loop(0, rows, body, 0)
    stores = [
        pltpu.make_async_copy(src, dst, out_sems.at[at])
        for at, (src, dst) in enumerate(((east_ref, east_to), (north_ref, north_to)))
    ]
    for store in stores:
        store.start()

    for copy in copies[2:]:
        copy.wait()
    stations = beam_ref.shape[0]
    planes, pixels = phase_ref.shape
    one = onehot(down(row_of_blocks(stations_ref[:, 0, :])), 0, stations)
    two = onehot(down(row_of_blocks(stations_ref[:, 1, :])), 0, stations)
    plane = onehot(down(row_of_blocks(plane_ref[...])), 0, planes).astype(F32)
    width = 256
    for at in range(0, pixels, width):
        re, im = pl.ds(at, width), pl.ds(pixels + at, width)
        one_re = jnp.dot(one, beam_ref[:, re], preferred_element_type=F32)
        one_im = jnp.dot(one, beam_ref[:, im], preferred_element_type=F32)
        two_re = jnp.dot(two, beam_ref[:, re], preferred_element_type=F32)
        two_im = jnp.dot(two, beam_ref[:, im], preferred_element_type=F32)
        pair_re = one_re * two_re + one_im * two_im
        pair_im = one_im * two_re - one_re * two_im
        phase = phase_ref[:, re]
        exact = lax.Precision.HIGHEST
        wave_re = jnp.dot(plane, jnp.cos(phase), precision=exact, preferred_element_type=F32)
        wave_im = jnp.dot(plane, jnp.sin(phase), precision=exact, preferred_element_type=F32)
        screen_ref[:, re] = pair_re * wave_re - pair_im * wave_im
        screen_ref[:, im] = pair_re * wave_im + pair_im * wave_re
    for store in stores:
        store.wait()


def image_kernel(cores, owned, place_ref, subgrid_ref, near_ref, far_ref, screen_ref, image_ref):
    half = near_ref.shape[0] * near_ref.shape[1]
    pixels = screen_ref.shape[1] // 2
    blocks = image_ref.shape[0]
    slots = down(slot_of(row_of_blocks(subgrid_ref[...]), place_ref[3], cores, owned))
    near, far = (onehot(slots, 0, half), onehot(slots, half, half))
    tiles = pixels // 128
    width = 256

    def rows_of(cells):
        held = (near_ref[:, :, cells].reshape(half, width), far_ref[:, :, cells].reshape(half, width))
        return jnp.dot(near, held[0], preferred_element_type=F32) + jnp.dot(far, held[1], preferred_element_type=F32)

    for at in range(0, pixels, width):
        re, im = pl.ds(at, width), pl.ds(pixels + at, width)
        model_re, model_im = (rows_of(re), rows_of(im))
        screen_re, screen_im = (screen_ref[:, re], screen_ref[:, im])
        image_re = (screen_re * model_re - screen_im * model_im).astype(BF16)
        image_im = (screen_re * model_im + screen_im * model_re).astype(BF16)
        for off in range(0, width, 128):
            q = (at + off) // 128
            image_ref[:, 16 * q : 16 * q + 16, :] = image_re[:, off : off + 128].reshape(blocks, 16, 128)
            q = q + tiles
            image_ref[:, 16 * q : 16 * q + 16, :] = image_im[:, off : off + 128].reshape(blocks, 16, 128)


def route_kernel(n_y, n_h, place_ref, reader_ref, rows_ref, other_ref, *out_refs):
    block = jnp.int32(0)
    for at in range(n_y * n_h):
        block = jnp.where(reader_ref[0, at] == place_ref[0], at, block)
    for by, out_ref in enumerate(out_refs, 1):
        to = lax.rem(place_ref[1] + by, n_y) * n_h + place_ref[2]

        @pl.when(block == to)
        def _():
            out_ref[...] = rows_ref[...]

        @pl.when(block != to)
        def _():
            out_ref[...] = other_ref[...]


def visibility_kernel(
    n_y,
    n_h,
    place_ref,
    reader_ref,
    images_ref,
    rows_ref,
    other_ref,
    came_1_ref,
    came_2_ref,
    came_3_ref,
    east_from,
    north_from,
    resid_ref,
    grid_ref,
    cells_ref,
    out_ref,
    east_ref,
    north_ref,
    sems,
):
    rows, channels = (resid_ref.shape[0], resid_ref.shape[1] // 2)
    facets = images_ref.shape[0]

    run = rows // 4
    copies = [
        [
            pltpu.make_async_copy(src.at[pl.ds(at * run, run)], dst.at[pl.ds(at * run, run)], sems.at[kind, at])
            for kind, (src, dst) in enumerate(((east_from, east_ref), (north_from, north_ref)))
        ]
        for at in range(4)
    ]
    for pair in copies:
        for copy in pair:
            copy.start()
    total = images_ref[0].astype(F32)
    for at in range(1, facets):
        total = total + images_ref[at].astype(F32)
    cells_ref[...] = total
    source = reader_ref[0, place_ref[0]]
    steps = lax.rem(place_ref[1] + n_y - lax.div(source, n_h), n_y)
    here = jnp.where(lax.rem(source, n_h) == place_ref[2], 0, 1)
    pick = jnp.where(steps == 0, here, steps + 1)
    for at, ref in enumerate((rows_ref, other_ref, came_1_ref, came_2_ref, came_3_ref)):

        @pl.when(pick == at)
        def _():
            resid_ref[...] = ref[...].astype(F32)

    width = 256

    def degrid(b):
        cells = cells_ref[pl.ds(b, 16, stride=16), :]

        def spread(first, second):
            return jnp.concatenate(
                [
                    jnp.concatenate([first[:, 32 * p : 32 * p + 32], second[:, 32 * p : 32 * p + 32]], axis=1)
                    for p in range(4)
                ],
                axis=0,
            )

        image = jnp.concatenate([spread(cells[0:8], -cells[8:16]), spread(cells[8:16], cells[0:8])], axis=0)
        high = image.astype(BF16)
        low = (image - high.astype(F32)).astype(BF16)
        operand = jnp.concatenate([high, low], axis=0)
        for at in range(0, channels, width):
            chans = pl.ds(at, width)
            inner = jnp.dot(operand, north_ref[b, :, chans], preferred_element_type=F32)
            inner = inner[:64] + inner[64:]
            inner_re, inner_im = (inner[:32], inner[32:])
            east = east_ref[b, :, chans].astype(F32)
            cos, sin = (east[:32], east[32:])
            vis_re = jnp.sum(cos * inner_re - sin * inner_im, axis=0, keepdims=True)
            vis_im = jnp.sum(cos * inner_im + sin * inner_re, axis=0, keepdims=True)
            row = pl.ds(b, 1)
            late = pl.ds(channels + at, width)
            resid_ref[row, chans] = resid_ref[row, chans] - vis_re
            resid_ref[row, late] = resid_ref[row, late] - vis_im

    def grid(b):
        products = jnp.zeros((64, 64), F32)
        for at in range(0, channels, width):
            chans, late = (pl.ds(at, width), pl.ds(channels + at, width))
            resid_re, resid_im = (resid_ref[pl.ds(b, 1), chans], resid_ref[pl.ds(b, 1), late])
            east = east_ref[b, :, chans].astype(F32)
            cos, sin = (east[:32], east[32:])
            weighted = jnp.concatenate([cos * resid_re + sin * resid_im, cos * resid_im - sin * resid_re], axis=0)
            products = products + lax.dot_general(
                weighted.astype(BF16),
                north_ref[b, :, chans],
                (((1,), (1,)), ((), ())),
                preferred_element_type=F32,
            )
        halves = (products[:32, :32] + products[32:, 32:], products[32:, :32] - products[:32, 32:])
        out_ref[pl.ds(b, 16, stride=16), :] = jnp.concatenate(
            [jnp.concatenate([half[8 * p : 8 * p + 8] for p in range(4)], axis=1) for half in halves], axis=0
        )

    for at, pair in enumerate(copies):
        for copy in pair:
            copy.wait()
        for b in range(at * run, at * run + run):
            degrid(b)
    for b in range(rows):
        grid(b)
    grid_ref[...] = out_ref[...].astype(BF16)


def regrid_kernel(scale, n_y, n_h, cores, owned, place_ref, subgrid_ref, screen_ref, *refs):
    grids, (near_ref, far_ref) = (refs[:-2], refs[-2:])
    blocks = []
    for at in range(len(grids)):
        by, flip = divmod(at, n_h)
        blocks.append(lax.rem(place_ref[1] + (n_y - by), n_y) * n_h + lax.rem(place_ref[2] + flip, n_h))
    half = near_ref.shape[0]
    pixels = screen_ref.shape[1] // 2
    tiles = pixels // 128
    count = screen_ref.shape[0]

    def screen_of(cells):
        rows = [screen_ref[pl.ds(pl.multiple_of(block * 16, 16), 16), cells] for block in blocks]
        return jnp.concatenate(rows, axis=0)

    def grid_of(q):
        return jnp.concatenate([ref[16 * q : 16 * q + 16, :] for ref in grids], axis=0).astype(F32)

    subs = lax.broadcasted_iota(jnp.int32, (2 * half, count), 0)
    target = jnp.concatenate([subgrid_ref[pl.ds(block, 1), :] for block in blocks], axis=1)
    target = slot_of(target, place_ref[3], cores, owned)
    sums = jnp.where(target == subs, 1.0, 0.0).astype(BF16)
    near, far = (sums[:half], sums[half:])
    for q in range(tiles):
        re, im = pl.ds(128 * q, 128), pl.ds(pixels + 128 * q, 128)
        grid_re, grid_im = (grid_of(q), grid_of(q + tiles))
        screen_re, screen_im = (screen_of(re), screen_of(im))
        out_re = (screen_re * grid_re + screen_im * grid_im) * scale
        out_im = (screen_re * grid_im - screen_im * grid_re) * scale
        for cells, value in ((re, out_re), (im, out_im)):
            high = value.astype(BF16)
            low = (value - high.astype(F32)).astype(BF16)
            near_ref[:, cells] = jnp.dot(near, high, preferred_element_type=F32) + jnp.dot(
                near, low, preferred_element_type=F32
            )
            far_ref[:, cells] = jnp.dot(far, high, preferred_element_type=F32) + jnp.dot(
                far, low, preferred_element_type=F32
            )


def shift(value, axis, by):
    size = lax.axis_size(axis)
    return lax.ppermute(value, axis, [(i, (i + by) % size) for i in range(size)])


def local(
    sectioned_rows,
    reader,
    baseline_coords,
    subgrid_index,
    stations,
    plane_index,
    model_grid,
    beam_screens,
    plane_phase,
    channel_freq,
):
    n_y, n_h, n_x, n_z, n_c = (lax.axis_size(axis) for axis in FACET + TILE)
    at_y, at_h, at_x, at_z, at_c = (lax.axis_index(axis) for axis in FACET + TILE)
    n_facet = n_y * n_h
    channels = channel_freq.shape[0]
    pixels = plane_phase.shape[1]
    row_block = sectioned_rows.shape[1]
    count = n_facet * row_block
    owned = model_grid.shape[1]
    subgrid_count = owned * n_x * n_z * n_c
    cell_rows = 2 * pixels // 128 * row_block
    grid_scale = 1.0 / math.sqrt(channels * n_facet * (row_block * n_x * n_z * n_c) / subgrid_count)
    ids = jnp.arange(4, dtype=jnp.int32)
    place = jnp.where(
        ids == 0, at_y * n_h + at_h, jnp.where(ids == 1, at_y, jnp.where(ids == 2, at_h, at_c))
    ).astype(jnp.int32)

    with jax.named_scope("model_gather"):
        copies = jnp.broadcast_to(model_grid, (n_x * n_z, owned, 2 * pixels))
        near = lax.all_to_all(copies, ("x", "z"), split_axis=0, concat_axis=0, tiled=True)

    operands = (baseline_coords, channel_freq.reshape(1, channels), stations, plane_index, plane_phase, beam_screens[0])
    east, north, screen = pl.pallas_call(
        prepare_kernel,
        out_shape=[jax.ShapeDtypeStruct((row_block, 64, channels), BF16)] * 2
        + [jax.ShapeDtypeStruct((count, 2 * pixels), F32)],
        in_specs=[SMEM] + [ANY] * len(operands),
        out_specs=[ANY, ANY, VMEM],
        scratch_shapes=[pltpu.VMEM(value.shape, value.dtype) for value in operands]
        + [
            pltpu.VMEM((row_block, 64, channels), BF16),
            pltpu.VMEM((row_block, 64, channels), BF16),
            pltpu.VMEM((10, 2 * row_block, channels), F32),
            pltpu.VMEM((8, 2 * row_block, channels), F32),
            pltpu.SemaphoreType.DMA((len(operands),)),
            pltpu.SemaphoreType.DMA((2,)),
        ],
        compiler_params=params(61),
        cost_estimate=pl.CostEstimate(flops=10**9, bytes_accessed=8 << 20, transcendentals=1 << 17),
        name="prepare",
    )(place, *operands)

    with jax.named_scope("visible_route"):
        rows = sectioned_rows[0]
        other = shift(rows, "h", 1)
        near, other, east, north, screen = lax.optimization_barrier((near, other, east, north, screen))
        far = shift(near, "c", 1)
        sent = pl.pallas_call(
            functools.partial(route_kernel, n_y, n_h),
            out_shape=[jax.ShapeDtypeStruct(rows.shape, BF16)] * (n_y - 1),
            in_specs=[SMEM, SMEM, VMEM, VMEM],
            out_specs=[VMEM] * (n_y - 1),
            compiler_params=params(4),
            cost_estimate=pl.CostEstimate(flops=10**6, bytes_accessed=1 << 18, transcendentals=0),
            name="route",
        )(place, reader, rows, other)

    images = pl.pallas_call(
        functools.partial(image_kernel, n_c, owned),
        out_shape=jax.ShapeDtypeStruct((n_facet, cell_rows, 128), BF16),
        in_specs=[SMEM] + [VMEM] * 4,
        out_specs=VMEM,
        compiler_params=params(8),
        cost_estimate=pl.CostEstimate(flops=10**8, bytes_accessed=2 << 20, transcendentals=0),
        name="images",
    )(place, subgrid_index, near, far, screen)

    arrived = lax.all_to_all(images, FACET, split_axis=0, concat_axis=0, tiled=True)
    came = [shift(value, "y", by) for by, value in enumerate(sent, 1)]

    residual, gridded = pl.pallas_call(
        functools.partial(visibility_kernel, n_y, n_h),
        out_shape=[
            jax.ShapeDtypeStruct((row_block, 2 * channels), F32),
            jax.ShapeDtypeStruct((cell_rows, 128), BF16),
        ],
        in_specs=[SMEM] * 2 + [VMEM] * 6 + [ANY] * 2,
        out_specs=[VMEM] * 2,
        scratch_shapes=[
            pltpu.VMEM((cell_rows, 128), F32),
            pltpu.VMEM((cell_rows, 128), F32),
            pltpu.VMEM(east.shape, BF16),
            pltpu.VMEM(north.shape, BF16),
            pltpu.SemaphoreType.DMA((2, 4)),
        ],
        compiler_params=params(61),
        cost_estimate=pl.CostEstimate(flops=10**9, bytes_accessed=8 << 20, transcendentals=0),
        name="visibilities",
    )(place, reader, arrived, rows, other, *came, east, north)

    with jax.named_scope("grid_gather"):
        beside = shift(gridded, "h", 1)
        grids = [gridded, beside]
        for by in range(1, n_y):
            grids += [shift(gridded, "y", by), shift(beside, "y", by)]

    half = subgrid_count // n_c
    near_sum, far_sum = pl.pallas_call(
        functools.partial(regrid_kernel, grid_scale, n_y, n_h, n_c, owned),
        out_shape=[jax.ShapeDtypeStruct((half, 2 * pixels), F32)] * 2,
        in_specs=[SMEM] + [VMEM] * (2 + n_facet),
        out_specs=[VMEM] * 2,
        compiler_params=params(8),
        cost_estimate=pl.CostEstimate(flops=10**8, bytes_accessed=3 << 20, transcendentals=0),
        name="regrid",
    )(place, subgrid_index, screen, *grids)

    with jax.named_scope("dirty_scatter"):
        chip_sum = (near_sum + shift(far_sum, "c", 1)).astype(BF16).reshape(n_x * n_z, owned, 2 * pixels)
        chips = lax.all_to_all(chip_sum, ("x", "z"), split_axis=0, concat_axis=0, tiled=True)
        dirty = jnp.sum(chips.astype(F32), axis=0)
    return (residual[None], dirty[None])


def solution(mesh):
    split = Mesh(mesh.devices.reshape(4, 2, 4, 4, 2), FACET + TILE)
    return jax.shard_map(
        local,
        mesh=split,
        in_specs=(
            P(FACET, TILE, None),
            P(TILE, None),
            P(None, None, TILE),
            P(None, TILE),
            P(None, None, TILE),
            P(None, TILE),
            P(FACET, TILE, None),
            P(FACET, None, None),
            P(),
            P(),
        ),
        out_specs=(P(FACET, TILE, None), P(FACET, TILE, None)),
        check_vma=False,
    )
```

```python
import functools
import math

import jax
import jax.numpy as jnp
from jax import lax
from jax.experimental import pallas as pl
from jax.experimental.pallas import tpu as pltpu
from jax.sharding import Mesh
from jax.sharding import PartitionSpec as P

TWO_PI = 2.0 * math.pi
F32 = jnp.float32
BF16 = jnp.bfloat16
FACET = ("y", "h")
TILE = ("x", "z", "c")
VMEM = pl.BlockSpec(memory_space=pltpu.VMEM)
SMEM = pl.BlockSpec(memory_space=pltpu.SMEM)
ANY = pl.BlockSpec(memory_space=pl.ANY)


def params(mib):
    return pltpu.CompilerParams(vmem_limit_bytes=mib << 20)


def cmul(a, b):
    return (a[0] * b[0] - a[1] * b[1], a[0] * b[1] + a[1] * b[0])


def conj(a):
    return (a[0], -a[1])


def row_of_blocks(values):
    return jnp.concatenate([values[at : at + 1, :] for at in range(values.shape[0])], axis=1)


def down(row):
    return jnp.broadcast_to(row, (128, 128)).T


def onehot(column, first, count):
    lanes = lax.broadcasted_iota(jnp.int32, (128, 128), 1)
    width = min(count, 128)
    parts = [
        jnp.where(column == lanes + (first + at), 1.0, 0.0).astype(BF16)[:, :width] for at in range(0, count, 128)
    ]
    return parts[0] if len(parts) == 1 else jnp.concatenate(parts, axis=1)


def slot_of(subgrid, core, cores, owned):
    held = lax.rem(lax.div(subgrid, owned) + (cores - core), cores)
    return (held * (128 // cores)) + lax.div(subgrid, owned * cores) * owned + lax.rem(subgrid, owned)


def table_kernel(place_ref, coords_ref, freq_ref, table_ref, powers, groups):
    rows = coords_ref.shape[2]
    coords = coords_ref[place_ref[0]]
    row = jnp.concatenate([coords[0:1], coords[1:2], jnp.zeros((1, 128 - 2 * rows), F32)], axis=1)
    column = (TWO_PI * down(row)[: 2 * rows]) * (1.0 / 32.0)
    angle = jnp.concatenate([column] * (freq_ref.shape[1] // 128), axis=1) * freq_ref[...]
    z1 = (jnp.cos(angle), jnp.sin(angle))
    z2 = cmul(z1, z1)
    z4 = cmul(z2, z2)
    z8 = cmul(z4, z4)
    z16 = cmul(z8, z8)
    low16 = conj(z16)
    for at, value in enumerate((z1, z2, z4, z8, z16)):
        powers[2 * at] = value[0]
        powers[2 * at + 1] = value[1]
    for at, value in enumerate((low16, cmul(low16, z1), cmul(low16, z2), cmul(low16, cmul(z1, z2)))):
        groups[2 * at] = value[0]
        groups[2 * at + 1] = value[1]
    sub = lax.broadcasted_iota(jnp.int32, (8, angle.shape[1]), 0)

    def row_of(ref, at, row):
        return (ref[2 * at, pl.ds(row, 1), :], ref[2 * at + 1, pl.ds(row, 1), :])

    def picked(factor, bit):
        on = (sub & bit) != 0
        return (jnp.where(on, factor[0], 1.0), jnp.where(on, factor[1], 0.0))

    def bits(factors):
        return cmul(cmul(picked(factors[0], 1), picked(factors[1], 2)), picked(factors[2], 4))

    def stacked(parts):
        return jnp.concatenate([part[0] for part in parts] + [part[1] for part in parts], axis=0).astype(BF16)

    def body(b):
        base = bits([row_of(powers, at, b) for at in (2, 3, 4)])
        table_ref[0, b] = stacked([cmul(base, row_of(groups, at, b)) for at in range(4)])
        row = b + rows
        base = bits([row_of(powers, at, row) for at in (0, 1, 2)])
        up8 = row_of(powers, 3, row)
        table_ref[1, b] = stacked(
            [cmul(base, row_of(groups, 0, row)), cmul(base, conj(up8)), base, cmul(base, up8)]
        )

    for b in range(rows):
        body(b)


def screen_kernel(stations_from, plane_from, phase_from, beam_from, screen_ref, *refs):
    sources, held, sems = ((stations_from, plane_from, phase_from, beam_from), refs[:4], refs[4])
    copies = [pltpu.make_async_copy(src, dst, sems.at[at]) for at, (src, dst) in enumerate(zip(sources, held))]
    for copy in copies:
        copy.start()
    stations_ref, plane_ref, phase_ref, beam_ref = held
    for copy in copies:
        copy.wait()
    stations = beam_ref.shape[0]
    planes, pixels = phase_ref.shape
    one = onehot(down(row_of_blocks(stations_ref[:, 0, :])), 0, stations)
    two = onehot(down(row_of_blocks(stations_ref[:, 1, :])), 0, stations)
    plane = onehot(down(row_of_blocks(plane_ref[...])), 0, planes).astype(F32)
    width = 256
    for at in range(0, pixels, width):
        re, im = pl.ds(at, width), pl.ds(pixels + at, width)
        one_re = jnp.dot(one, beam_ref[:, re], preferred_element_type=F32)
        one_im = jnp.dot(one, beam_ref[:, im], preferred_element_type=F32)
        two_re = jnp.dot(two, beam_ref[:, re], preferred_element_type=F32)
        two_im = jnp.dot(two, beam_ref[:, im], preferred_element_type=F32)
        pair_re = one_re * two_re + one_im * two_im
        pair_im = one_im * two_re - one_re * two_im
        phase = phase_ref[:, re]
        exact = lax.Precision.HIGHEST
        wave_re = jnp.dot(plane, jnp.cos(phase), precision=exact, preferred_element_type=F32)
        wave_im = jnp.dot(plane, jnp.sin(phase), precision=exact, preferred_element_type=F32)
        screen_ref[:, re] = pair_re * wave_re - pair_im * wave_im
        screen_ref[:, im] = pair_re * wave_im + pair_im * wave_re


def blocks_from(place_ref, n_y, n_h, sign):
    return [
        lax.rem(place_ref[1] + (n_y + sign * by) % n_y, n_y) * n_h + lax.rem(place_ref[2] + flip, n_h)
        for by in range(n_y)
        for flip in range(n_h)
    ]


def rows_of_blocks(ref, blocks, cells):
    return jnp.concatenate([ref[pl.ds(pl.multiple_of(block * 16, 16), 16), cells] for block in blocks], axis=0)


def image_kernel(n_y, n_h, cores, owned, place_ref, subgrid_ref, near_ref, far_ref, screen_ref, *image_refs):
    half = near_ref.shape[0] * near_ref.shape[1]
    pixels = screen_ref.shape[1] // 2
    blocks = blocks_from(place_ref, n_y, n_h, 1)
    subgrids = jnp.concatenate([subgrid_ref[pl.ds(block, 1), :] for block in blocks], axis=1)
    slots = down(slot_of(subgrids, place_ref[3], cores, owned))
    near, far = (onehot(slots, 0, half), onehot(slots, half, half))
    tiles = pixels // 128
    width = 256

    def rows_of(cells):
        held = (near_ref[:, :, cells].reshape(half, width), far_ref[:, :, cells].reshape(half, width))
        return jnp.dot(near, held[0], preferred_element_type=F32) + jnp.dot(far, held[1], preferred_element_type=F32)

    for at in range(0, pixels, width):
        re, im = pl.ds(at, width), pl.ds(pixels + at, width)
        model_re, model_im = (rows_of(re), rows_of(im))
        screen_re, screen_im = (rows_of_blocks(screen_ref, blocks, re), rows_of_blocks(screen_ref, blocks, im))
        image_re = (screen_re * model_re - screen_im * model_im).astype(BF16)
        image_im = (screen_re * model_im + screen_im * model_re).astype(BF16)
        for off in range(0, width, 128):
            for image, q in ((image_re, (at + off) // 128), (image_im, (at + off) // 128 + tiles)):
                for j in range(len(blocks)):
                    image_refs[j // n_h][j % n_h, 16 * q : 16 * q + 16, :] = image[
                        16 * j : 16 * j + 16, off : off + 128
                    ]


def sum_kernel(*refs):
    pieces, sums = (refs[:-2], refs[-2:])
    for flip, sum_ref in enumerate(sums):
        total = pieces[0][flip].astype(F32)
        for piece in pieces[1:]:
            total = total + piece[flip].astype(F32)
        sum_ref[...] = total


def route_kernel(n_y, n_h, place_ref, reader_ref, rows_ref, other_ref, *out_refs):
    block = jnp.int32(0)
    for at in range(n_y * n_h):
        block = jnp.where(reader_ref[0, at] == place_ref[0], at, block)
    for by, out_ref in enumerate(out_refs, 1):
        to = lax.rem(place_ref[1] + by, n_y) * n_h + place_ref[2]

        @pl.when(block == to)
        def _():
            out_ref[...] = rows_ref[...]

        @pl.when(block != to)
        def _():
            out_ref[...] = other_ref[...]


def visibility_kernel(
    n_y,
    n_h,
    place_ref,
    reader_ref,
    near_ref,
    far_ref,
    rows_ref,
    other_ref,
    came_1_ref,
    came_2_ref,
    came_3_ref,
    table_ref,
    resid_ref,
    grid_ref,
    cells_ref,
    out_ref,
):
    rows, channels = (resid_ref.shape[0], resid_ref.shape[1] // 2)
    cells_ref[...] = near_ref[...] + far_ref[...]
    source = reader_ref[0, place_ref[0]]
    steps = lax.rem(place_ref[1] + n_y - lax.div(source, n_h), n_y)
    here = jnp.where(lax.rem(source, n_h) == place_ref[2], 0, 1)
    pick = jnp.where(steps == 0, here, steps + 1)
    for at, ref in enumerate((rows_ref, other_ref, came_1_ref, came_2_ref, came_3_ref)):

        @pl.when(pick == at)
        def _():
            resid_ref[...] = ref[...].astype(F32)

    width = 256

    def degrid(b):
        cells = cells_ref[pl.ds(b, 16, stride=16), :]

        def spread(first, second):
            return jnp.concatenate(
                [
                    jnp.concatenate([first[:, 32 * p : 32 * p + 32], second[:, 32 * p : 32 * p + 32]], axis=1)
                    for p in range(4)
                ],
                axis=0,
            )

        image = jnp.concatenate([spread(cells[0:8], -cells[8:16]), spread(cells[8:16], cells[0:8])], axis=0)
        high = image.astype(BF16)
        low = (image - high.astype(F32)).astype(BF16)
        operand = jnp.concatenate([high, low], axis=1)
        for at in range(0, channels, width):
            chans = pl.ds(at, width)
            north = table_ref[1, b, :, chans]
            inner = jnp.dot(operand, jnp.concatenate([north, north], axis=0), preferred_element_type=F32)
            inner_re, inner_im = (inner[:32], inner[32:])
            east = table_ref[0, b, :, chans].astype(F32)
            cos, sin = (east[:32], east[32:])
            vis_re = jnp.sum(cos * inner_re - sin * inner_im, axis=0, keepdims=True)
            vis_im = jnp.sum(cos * inner_im + sin * inner_re, axis=0, keepdims=True)
            row = pl.ds(b, 1)
            late = pl.ds(channels + at, width)
            resid_ref[row, chans] = resid_ref[row, chans] - vis_re
            resid_ref[row, late] = resid_ref[row, late] - vis_im

    def grid(b):
        products = jnp.zeros((64, 64), F32)
        for at in range(0, channels, width):
            chans, late = (pl.ds(at, width), pl.ds(channels + at, width))
            resid_re, resid_im = (resid_ref[pl.ds(b, 1), chans], resid_ref[pl.ds(b, 1), late])
            east = table_ref[0, b, :, chans].astype(F32)
            cos, sin = (east[:32], east[32:])
            weighted = jnp.concatenate([cos * resid_re + sin * resid_im, cos * resid_im - sin * resid_re], axis=0)
            products = products + lax.dot_general(
                weighted.astype(BF16),
                table_ref[1, b, :, chans],
                (((1,), (1,)), ((), ())),
                preferred_element_type=F32,
            )
        halves = (products[:32, :32] + products[32:, 32:], products[32:, :32] - products[:32, 32:])
        out_ref[pl.ds(b, 16, stride=16), :] = jnp.concatenate(
            [jnp.concatenate([half[8 * p : 8 * p + 8] for p in range(4)], axis=1) for half in halves], axis=0
        )

    for b in range(rows):
        degrid(b)
    for b in range(rows):
        grid(b)
    grid_ref[...] = out_ref[...].astype(BF16)


def regrid_kernel(scale, n_y, n_h, cores, owned, place_ref, subgrid_ref, screen_ref, *refs):
    grids, (near_ref, far_ref) = (refs[:-2], refs[-2:])
    blocks = blocks_from(place_ref, n_y, n_h, -1)
    half = near_ref.shape[0]
    pixels = screen_ref.shape[1] // 2
    tiles = pixels // 128
    count = screen_ref.shape[0]

    def grid_of(q):
        return jnp.concatenate([ref[16 * q : 16 * q + 16, :] for ref in grids], axis=0).astype(F32)

    subs = lax.broadcasted_iota(jnp.int32, (2 * half, count), 0)
    target = jnp.concatenate([subgrid_ref[pl.ds(block, 1), :] for block in blocks], axis=1)
    target = slot_of(target, place_ref[3], cores, owned)
    sums = jnp.where(target == subs, 1.0, 0.0).astype(BF16)
    near, far = (sums[:half], sums[half:])
    for q in range(tiles):
        re, im = pl.ds(128 * q, 128), pl.ds(pixels + 128 * q, 128)
        grid_re, grid_im = (grid_of(q), grid_of(q + tiles))
        screen_re, screen_im = (rows_of_blocks(screen_ref, blocks, re), rows_of_blocks(screen_ref, blocks, im))
        out_re = (screen_re * grid_re + screen_im * grid_im) * scale
        out_im = (screen_re * grid_im - screen_im * grid_re) * scale
        for cells, value in ((re, out_re), (im, out_im)):
            high = value.astype(BF16)
            low = (value - high.astype(F32)).astype(BF16)
            near_ref[:, cells] = jnp.dot(near, high, preferred_element_type=F32) + jnp.dot(
                near, low, preferred_element_type=F32
            )
            far_ref[:, cells] = jnp.dot(far, high, preferred_element_type=F32) + jnp.dot(
                far, low, preferred_element_type=F32
            )


def shift(value, axis, by):
    size = lax.axis_size(axis)
    return lax.ppermute(value, axis, [(i, (i + by) % size) for i in range(size)])


def local(
    sectioned_rows,
    reader,
    baseline_coords,
    subgrid_index,
    stations,
    plane_index,
    model_grid,
    beam_screens,
    plane_phase,
    channel_freq,
):
    n_y, n_h, n_x, n_z, n_c = (lax.axis_size(axis) for axis in FACET + TILE)
    at_y, at_h, at_x, at_z, at_c = (lax.axis_index(axis) for axis in FACET + TILE)
    n_facet = n_y * n_h
    channels = channel_freq.shape[0]
    pixels = plane_phase.shape[1]
    row_block = sectioned_rows.shape[1]
    count = n_facet * row_block
    owned = model_grid.shape[1]
    subgrid_count = owned * n_x * n_z * n_c
    cell_rows = 2 * pixels // 128 * row_block
    grid_scale = 1.0 / math.sqrt(channels * n_facet * (row_block * n_x * n_z * n_c) / subgrid_count)
    ids = jnp.arange(4, dtype=jnp.int32)
    place = jnp.where(
        ids == 0, at_y * n_h + at_h, jnp.where(ids == 1, at_y, jnp.where(ids == 2, at_h, at_c))
    ).astype(jnp.int32)

    with jax.named_scope("model_gather"):
        copies = jnp.broadcast_to(model_grid, (n_x * n_z, owned, 2 * pixels))
        near = lax.all_to_all(copies, ("x", "z"), split_axis=0, concat_axis=0, tiled=True)

    operands = (stations, plane_index, plane_phase, beam_screens[0])
    screen = pl.pallas_call(
        screen_kernel,
        out_shape=jax.ShapeDtypeStruct((count, 2 * pixels), F32),
        in_specs=[ANY] * len(operands),
        out_specs=VMEM,
        scratch_shapes=[pltpu.VMEM(value.shape, value.dtype) for value in operands]
        + [pltpu.SemaphoreType.DMA((len(operands),))],
        compiler_params=params(58),
        cost_estimate=pl.CostEstimate(flops=10**9, bytes_accessed=4 << 20, transcendentals=1 << 16),
        name="screens",
    )(*operands)

    near, screen = lax.optimization_barrier((near, screen))
    far = shift(near, "c", 1)
    images = pl.pallas_call(
        functools.partial(image_kernel, n_y, n_h, n_c, owned),
        out_shape=[jax.ShapeDtypeStruct((n_h, cell_rows, 128), BF16)] * n_y,
        in_specs=[SMEM] + [VMEM] * 4,
        out_specs=[VMEM] * n_y,
        compiler_params=params(8),
        cost_estimate=pl.CostEstimate(flops=10**8, bytes_accessed=2 << 20, transcendentals=0),
        name="images",
    )(place, subgrid_index, near, far, screen)
    rows, *images = lax.optimization_barrier((sectioned_rows[0], *images))

    with jax.named_scope("visible_route"):
        other = shift(rows, "h", 1)
        sent = pl.pallas_call(
            functools.partial(route_kernel, n_y, n_h),
            out_shape=[jax.ShapeDtypeStruct(rows.shape, BF16)] * (n_y - 1),
            in_specs=[SMEM, SMEM, VMEM, VMEM],
            out_specs=[VMEM] * (n_y - 1),
            compiler_params=params(4),
            cost_estimate=pl.CostEstimate(flops=10**6, bytes_accessed=1 << 18, transcendentals=0),
            name="route",
        )(place, reader, rows, other)

    with jax.named_scope("image_sum"):
        pieces = [images[0]] + [shift(images[by], "y", by) for by in range(1, n_y)]
        own_sum, other_sum = pl.pallas_call(
            sum_kernel,
            out_shape=[jax.ShapeDtypeStruct((cell_rows, 128), F32)] * 2,
            in_specs=[VMEM] * n_y,
            out_specs=[VMEM] * 2,
            compiler_params=params(4),
            cost_estimate=pl.CostEstimate(flops=10**6, bytes_accessed=1 << 20, transcendentals=0),
            name="image_sums",
        )(*pieces)
        later, own_sum = lax.optimization_barrier((place, own_sum))
        beside_sum = shift(other_sum, "h", 1)

    tables = pl.pallas_call(
        table_kernel,
        out_shape=jax.ShapeDtypeStruct((2, row_block, 64, channels), BF16),
        in_specs=[SMEM, VMEM, VMEM],
        out_specs=VMEM,
        scratch_shapes=[
            pltpu.VMEM((10, 2 * row_block, channels), F32),
            pltpu.VMEM((8, 2 * row_block, channels), F32),
        ],
        compiler_params=params(16),
        cost_estimate=pl.CostEstimate(flops=10**9, bytes_accessed=8 << 20, transcendentals=1 << 17),
        name="tables",
    )(later, baseline_coords, channel_freq.reshape(1, channels))
    came = [shift(value, "y", by) for by, value in enumerate(sent, 1)]

    residual, gridded = pl.pallas_call(
        functools.partial(visibility_kernel, n_y, n_h),
        out_shape=[
            jax.ShapeDtypeStruct((row_block, 2 * channels), F32),
            jax.ShapeDtypeStruct((cell_rows, 128), BF16),
        ],
        in_specs=[SMEM] * 2 + [VMEM] * 8,
        out_specs=[VMEM] * 2,
        scratch_shapes=[pltpu.VMEM((cell_rows, 128), F32), pltpu.VMEM((cell_rows, 128), F32)],
        compiler_params=params(16),
        cost_estimate=pl.CostEstimate(flops=10**9, bytes_accessed=8 << 20, transcendentals=0),
        name="visibilities",
    )(place, reader, own_sum, beside_sum, rows, other, *came, tables)

    with jax.named_scope("grid_gather"):
        beside = shift(gridded, "h", 1)
        grids = [gridded, beside]
        for by in range(1, n_y):
            grids += [shift(gridded, "y", by), shift(beside, "y", by)]

    half = subgrid_count // n_c
    near_sum, far_sum = pl.pallas_call(
        functools.partial(regrid_kernel, grid_scale, n_y, n_h, n_c, owned),
        out_shape=[jax.ShapeDtypeStruct((half, 2 * pixels), F32)] * 2,
        in_specs=[SMEM] + [VMEM] * (2 + n_facet),
        out_specs=[VMEM] * 2,
        compiler_params=params(8),
        cost_estimate=pl.CostEstimate(flops=10**8, bytes_accessed=3 << 20, transcendentals=0),
        name="regrid",
    )(place, subgrid_index, screen, *grids)

    with jax.named_scope("dirty_scatter"):
        chip_sum = (near_sum + shift(far_sum, "c", 1)).astype(BF16).reshape(n_x * n_z, owned, 2 * pixels)
        chips = lax.all_to_all(chip_sum, ("x", "z"), split_axis=0, concat_axis=0, tiled=True)
        dirty = jnp.sum(chips.astype(F32), axis=0)
    return (residual[None], dirty[None])


def solution(mesh):
    split = Mesh(mesh.devices.reshape(4, 2, 4, 4, 2), FACET + TILE)
    return jax.shard_map(
        local,
        mesh=split,
        in_specs=(
            P(FACET, TILE, None),
            P(TILE, None),
            P(None, None, TILE),
            P(None, TILE),
            P(None, None, TILE),
            P(None, TILE),
            P(FACET, TILE, None),
            P(FACET, None, None),
            P(),
            P(),
        ),
        out_specs=(P(FACET, TILE, None), P(FACET, TILE, None)),
        check_vma=False,
    )
```

```python
import functools
import math

import jax
import jax.numpy as jnp
from jax import lax
from jax.experimental import pallas as pl
from jax.experimental.pallas import tpu as pltpu
from jax.sharding import Mesh
from jax.sharding import PartitionSpec as P

TWO_PI = 2.0 * math.pi
F32 = jnp.float32
BF16 = jnp.bfloat16
FACET = ("y", "h")
TILE = ("x", "z", "c")
VMEM = pl.BlockSpec(memory_space=pltpu.VMEM)
SMEM = pl.BlockSpec(memory_space=pltpu.SMEM)
ANY = pl.BlockSpec(memory_space=pl.ANY)


def params(mib):
    return pltpu.CompilerParams(vmem_limit_bytes=mib << 20)


def cmul(a, b):
    return (a[0] * b[0] - a[1] * b[1], a[0] * b[1] + a[1] * b[0])


def conj(a):
    return (a[0], -a[1])


def row_of_blocks(values):
    return jnp.concatenate([values[at : at + 1, :] for at in range(values.shape[0])], axis=1)


def down(row):
    return jnp.broadcast_to(row, (128, 128)).T


def onehot(column, first, count):
    lanes = lax.broadcasted_iota(jnp.int32, (128, 128), 1)
    width = min(count, 128)
    parts = [
        jnp.where(column == lanes + (first + at), 1.0, 0.0).astype(BF16)[:, :width] for at in range(0, count, 128)
    ]
    return parts[0] if len(parts) == 1 else jnp.concatenate(parts, axis=1)


def slot_of(subgrid, core, cores, owned):
    held = lax.rem(lax.div(subgrid, owned) + (cores - core), cores)
    return (held * (128 // cores)) + lax.div(subgrid, owned * cores) * owned + lax.rem(subgrid, owned)


def table_kernel(n_h, kind, coords_ref, freq_ref, table_ref, powers, groups):
    rows = coords_ref.shape[2]
    coords = coords_ref[lax.axis_index("y") * n_h + lax.axis_index("h")]
    row = jnp.concatenate([coords[kind : kind + 1], jnp.zeros((1, 128 - rows), F32)], axis=1)
    column = (TWO_PI * down(row)[:rows]) * (1.0 / 32.0)
    angle = jnp.concatenate([column] * (freq_ref.shape[1] // 128), axis=1) * freq_ref[...]
    z1 = (jnp.cos(angle), jnp.sin(angle))
    z2 = cmul(z1, z1)
    z4 = cmul(z2, z2)
    z8 = cmul(z4, z4)
    z16 = cmul(z8, z8)
    low16 = conj(z16)
    for at, value in enumerate((z1, z2, z4, z8, z16)):
        powers[2 * at] = value[0]
        powers[2 * at + 1] = value[1]
    for at, value in enumerate((low16, cmul(low16, z1), cmul(low16, z2), cmul(low16, cmul(z1, z2)))):
        groups[2 * at] = value[0]
        groups[2 * at + 1] = value[1]
    sub = lax.broadcasted_iota(jnp.int32, (8, angle.shape[1]), 0)

    def row_of(ref, at, row):
        return (ref[2 * at, pl.ds(row, 1), :], ref[2 * at + 1, pl.ds(row, 1), :])

    def picked(factor, bit):
        on = (sub & bit) != 0
        return (jnp.where(on, factor[0], 1.0), jnp.where(on, factor[1], 0.0))

    def bits(factors):
        return cmul(cmul(picked(factors[0], 1), picked(factors[1], 2)), picked(factors[2], 4))

    def stacked(parts):
        return jnp.concatenate([part[0] for part in parts] + [part[1] for part in parts], axis=0).astype(BF16)

    def body(b):
        base = bits([row_of(powers, at, b) for at in ((2, 3, 4), (0, 1, 2))[kind]])
        if kind == 0:
            table_ref[b] = stacked([cmul(base, row_of(groups, at, b)) for at in range(4)])
        else:
            up8 = row_of(powers, 3, b)
            table_ref[b] = stacked([cmul(base, row_of(groups, 0, b)), cmul(base, conj(up8)), base, cmul(base, up8)])

    for b in range(rows):
        body(b)


def screen_kernel(stations_from, plane_from, phase_from, beam_from, screen_ref, *refs):
    sources, held, sems = ((stations_from, plane_from, phase_from, beam_from), refs[:4], refs[4])
    copies = [pltpu.make_async_copy(src, dst, sems.at[at]) for at, (src, dst) in enumerate(zip(sources, held))]
    for copy in copies:
        copy.start()
    stations_ref, plane_ref, phase_ref, beam_ref = held
    for copy in copies:
        copy.wait()
    stations = beam_ref.shape[0]
    planes, pixels = phase_ref.shape
    one = onehot(down(row_of_blocks(stations_ref[:, 0, :])), 0, stations)
    two = onehot(down(row_of_blocks(stations_ref[:, 1, :])), 0, stations)
    plane = onehot(down(row_of_blocks(plane_ref[...])), 0, planes).astype(F32)
    width = 256
    for at in range(0, pixels, width):
        re, im = pl.ds(at, width), pl.ds(pixels + at, width)
        one_re = jnp.dot(one, beam_ref[:, re], preferred_element_type=F32)
        one_im = jnp.dot(one, beam_ref[:, im], preferred_element_type=F32)
        two_re = jnp.dot(two, beam_ref[:, re], preferred_element_type=F32)
        two_im = jnp.dot(two, beam_ref[:, im], preferred_element_type=F32)
        pair_re = one_re * two_re + one_im * two_im
        pair_im = one_im * two_re - one_re * two_im
        phase = phase_ref[:, re]
        exact = lax.Precision.HIGHEST
        wave_re = jnp.dot(plane, jnp.cos(phase), precision=exact, preferred_element_type=F32)
        wave_im = jnp.dot(plane, jnp.sin(phase), precision=exact, preferred_element_type=F32)
        screen_ref[:, re] = pair_re * wave_re - pair_im * wave_im
        screen_ref[:, im] = pair_re * wave_im + pair_im * wave_re


def blocks_from(n_y, n_h, sign):
    at_y, at_h = (lax.axis_index("y"), lax.axis_index("h"))
    return [
        lax.rem(at_y + (n_y + sign * by) % n_y, n_y) * n_h + lax.rem(at_h + flip, n_h)
        for by in range(n_y)
        for flip in range(n_h)
    ]


def rows_of_blocks(ref, blocks, cells):
    return jnp.concatenate([ref[pl.ds(pl.multiple_of(block * 16, 16), 16), cells] for block in blocks], axis=0)


def image_kernel(n_y, n_h, cores, owned, subgrid_ref, near_ref, far_ref, screen_ref, *image_refs):
    half = near_ref.shape[0] * near_ref.shape[1]
    pixels = screen_ref.shape[1] // 2
    blocks = blocks_from(n_y, n_h, 1)
    subgrids = jnp.concatenate([subgrid_ref[pl.ds(block, 1), :] for block in blocks], axis=1)
    slots = down(slot_of(subgrids, lax.axis_index("c"), cores, owned))
    near, far = (onehot(slots, 0, half), onehot(slots, half, half))
    tiles = pixels // 128
    width = 256

    def rows_of(cells):
        held = (near_ref[:, :, cells].reshape(half, width), far_ref[:, :, cells].reshape(half, width))
        return jnp.dot(near, held[0], preferred_element_type=F32) + jnp.dot(far, held[1], preferred_element_type=F32)

    for at in range(0, pixels, width):
        re, im = pl.ds(at, width), pl.ds(pixels + at, width)
        model_re, model_im = (rows_of(re), rows_of(im))
        screen_re, screen_im = (rows_of_blocks(screen_ref, blocks, re), rows_of_blocks(screen_ref, blocks, im))
        image_re = (screen_re * model_re - screen_im * model_im).astype(BF16)
        image_im = (screen_re * model_im + screen_im * model_re).astype(BF16)
        for off in range(0, width, 128):
            for image, q in ((image_re, (at + off) // 128), (image_im, (at + off) // 128 + tiles)):
                for j in range(len(blocks)):
                    image_refs[j // n_h][j % n_h, 16 * q : 16 * q + 16, :] = image[
                        16 * j : 16 * j + 16, off : off + 128
                    ]


def sum_kernel(*refs):
    pieces, sums = (refs[:-2], refs[-2:])
    for flip, sum_ref in enumerate(sums):
        total = pieces[0][flip].astype(F32)
        for piece in pieces[1:]:
            total = total + piece[flip].astype(F32)
        sum_ref[...] = total


def route_kernel(n_y, n_h, reader_ref, rows_ref, other_ref, pick_ref, *out_refs):
    at_y, at_h = (lax.axis_index("y"), lax.axis_index("h"))
    own = at_y * n_h + at_h
    source = reader_ref[0, own]
    steps = lax.rem(at_y + n_y - lax.div(source, n_h), n_y)
    here = jnp.where(lax.rem(source, n_h) == at_h, 0, 1)
    pick_ref[...] = jnp.full(pick_ref.shape, jnp.where(steps == 0, here, steps + 1), jnp.int32)
    block = jnp.int32(0)
    for at in range(n_y * n_h):
        block = jnp.where(reader_ref[0, at] == own, at, block)
    for by, out_ref in enumerate(out_refs, 1):
        to = lax.rem(at_y + by, n_y) * n_h + at_h

        @pl.when(block == to)
        def _():
            out_ref[...] = rows_ref[...]

        @pl.when(block != to)
        def _():
            out_ref[...] = other_ref[...]


def visibility_kernel(
    pick_ref,
    near_ref,
    far_ref,
    rows_ref,
    other_ref,
    came_1_ref,
    came_2_ref,
    came_3_ref,
    east_ref,
    north_ref,
    resid_ref,
    grid_ref,
    cells_ref,
    out_ref,
):
    rows, channels = (resid_ref.shape[0], resid_ref.shape[1] // 2)
    cells_ref[...] = near_ref[...] + far_ref[...]
    found = (rows_ref, other_ref, came_1_ref, came_2_ref, came_3_ref)
    for at in range(0, 2 * channels, 128):
        chans = pl.ds(at, 128)
        visible = found[0][:, chans].astype(F32)
        for which, ref in enumerate(found[1:], 1):
            visible = jnp.where(pick_ref[...] == which, ref[:, chans].astype(F32), visible)
        resid_ref[:, chans] = visible
    width = 256

    def degrid(b):
        cells = cells_ref[pl.ds(b, 16, stride=16), :]

        def spread(first, second):
            return jnp.concatenate(
                [
                    jnp.concatenate([first[:, 32 * p : 32 * p + 32], second[:, 32 * p : 32 * p + 32]], axis=1)
                    for p in range(4)
                ],
                axis=0,
            )

        image = jnp.concatenate([spread(cells[0:8], -cells[8:16]), spread(cells[8:16], cells[0:8])], axis=0)
        high = image.astype(BF16)
        low = (image - high.astype(F32)).astype(BF16)
        operand = jnp.concatenate([high, low], axis=1)
        for at in range(0, channels, width):
            chans = pl.ds(at, width)
            north = north_ref[b, :, chans]
            inner = jnp.dot(operand, jnp.concatenate([north, north], axis=0), preferred_element_type=F32)
            inner_re, inner_im = (inner[:32], inner[32:])
            east = east_ref[b, :, chans].astype(F32)
            cos, sin = (east[:32], east[32:])
            vis_re = jnp.sum(cos * inner_re - sin * inner_im, axis=0, keepdims=True)
            vis_im = jnp.sum(cos * inner_im + sin * inner_re, axis=0, keepdims=True)
            row = pl.ds(b, 1)
            late = pl.ds(channels + at, width)
            resid_ref[row, chans] = resid_ref[row, chans] - vis_re
            resid_ref[row, late] = resid_ref[row, late] - vis_im

    def grid(b):
        products = jnp.zeros((64, 64), F32)
        for at in range(0, channels, width):
            chans, late = (pl.ds(at, width), pl.ds(channels + at, width))
            resid_re, resid_im = (resid_ref[pl.ds(b, 1), chans], resid_ref[pl.ds(b, 1), late])
            east = east_ref[b, :, chans].astype(F32)
            cos, sin = (east[:32], east[32:])
            weighted = jnp.concatenate([cos * resid_re + sin * resid_im, cos * resid_im - sin * resid_re], axis=0)
            products = products + lax.dot_general(
                weighted.astype(BF16),
                north_ref[b, :, chans],
                (((1,), (1,)), ((), ())),
                preferred_element_type=F32,
            )
        halves = (products[:32, :32] + products[32:, 32:], products[32:, :32] - products[:32, 32:])
        out_ref[pl.ds(b, 16, stride=16), :] = jnp.concatenate(
            [jnp.concatenate([half[8 * p : 8 * p + 8] for p in range(4)], axis=1) for half in halves], axis=0
        )

    for b in range(rows):
        degrid(b)
    for b in range(rows):
        grid(b)
    grid_ref[...] = out_ref[...].astype(BF16)


def regrid_kernel(scale, n_y, n_h, cores, owned, other, subgrid_ref, screen_ref, *refs):
    grids, sum_ref = (refs[:-1], refs[-1])
    blocks = blocks_from(n_y, n_h, -1)
    half = sum_ref.shape[0]
    pixels = screen_ref.shape[1] // 2
    tiles = pixels // 128
    count = screen_ref.shape[0]

    def grid_of(q):
        return jnp.concatenate([ref[16 * q : 16 * q + 16, :] for ref in grids], axis=0).astype(F32)

    subs = lax.broadcasted_iota(jnp.int32, (half, count), 0) + other * half
    target = jnp.concatenate([subgrid_ref[pl.ds(block, 1), :] for block in blocks], axis=1)
    target = slot_of(target, lax.axis_index("c"), cores, owned)
    sums = jnp.where(target == subs, 1.0, 0.0).astype(BF16)
    sums = jnp.concatenate([sums, sums], axis=1)
    for q in range(tiles):
        re, im = pl.ds(128 * q, 128), pl.ds(pixels + 128 * q, 128)
        grid_re, grid_im = (grid_of(q), grid_of(q + tiles))
        screen_re, screen_im = (rows_of_blocks(screen_ref, blocks, re), rows_of_blocks(screen_ref, blocks, im))
        out_re = (screen_re * grid_re + screen_im * grid_im) * scale
        out_im = (screen_re * grid_im - screen_im * grid_re) * scale
        value = jnp.concatenate([out_re, out_im], axis=1)
        high = value.astype(BF16)
        low = (value - high.astype(F32)).astype(BF16)
        both = jnp.dot(sums, jnp.concatenate([high, low], axis=0), preferred_element_type=F32)
        sum_ref[:, re] = both[:, :128]
        sum_ref[:, im] = both[:, 128:]


def shift(value, axis, by):
    size = lax.axis_size(axis)
    return lax.ppermute(value, axis, [(i, (i + by) % size) for i in range(size)])


def local(
    sectioned_rows,
    reader,
    baseline_coords,
    subgrid_index,
    stations,
    plane_index,
    model_grid,
    beam_screens,
    plane_phase,
    channel_freq,
):
    n_y, n_h, n_x, n_z, n_c = (lax.axis_size(axis) for axis in FACET + TILE)
    n_facet = n_y * n_h
    channels = channel_freq.shape[0]
    pixels = plane_phase.shape[1]
    row_block = sectioned_rows.shape[1]
    count = n_facet * row_block
    owned = model_grid.shape[1]
    subgrid_count = owned * n_x * n_z * n_c
    cell_rows = 2 * pixels // 128 * row_block
    grid_scale = 1.0 / math.sqrt(channels * n_facet * (row_block * n_x * n_z * n_c) / subgrid_count)
    with jax.named_scope("model_gather"):
        copies = jnp.broadcast_to(model_grid, (n_x * n_z, owned, 2 * pixels))
        near = lax.all_to_all(copies, ("x", "z"), split_axis=0, concat_axis=0, tiled=True)

    operands = (stations, plane_index, plane_phase, beam_screens[0])
    screen = pl.pallas_call(
        screen_kernel,
        out_shape=jax.ShapeDtypeStruct((count, 2 * pixels), F32),
        in_specs=[ANY] * len(operands),
        out_specs=VMEM,
        scratch_shapes=[pltpu.VMEM(value.shape, value.dtype) for value in operands]
        + [pltpu.SemaphoreType.DMA((len(operands),))],
        compiler_params=params(44),
        cost_estimate=pl.CostEstimate(flops=10**9, bytes_accessed=4 << 20, transcendentals=1 << 16),
        name="screens",
    )(*operands)

    near, screen = lax.optimization_barrier((near, screen))
    far = shift(near, "c", 1)
    images = pl.pallas_call(
        functools.partial(image_kernel, n_y, n_h, n_c, owned),
        out_shape=[jax.ShapeDtypeStruct((n_h, cell_rows, 128), BF16)] * n_y,
        in_specs=[VMEM] * 4,
        out_specs=[VMEM] * n_y,
        compiler_params=params(8),
        cost_estimate=pl.CostEstimate(flops=10**8, bytes_accessed=2 << 20, transcendentals=0),
        name="images",
    )(subgrid_index, near, far, screen)
    rows, soon, *images = lax.optimization_barrier((sectioned_rows[0], baseline_coords, *images))

    with jax.named_scope("visible_route"):
        other = shift(rows, "h", 1)
        pick, *sent = pl.pallas_call(
            functools.partial(route_kernel, n_y, n_h),
            out_shape=[jax.ShapeDtypeStruct((row_block, 128), jnp.int32)]
            + [jax.ShapeDtypeStruct(rows.shape, BF16)] * (n_y - 1),
            in_specs=[SMEM, VMEM, VMEM],
            out_specs=[VMEM] * n_y,
            compiler_params=params(4),
            cost_estimate=pl.CostEstimate(flops=10**6, bytes_accessed=1 << 18, transcendentals=0),
            name="route",
        )(reader, rows, other)

    def table(kind, coords):
        return pl.pallas_call(
            functools.partial(table_kernel, n_h, kind),
            out_shape=jax.ShapeDtypeStruct((row_block, 64, channels), BF16),
            in_specs=[VMEM] * 2,
            out_specs=VMEM,
            scratch_shapes=[
                pltpu.VMEM((10, row_block, channels), F32),
                pltpu.VMEM((8, row_block, channels), F32),
            ],
            compiler_params=params(16),
            cost_estimate=pl.CostEstimate(flops=10**9, bytes_accessed=4 << 20, transcendentals=1 << 16),
            name=("east", "north")[kind],
        )(coords, channel_freq.reshape(1, channels))

    with jax.named_scope("image_sum"):
        north = table(1, soon)
        images[0], north = lax.optimization_barrier((images[0], north))
        pieces = [images[0]] + [shift(images[by], "y", by) for by in range(1, n_y)]
        own_sum, other_sum = pl.pallas_call(
            sum_kernel,
            out_shape=[jax.ShapeDtypeStruct((cell_rows, 128), F32)] * 2,
            in_specs=[VMEM] * n_y,
            out_specs=[VMEM] * 2,
            compiler_params=params(4),
            cost_estimate=pl.CostEstimate(flops=10**6, bytes_accessed=1 << 20, transcendentals=0),
            name="image_sums",
        )(*pieces)
        later, own_sum = lax.optimization_barrier((baseline_coords, own_sum))
        beside_sum = shift(other_sum, "h", 1)

    east = table(0, later)
    came = [shift(value, "y", by) for by, value in enumerate(sent, 1)]

    residual, gridded = pl.pallas_call(
        visibility_kernel,
        out_shape=[
            jax.ShapeDtypeStruct((row_block, 2 * channels), F32),
            jax.ShapeDtypeStruct((cell_rows, 128), BF16),
        ],
        in_specs=[VMEM] * 10,
        out_specs=[VMEM] * 2,
        scratch_shapes=[pltpu.VMEM((cell_rows, 128), F32), pltpu.VMEM((cell_rows, 128), F32)],
        compiler_params=params(16),
        cost_estimate=pl.CostEstimate(flops=10**9, bytes_accessed=8 << 20, transcendentals=0),
        name="visibilities",
    )(pick, own_sum, beside_sum, rows, other, *came, east, north)

    with jax.named_scope("grid_gather"):
        beside = shift(gridded, "h", 1)
        grids = [gridded, beside]
        for by in range(1, n_y):
            grids += [shift(gridded, "y", by), shift(beside, "y", by)]

    half = subgrid_count // n_c

    def regrid(other, subgrids):
        return pl.pallas_call(
            functools.partial(regrid_kernel, grid_scale, n_y, n_h, n_c, owned, other),
            out_shape=jax.ShapeDtypeStruct((half, 2 * pixels), F32),
            in_specs=[VMEM] * (2 + n_facet),
            out_specs=VMEM,
            compiler_params=params(8),
            cost_estimate=pl.CostEstimate(flops=10**8, bytes_accessed=3 << 20, transcendentals=0),
            name=("regrid_near", "regrid_far")[other],
        )(subgrids, screen, *grids)

    far_sum = regrid(1, subgrid_index)
    subgrids, far_sum = lax.optimization_barrier((subgrid_index, far_sum))
    near_sum = regrid(0, subgrids)

    with jax.named_scope("dirty_scatter"):
        chip_sum = (near_sum + shift(far_sum, "c", 1)).astype(BF16).reshape(n_x * n_z, owned, 2 * pixels)
        chips = lax.all_to_all(chip_sum, ("x", "z"), split_axis=0, concat_axis=0, tiled=True)
        dirty = jnp.sum(chips.astype(F32), axis=0)
    return (residual[None], dirty[None])


def solution(mesh):
    split = Mesh(mesh.devices.reshape(4, 2, 4, 4, 2), FACET + TILE)
    return jax.shard_map(
        local,
        mesh=split,
        in_specs=(
            P(FACET, TILE, None),
            P(TILE, None),
            P(None, None, TILE),
            P(None, TILE),
            P(None, None, TILE),
            P(None, TILE),
            P(FACET, TILE, None),
            P(FACET, None, None),
            P(),
            P(),
        ),
        out_specs=(P(FACET, TILE, None), P(FACET, TILE, None)),
        check_vma=False,
    )
```

```python
import functools
import math

import jax
import jax.numpy as jnp
from jax import lax
from jax.experimental import pallas as pl
from jax.experimental.pallas import tpu as pltpu
from jax.sharding import Mesh
from jax.sharding import PartitionSpec as P

TWO_PI = 2.0 * math.pi
F32 = jnp.float32
BF16 = jnp.bfloat16
FACET = ("y", "h")
TILE = ("x", "z", "c")
VMEM = pl.BlockSpec(memory_space=pltpu.VMEM)
SMEM = pl.BlockSpec(memory_space=pltpu.SMEM)
ANY = pl.BlockSpec(memory_space=pl.ANY)


def params(mib):
    return pltpu.CompilerParams(vmem_limit_bytes=mib << 20)


def cmul(a, b):
    return (a[0] * b[0] - a[1] * b[1], a[0] * b[1] + a[1] * b[0])


def conj(a):
    return (a[0], -a[1])


def row_of_blocks(values):
    return jnp.concatenate([values[at : at + 1, :] for at in range(values.shape[0])], axis=1)


def down(row):
    return jnp.broadcast_to(row, (128, 128)).T


def onehot(column, first, count):
    lanes = lax.broadcasted_iota(jnp.int32, (128, 128), 1)
    width = min(count, 128)
    parts = [
        jnp.where(column == lanes + (first + at), 1.0, 0.0).astype(BF16)[:, :width] for at in range(0, count, 128)
    ]
    return parts[0] if len(parts) == 1 else jnp.concatenate(parts, axis=1)


def slot_of(subgrid, core, cores, owned):
    held = lax.rem(lax.div(subgrid, owned) + (cores - core), cores)
    return (held * (128 // cores)) + lax.div(subgrid, owned * cores) * owned + lax.rem(subgrid, owned)


def table_kernel(n_h, kind, coords_ref, freq_ref, table_ref, powers, groups):
    rows = coords_ref.shape[2]
    coords = coords_ref[lax.axis_index("y") * n_h + lax.axis_index("h")]
    row = jnp.concatenate([coords[kind : kind + 1], jnp.zeros((1, 128 - rows), F32)], axis=1)
    column = (TWO_PI * down(row)[:rows]) * (1.0 / 32.0)
    angle = jnp.concatenate([column] * (freq_ref.shape[1] // 128), axis=1) * freq_ref[...]
    z1 = (jnp.cos(angle), jnp.sin(angle))
    z2 = cmul(z1, z1)
    z4 = cmul(z2, z2)
    z8 = cmul(z4, z4)
    z16 = cmul(z8, z8)
    low16 = conj(z16)
    for at, value in enumerate((z1, z2, z4, z8, z16)):
        powers[2 * at] = value[0]
        powers[2 * at + 1] = value[1]
    for at, value in enumerate((low16, cmul(low16, z1), cmul(low16, z2), cmul(low16, cmul(z1, z2)))):
        groups[2 * at] = value[0]
        groups[2 * at + 1] = value[1]
    sub = lax.broadcasted_iota(jnp.int32, (8, angle.shape[1]), 0)

    def row_of(ref, at, row):
        return (ref[2 * at, pl.ds(row, 1), :], ref[2 * at + 1, pl.ds(row, 1), :])

    def picked(factor, bit):
        on = (sub & bit) != 0
        return (jnp.where(on, factor[0], 1.0), jnp.where(on, factor[1], 0.0))

    def bits(factors):
        return cmul(cmul(picked(factors[0], 1), picked(factors[1], 2)), picked(factors[2], 4))

    def stacked(parts):
        return jnp.concatenate([part[0] for part in parts] + [part[1] for part in parts], axis=0).astype(BF16)

    def body(b):
        base = bits([row_of(powers, at, b) for at in ((2, 3, 4), (0, 1, 2))[kind]])
        if kind == 0:
            table_ref[b] = stacked([cmul(base, row_of(groups, at, b)) for at in range(4)])
        else:
            up8 = row_of(powers, 3, b)
            table_ref[b] = stacked([cmul(base, row_of(groups, 0, b)), cmul(base, conj(up8)), base, cmul(base, up8)])

    for b in range(rows):
        body(b)


def screen_kernel(stations_from, plane_from, phase_from, beam_from, screen_ref, *refs):
    sources, held, sems = ((stations_from, plane_from, phase_from, beam_from), refs[:4], refs[4])
    copies = [pltpu.make_async_copy(src, dst, sems.at[at]) for at, (src, dst) in enumerate(zip(sources, held))]
    for copy in copies:
        copy.start()
    stations_ref, plane_ref, phase_ref, beam_ref = held
    for copy in copies:
        copy.wait()
    stations = beam_ref.shape[0]
    planes, pixels = phase_ref.shape
    one = onehot(down(row_of_blocks(stations_ref[:, 0, :])), 0, stations)
    two = onehot(down(row_of_blocks(stations_ref[:, 1, :])), 0, stations)
    plane = onehot(down(row_of_blocks(plane_ref[...])), 0, planes).astype(F32)
    width = 256
    for at in range(0, pixels, width):
        re, im = pl.ds(at, width), pl.ds(pixels + at, width)
        one_re = jnp.dot(one, beam_ref[:, re], preferred_element_type=F32)
        one_im = jnp.dot(one, beam_ref[:, im], preferred_element_type=F32)
        two_re = jnp.dot(two, beam_ref[:, re], preferred_element_type=F32)
        two_im = jnp.dot(two, beam_ref[:, im], preferred_element_type=F32)
        pair_re = one_re * two_re + one_im * two_im
        pair_im = one_im * two_re - one_re * two_im
        phase = phase_ref[:, re]
        exact = lax.Precision.HIGHEST
        wave_re = jnp.dot(plane, jnp.cos(phase), precision=exact, preferred_element_type=F32)
        wave_im = jnp.dot(plane, jnp.sin(phase), precision=exact, preferred_element_type=F32)
        screen_ref[:, re] = pair_re * wave_re - pair_im * wave_im
        screen_ref[:, im] = pair_re * wave_im + pair_im * wave_re


def blocks_from(n_y, n_h, sign):
    at_y, at_h = (lax.axis_index("y"), lax.axis_index("h"))
    return [
        lax.rem(at_y + (n_y + sign * by) % n_y, n_y) * n_h + lax.rem(at_h + flip, n_h)
        for by in range(n_y)
        for flip in range(n_h)
    ]


def rows_of_blocks(ref, blocks, cells):
    return jnp.concatenate([ref[pl.ds(pl.multiple_of(block * 16, 16), 16), cells] for block in blocks], axis=0)


def image_kernel(n_y, n_h, cores, owned, subgrid_ref, near_ref, far_ref, screen_ref, *image_refs):
    half = near_ref.shape[0] * near_ref.shape[1]
    pixels = screen_ref.shape[1] // 2
    blocks = blocks_from(n_y, n_h, 1)
    subgrids = jnp.concatenate([subgrid_ref[pl.ds(block, 1), :] for block in blocks], axis=1)
    slots = down(slot_of(subgrids, lax.axis_index("c"), cores, owned))
    near, far = (onehot(slots, 0, half), onehot(slots, half, half))
    tiles = pixels // 128
    width = 256

    def rows_of(cells):
        held = (near_ref[:, :, cells].reshape(half, width), far_ref[:, :, cells].reshape(half, width))
        return jnp.dot(near, held[0], preferred_element_type=F32) + jnp.dot(far, held[1], preferred_element_type=F32)

    for at in range(0, pixels, width):
        re, im = pl.ds(at, width), pl.ds(pixels + at, width)
        model_re, model_im = (rows_of(re), rows_of(im))
        screen_re, screen_im = (rows_of_blocks(screen_ref, blocks, re), rows_of_blocks(screen_ref, blocks, im))
        image_re = (screen_re * model_re - screen_im * model_im).astype(BF16)
        image_im = (screen_re * model_im + screen_im * model_re).astype(BF16)
        for off in range(0, width, 128):
            for image, q in ((image_re, (at + off) // 128), (image_im, (at + off) // 128 + tiles)):
                for j in range(len(blocks)):
                    image_refs[j // n_h][j % n_h, 16 * q : 16 * q + 16, :] = image[
                        16 * j : 16 * j + 16, off : off + 128
                    ]


def sum_kernel(*refs):
    pieces, sums = (refs[:-2], refs[-2:])
    for flip, sum_ref in enumerate(sums):
        total = pieces[0][flip].astype(F32)
        for piece in pieces[1:]:
            total = total + piece[flip].astype(F32)
        sum_ref[...] = total


def route_kernel(n_y, n_h, reader_ref, rows_ref, other_ref, pick_ref, *out_refs):
    at_y, at_h = (lax.axis_index("y"), lax.axis_index("h"))
    own = at_y * n_h + at_h
    source = reader_ref[0, own]
    steps = lax.rem(at_y + n_y - lax.div(source, n_h), n_y)
    here = jnp.where(lax.rem(source, n_h) == at_h, 0, 1)
    pick_ref[...] = jnp.full(pick_ref.shape, jnp.where(steps == 0, here, steps + 1), jnp.int32)
    block = jnp.int32(0)
    for at in range(n_y * n_h):
        block = jnp.where(reader_ref[0, at] == own, at, block)
    for by, out_ref in enumerate(out_refs, 1):
        to = lax.rem(at_y + by, n_y) * n_h + at_h

        @pl.when(block == to)
        def _():
            out_ref[...] = rows_ref[...]

        @pl.when(block != to)
        def _():
            out_ref[...] = other_ref[...]


def degrid_kernel(near_ref, far_ref, east_ref, north_ref, predicted_ref, cells_ref):
    rows, channels = (predicted_ref.shape[0], predicted_ref.shape[1] // 2)
    cells_ref[...] = near_ref[...] + far_ref[...]
    width = 256

    def degrid(b):
        cells = cells_ref[pl.ds(b, 16, stride=16), :]

        def spread(first, second):
            return jnp.concatenate(
                [
                    jnp.concatenate([first[:, 32 * p : 32 * p + 32], second[:, 32 * p : 32 * p + 32]], axis=1)
                    for p in range(4)
                ],
                axis=0,
            )

        image = jnp.concatenate([spread(cells[0:8], -cells[8:16]), spread(cells[8:16], cells[0:8])], axis=0)
        high = image.astype(BF16)
        low = (image - high.astype(F32)).astype(BF16)
        operand = jnp.concatenate([high, low], axis=1)
        for at in range(0, channels, width):
            chans = pl.ds(at, width)
            north = north_ref[b, :, chans]
            inner = jnp.dot(operand, jnp.concatenate([north, north], axis=0), preferred_element_type=F32)
            inner_re, inner_im = (inner[:32], inner[32:])
            east = east_ref[b, :, chans].astype(F32)
            cos, sin = (east[:32], east[32:])
            vis_re = jnp.sum(cos * inner_re - sin * inner_im, axis=0, keepdims=True)
            vis_im = jnp.sum(cos * inner_im + sin * inner_re, axis=0, keepdims=True)
            row = pl.ds(b, 1)
            late = pl.ds(channels + at, width)
            predicted_ref[row, chans] = vis_re
            predicted_ref[row, late] = vis_im

    for b in range(rows):
        degrid(b)


def grid_kernel(
    pick_ref,
    rows_ref,
    other_ref,
    came_1_ref,
    came_2_ref,
    came_3_ref,
    predicted_ref,
    east_ref,
    north_ref,
    resid_ref,
    grid_ref,
    out_ref,
):
    rows, channels = (resid_ref.shape[0], resid_ref.shape[1] // 2)
    found = (rows_ref, other_ref, came_1_ref, came_2_ref, came_3_ref)
    for at in range(0, 2 * channels, 128):
        chans = pl.ds(at, 128)
        visible = found[0][:, chans].astype(F32)
        for which, ref in enumerate(found[1:], 1):
            visible = jnp.where(pick_ref[...] == which, ref[:, chans].astype(F32), visible)
        resid_ref[:, chans] = visible - predicted_ref[:, chans]
    width = 256

    def grid(b):
        products = jnp.zeros((64, 64), F32)
        for at in range(0, channels, width):
            chans, late = (pl.ds(at, width), pl.ds(channels + at, width))
            resid_re, resid_im = (resid_ref[pl.ds(b, 1), chans], resid_ref[pl.ds(b, 1), late])
            east = east_ref[b, :, chans].astype(F32)
            cos, sin = (east[:32], east[32:])
            weighted = jnp.concatenate([cos * resid_re + sin * resid_im, cos * resid_im - sin * resid_re], axis=0)
            products = products + lax.dot_general(
                weighted.astype(BF16),
                north_ref[b, :, chans],
                (((1,), (1,)), ((), ())),
                preferred_element_type=F32,
            )
        halves = (products[:32, :32] + products[32:, 32:], products[32:, :32] - products[:32, 32:])
        out_ref[pl.ds(b, 16, stride=16), :] = jnp.concatenate(
            [jnp.concatenate([half[8 * p : 8 * p + 8] for p in range(4)], axis=1) for half in halves], axis=0
        )

    for b in range(rows):
        grid(b)
    grid_ref[...] = out_ref[...].astype(BF16)


def regrid_kernel(scale, n_y, n_h, cores, owned, other, subgrid_ref, screen_ref, *refs):
    grids, sum_ref = (refs[:-1], refs[-1])
    blocks = blocks_from(n_y, n_h, -1)
    half = sum_ref.shape[0]
    pixels = screen_ref.shape[1] // 2
    tiles = pixels // 128
    count = screen_ref.shape[0]

    def grid_of(q):
        return jnp.concatenate([ref[16 * q : 16 * q + 16, :] for ref in grids], axis=0).astype(F32)

    subs = lax.broadcasted_iota(jnp.int32, (half, count), 0) + other * half
    target = jnp.concatenate([subgrid_ref[pl.ds(block, 1), :] for block in blocks], axis=1)
    target = slot_of(target, lax.axis_index("c"), cores, owned)
    sums = jnp.where(target == subs, 1.0, 0.0).astype(BF16)
    sums = jnp.concatenate([sums, sums], axis=1)
    for q in range(tiles):
        re, im = pl.ds(128 * q, 128), pl.ds(pixels + 128 * q, 128)
        grid_re, grid_im = (grid_of(q), grid_of(q + tiles))
        screen_re, screen_im = (rows_of_blocks(screen_ref, blocks, re), rows_of_blocks(screen_ref, blocks, im))
        out_re = (screen_re * grid_re + screen_im * grid_im) * scale
        out_im = (screen_re * grid_im - screen_im * grid_re) * scale
        value = jnp.concatenate([out_re, out_im], axis=1)
        high = value.astype(BF16)
        low = (value - high.astype(F32)).astype(BF16)
        both = jnp.dot(sums, jnp.concatenate([high, low], axis=0), preferred_element_type=F32)
        sum_ref[:, re] = both[:, :128]
        sum_ref[:, im] = both[:, 128:]


def shift(value, axis, by):
    size = lax.axis_size(axis)
    return lax.ppermute(value, axis, [(i, (i + by) % size) for i in range(size)])


def far_first(size):
    return sorted(range(1, size), key=lambda by: -min(by, size - by))


def local(
    sectioned_rows,
    reader,
    baseline_coords,
    subgrid_index,
    stations,
    plane_index,
    model_grid,
    beam_screens,
    plane_phase,
    channel_freq,
):
    n_y, n_h, n_x, n_z, n_c = (lax.axis_size(axis) for axis in FACET + TILE)
    n_facet = n_y * n_h
    channels = channel_freq.shape[0]
    pixels = plane_phase.shape[1]
    row_block = sectioned_rows.shape[1]
    count = n_facet * row_block
    owned = model_grid.shape[1]
    subgrid_count = owned * n_x * n_z * n_c
    cell_rows = 2 * pixels // 128 * row_block
    grid_scale = 1.0 / math.sqrt(channels * n_facet * (row_block * n_x * n_z * n_c) / subgrid_count)
    with jax.named_scope("model_gather"):
        copies = jnp.broadcast_to(model_grid, (n_x * n_z, owned, 2 * pixels))
        near = lax.all_to_all(copies, ("x", "z"), split_axis=0, concat_axis=0, tiled=True)

    operands = (stations, plane_index, plane_phase, beam_screens[0])
    screen = pl.pallas_call(
        screen_kernel,
        out_shape=jax.ShapeDtypeStruct((count, 2 * pixels), F32),
        in_specs=[ANY] * len(operands),
        out_specs=VMEM,
        scratch_shapes=[pltpu.VMEM(value.shape, value.dtype) for value in operands]
        + [pltpu.SemaphoreType.DMA((len(operands),))],
        compiler_params=params(44),
        cost_estimate=pl.CostEstimate(flops=10**9, bytes_accessed=4 << 20, transcendentals=1 << 16),
        name="screens",
    )(*operands)

    near, screen = lax.optimization_barrier((near, screen))
    far = shift(near, "c", 1)
    images = pl.pallas_call(
        functools.partial(image_kernel, n_y, n_h, n_c, owned),
        out_shape=[jax.ShapeDtypeStruct((n_h, cell_rows, 128), BF16)] * n_y,
        in_specs=[VMEM] * 4,
        out_specs=[VMEM] * n_y,
        compiler_params=params(8),
        cost_estimate=pl.CostEstimate(flops=10**8, bytes_accessed=2 << 20, transcendentals=0),
        name="images",
    )(subgrid_index, near, far, screen)
    rows, soon, *images = lax.optimization_barrier((sectioned_rows[0], baseline_coords, *images))

    with jax.named_scope("visible_route"):
        other = shift(rows, "h", 1)
        pick, *sent = pl.pallas_call(
            functools.partial(route_kernel, n_y, n_h),
            out_shape=[jax.ShapeDtypeStruct((row_block, 128), jnp.int32)]
            + [jax.ShapeDtypeStruct(rows.shape, BF16)] * (n_y - 1),
            in_specs=[SMEM, VMEM, VMEM],
            out_specs=[VMEM] * n_y,
            compiler_params=params(4),
            cost_estimate=pl.CostEstimate(flops=10**6, bytes_accessed=1 << 18, transcendentals=0),
            name="route",
        )(reader, rows, other)

    def table(kind, coords):
        return pl.pallas_call(
            functools.partial(table_kernel, n_h, kind),
            out_shape=jax.ShapeDtypeStruct((row_block, 64, channels), BF16),
            in_specs=[VMEM] * 2,
            out_specs=VMEM,
            scratch_shapes=[
                pltpu.VMEM((10, row_block, channels), F32),
                pltpu.VMEM((8, row_block, channels), F32),
            ],
            compiler_params=params(16),
            cost_estimate=pl.CostEstimate(flops=10**9, bytes_accessed=4 << 20, transcendentals=1 << 16),
            name=("east", "north")[kind],
        )(coords, channel_freq.reshape(1, channels))

    with jax.named_scope("image_sum"):
        north = table(1, soon)
        images[0], north = lax.optimization_barrier((images[0], north))
        pieces = dict((by, shift(images[by], "y", by)) for by in far_first(n_y))
        pieces = [images[0]] + [pieces[by] for by in range(1, n_y)]
        own_sum, other_sum = pl.pallas_call(
            sum_kernel,
            out_shape=[jax.ShapeDtypeStruct((cell_rows, 128), F32)] * 2,
            in_specs=[VMEM] * n_y,
            out_specs=[VMEM] * 2,
            compiler_params=params(4),
            cost_estimate=pl.CostEstimate(flops=10**6, bytes_accessed=1 << 20, transcendentals=0),
            name="image_sums",
        )(*pieces)
        later, own_sum = lax.optimization_barrier((baseline_coords, own_sum))
        beside_sum = shift(other_sum, "h", 1)

    east = table(0, later)
    came = dict((by, shift(sent[by - 1], "y", by)) for by in far_first(n_y))
    came = [came[by] for by in range(1, n_y)]

    predicted = pl.pallas_call(
        degrid_kernel,
        out_shape=jax.ShapeDtypeStruct((row_block, 2 * channels), F32),
        in_specs=[VMEM] * 4,
        out_specs=VMEM,
        scratch_shapes=[pltpu.VMEM((cell_rows, 128), F32)],
        compiler_params=params(16),
        cost_estimate=pl.CostEstimate(flops=10**9, bytes_accessed=5 << 20, transcendentals=0),
        name="degrid",
    )(own_sum, beside_sum, east, north)

    residual, gridded = pl.pallas_call(
        grid_kernel,
        out_shape=[
            jax.ShapeDtypeStruct((row_block, 2 * channels), F32),
            jax.ShapeDtypeStruct((cell_rows, 128), BF16),
        ],
        in_specs=[VMEM] * 9,
        out_specs=[VMEM] * 2,
        scratch_shapes=[pltpu.VMEM((cell_rows, 128), F32)],
        compiler_params=params(16),
        cost_estimate=pl.CostEstimate(flops=10**9, bytes_accessed=5 << 20, transcendentals=0),
        name="grid",
    )(pick, rows, other, *came, predicted, east, north)

    with jax.named_scope("grid_gather"):
        beside = shift(gridded, "h", 1)
        moved = dict((by, (shift(gridded, "y", by), shift(beside, "y", by))) for by in reversed(far_first(n_y)))
        grids = [gridded, beside]
        for by in range(1, n_y):
            grids += moved[by]

    half = subgrid_count // n_c

    def regrid(other, subgrids):
        return pl.pallas_call(
            functools.partial(regrid_kernel, grid_scale, n_y, n_h, n_c, owned, other),
            out_shape=jax.ShapeDtypeStruct((half, 2 * pixels), F32),
            in_specs=[VMEM] * (2 + n_facet),
            out_specs=VMEM,
            compiler_params=params(8),
            cost_estimate=pl.CostEstimate(flops=10**8, bytes_accessed=3 << 20, transcendentals=0),
            name=("regrid_near", "regrid_far")[other],
        )(subgrids, screen, *grids)

    far_sum = regrid(1, subgrid_index)
    subgrids, far_sum = lax.optimization_barrier((subgrid_index, far_sum))
    near_sum = regrid(0, subgrids)

    with jax.named_scope("dirty_scatter"):
        chip_sum = (near_sum + shift(far_sum, "c", 1)).astype(BF16).reshape(n_x * n_z, owned, 2 * pixels)
        chips = lax.all_to_all(chip_sum, ("x", "z"), split_axis=0, concat_axis=0, tiled=True)
        dirty = jnp.sum(chips.astype(F32), axis=0)
    return (residual[None], dirty[None])


def solution(mesh):
    split = Mesh(mesh.devices.reshape(4, 2, 4, 4, 2), FACET + TILE)
    return jax.shard_map(
        local,
        mesh=split,
        in_specs=(
            P(FACET, TILE, None),
            P(TILE, None),
            P(None, None, TILE),
            P(None, TILE),
            P(None, None, TILE),
            P(None, TILE),
            P(FACET, TILE, None),
            P(FACET, None, None),
            P(),
            P(),
        ),
        out_specs=(P(FACET, TILE, None), P(FACET, TILE, None)),
        check_vma=False,
    )
```

```python
import functools
import math

import jax
import jax.numpy as jnp
from jax import lax
from jax.experimental import pallas as pl
from jax.experimental.pallas import tpu as pltpu
from jax.sharding import Mesh
from jax.sharding import PartitionSpec as P

TWO_PI = 2.0 * math.pi
F32 = jnp.float32
BF16 = jnp.bfloat16
FACET = ("y", "h")
TILE = ("x", "z", "c")
VMEM = pl.BlockSpec(memory_space=pltpu.VMEM)
SMEM = pl.BlockSpec(memory_space=pltpu.SMEM)
ANY = pl.BlockSpec(memory_space=pl.ANY)


def params(mib):
    return pltpu.CompilerParams(vmem_limit_bytes=mib << 20)


def cmul(a, b):
    return (a[0] * b[0] - a[1] * b[1], a[0] * b[1] + a[1] * b[0])


def conj(a):
    return (a[0], -a[1])


def row_of_blocks(values):
    return jnp.concatenate([values[at : at + 1, :] for at in range(values.shape[0])], axis=1)


def down(row):
    return jnp.broadcast_to(row, (128, 128)).T


def onehot(column, first, count):
    lanes = lax.broadcasted_iota(jnp.int32, (128, 128), 1)
    width = min(count, 128)
    parts = [
        jnp.where(column == lanes + (first + at), 1.0, 0.0).astype(BF16)[:, :width] for at in range(0, count, 128)
    ]
    return parts[0] if len(parts) == 1 else jnp.concatenate(parts, axis=1)


def slot_of(subgrid, core, cores, owned):
    held = lax.rem(lax.div(subgrid, owned) + (cores - core), cores)
    return (held * (128 // cores)) + lax.div(subgrid, owned * cores) * owned + lax.rem(subgrid, owned)


def table_kernel(n_h, kind, coords_ref, freq_ref, table_ref, powers, groups):
    rows = coords_ref.shape[2]
    coords = coords_ref[lax.axis_index("y") * n_h + lax.axis_index("h")]
    row = jnp.concatenate([coords[kind : kind + 1], jnp.zeros((1, 128 - rows), F32)], axis=1)
    column = (TWO_PI * down(row)[:rows]) * (1.0 / 32.0)
    angle = jnp.concatenate([column] * (freq_ref.shape[1] // 128), axis=1) * freq_ref[...]
    z1 = (jnp.cos(angle), jnp.sin(angle))
    z2 = cmul(z1, z1)
    z4 = cmul(z2, z2)
    z8 = cmul(z4, z4)
    z16 = cmul(z8, z8)
    low16 = conj(z16)
    for at, value in enumerate((z1, z2, z4, z8, z16)):
        powers[2 * at] = value[0]
        powers[2 * at + 1] = value[1]
    for at, value in enumerate((low16, cmul(low16, z1), cmul(low16, z2), cmul(low16, cmul(z1, z2)))):
        groups[2 * at] = value[0]
        groups[2 * at + 1] = value[1]
    sub = lax.broadcasted_iota(jnp.int32, (8, angle.shape[1]), 0)

    def row_of(ref, at, row):
        return (ref[2 * at, pl.ds(row, 1), :], ref[2 * at + 1, pl.ds(row, 1), :])

    def picked(factor, bit):
        on = (sub & bit) != 0
        return (jnp.where(on, factor[0], 1.0), jnp.where(on, factor[1], 0.0))

    def bits(factors):
        return cmul(cmul(picked(factors[0], 1), picked(factors[1], 2)), picked(factors[2], 4))

    def stacked(parts):
        return jnp.concatenate([part[0] for part in parts] + [part[1] for part in parts], axis=0).astype(BF16)

    def body(b):
        base = bits([row_of(powers, at, b) for at in ((2, 3, 4), (0, 1, 2))[kind]])
        if kind == 0:
            table_ref[b] = stacked([cmul(base, row_of(groups, at, b)) for at in range(4)])
        else:
            up8 = row_of(powers, 3, b)
            table_ref[b] = stacked([cmul(base, row_of(groups, 0, b)), cmul(base, conj(up8)), base, cmul(base, up8)])

    for b in range(rows):
        body(b)


def screen_kernel(stations_from, plane_from, phase_from, beam_from, screen_ref, *refs):
    sources, held, sems = ((stations_from, plane_from, phase_from, beam_from), refs[:4], refs[4])
    copies = [pltpu.make_async_copy(src, dst, sems.at[at]) for at, (src, dst) in enumerate(zip(sources, held))]
    for copy in copies:
        copy.start()
    stations_ref, plane_ref, phase_ref, beam_ref = held
    for copy in copies:
        copy.wait()
    stations = beam_ref.shape[0]
    planes, pixels = phase_ref.shape
    one = onehot(down(row_of_blocks(stations_ref[:, 0, :])), 0, stations)
    two = onehot(down(row_of_blocks(stations_ref[:, 1, :])), 0, stations)
    plane = onehot(down(row_of_blocks(plane_ref[...])), 0, planes).astype(F32)
    width = 256
    for at in range(0, pixels, width):
        re, im = pl.ds(at, width), pl.ds(pixels + at, width)
        one_re = jnp.dot(one, beam_ref[:, re], preferred_element_type=F32)
        one_im = jnp.dot(one, beam_ref[:, im], preferred_element_type=F32)
        two_re = jnp.dot(two, beam_ref[:, re], preferred_element_type=F32)
        two_im = jnp.dot(two, beam_ref[:, im], preferred_element_type=F32)
        pair_re = one_re * two_re + one_im * two_im
        pair_im = one_im * two_re - one_re * two_im
        phase = phase_ref[:, re]
        exact = lax.Precision.HIGHEST
        wave_re = jnp.dot(plane, jnp.cos(phase), precision=exact, preferred_element_type=F32)
        wave_im = jnp.dot(plane, jnp.sin(phase), precision=exact, preferred_element_type=F32)
        screen_ref[:, re] = pair_re * wave_re - pair_im * wave_im
        screen_ref[:, im] = pair_re * wave_im + pair_im * wave_re


def blocks_from(n_y, n_h, sign):
    at_y, at_h = (lax.axis_index("y"), lax.axis_index("h"))
    return [
        lax.rem(at_y + (n_y + sign * by) % n_y, n_y) * n_h + lax.rem(at_h + flip, n_h)
        for by in range(n_y)
        for flip in range(n_h)
    ]


def rows_of_blocks(ref, blocks, cells):
    return jnp.concatenate([ref[pl.ds(pl.multiple_of(block * 16, 16), 16), cells] for block in blocks], axis=0)


def image_kernel(n_y, n_h, cores, owned, subgrid_ref, near_ref, far_ref, screen_ref, *image_refs):
    half = near_ref.shape[0] * near_ref.shape[1]
    pixels = screen_ref.shape[1] // 2
    blocks = blocks_from(n_y, n_h, 1)
    subgrids = jnp.concatenate([subgrid_ref[pl.ds(block, 1), :] for block in blocks], axis=1)
    slots = down(slot_of(subgrids, lax.axis_index("c"), cores, owned))
    near, far = (onehot(slots, 0, half), onehot(slots, half, half))
    tiles = pixels // 128
    width = 256

    def rows_of(cells):
        held = (near_ref[:, :, cells].reshape(half, width), far_ref[:, :, cells].reshape(half, width))
        return jnp.dot(near, held[0], preferred_element_type=F32) + jnp.dot(far, held[1], preferred_element_type=F32)

    for at in range(0, pixels, width):
        re, im = pl.ds(at, width), pl.ds(pixels + at, width)
        model_re, model_im = (rows_of(re), rows_of(im))
        screen_re, screen_im = (rows_of_blocks(screen_ref, blocks, re), rows_of_blocks(screen_ref, blocks, im))
        image_re = (screen_re * model_re - screen_im * model_im).astype(BF16)
        image_im = (screen_re * model_im + screen_im * model_re).astype(BF16)
        for off in range(0, width, 128):
            for image, q in ((image_re, (at + off) // 128), (image_im, (at + off) // 128 + tiles)):
                for j in range(len(blocks)):
                    image_refs[j // n_h][j % n_h, 16 * q : 16 * q + 16, :] = image[
                        16 * j : 16 * j + 16, off : off + 128
                    ]


def sum_kernel(*refs):
    pieces, sums = (refs[:-2], refs[-2:])
    for flip, sum_ref in enumerate(sums):
        total = pieces[0][flip].astype(F32)
        for piece in pieces[1:]:
            total = total + piece[flip].astype(F32)
        sum_ref[...] = total


def route_kernel(n_y, n_h, reader_ref, rows_ref, other_ref, pick_ref, *out_refs):
    at_y, at_h = (lax.axis_index("y"), lax.axis_index("h"))
    own = at_y * n_h + at_h
    source = reader_ref[0, own]
    steps = lax.rem(at_y + n_y - lax.div(source, n_h), n_y)
    here = jnp.where(lax.rem(source, n_h) == at_h, 0, 1)
    pick_ref[...] = jnp.full(pick_ref.shape, jnp.where(steps == 0, here, steps + 1), jnp.int32)
    block = jnp.int32(0)
    for at in range(n_y * n_h):
        block = jnp.where(reader_ref[0, at] == own, at, block)
    for by, out_ref in enumerate(out_refs, 1):
        to = lax.rem(at_y + by, n_y) * n_h + at_h

        @pl.when(block == to)
        def _():
            out_ref[...] = rows_ref[...]

        @pl.when(block != to)
        def _():
            out_ref[...] = other_ref[...]


def degrid_kernel(near_ref, far_ref, east_ref, north_ref, predicted_ref, cells_ref):
    rows, channels = (predicted_ref.shape[0], predicted_ref.shape[1] // 2)
    cells_ref[...] = near_ref[...] + far_ref[...]
    width = 256

    def degrid(b):
        cells = cells_ref[pl.ds(b, 16, stride=16), :]

        def spread(first, second):
            return jnp.concatenate(
                [
                    jnp.concatenate([first[:, 32 * p : 32 * p + 32], second[:, 32 * p : 32 * p + 32]], axis=1)
                    for p in range(4)
                ],
                axis=0,
            )

        image = jnp.concatenate([spread(cells[0:8], -cells[8:16]), spread(cells[8:16], cells[0:8])], axis=0)
        high = image.astype(BF16)
        low = (image - high.astype(F32)).astype(BF16)
        operand = jnp.concatenate([high, low], axis=1)
        for at in range(0, channels, width):
            chans = pl.ds(at, width)
            north = north_ref[b, :, chans]
            inner = jnp.dot(operand, jnp.concatenate([north, north], axis=0), preferred_element_type=F32)
            inner_re, inner_im = (inner[:32], inner[32:])
            east = east_ref[b, :, chans].astype(F32)
            cos, sin = (east[:32], east[32:])
            vis_re = jnp.sum(cos * inner_re - sin * inner_im, axis=0, keepdims=True)
            vis_im = jnp.sum(cos * inner_im + sin * inner_re, axis=0, keepdims=True)
            row = pl.ds(b, 1)
            late = pl.ds(channels + at, width)
            predicted_ref[row, chans] = vis_re
            predicted_ref[row, late] = vis_im

    for b in range(rows):
        degrid(b)


def residual_kernel(pick_ref, *refs):
    found, (predicted_ref, resid_ref) = (refs[:-2], refs[-2:])
    for at in range(0, resid_ref.shape[1], 128):
        chans = pl.ds(at, 128)
        visible = found[0][:, chans].astype(F32)
        for which, ref in enumerate(found[1:], 1):
            visible = jnp.where(pick_ref[...] == which, ref[:, chans].astype(F32), visible)
        resid_ref[:, chans] = visible - predicted_ref[:, chans]


def grid_kernel(
    pick_ref,
    rows_ref,
    other_ref,
    came_1_ref,
    came_2_ref,
    came_3_ref,
    predicted_ref,
    east_ref,
    north_ref,
    grid_ref,
    out_ref,
    resid_ref,
):
    rows, channels = (resid_ref.shape[0], resid_ref.shape[1] // 2)
    residual_kernel(
        pick_ref, rows_ref, other_ref, came_1_ref, came_2_ref, came_3_ref, predicted_ref, resid_ref
    )
    width = 256

    def grid(b):
        products = jnp.zeros((64, 64), F32)
        for at in range(0, channels, width):
            chans, late = (pl.ds(at, width), pl.ds(channels + at, width))
            resid_re, resid_im = (resid_ref[pl.ds(b, 1), chans], resid_ref[pl.ds(b, 1), late])
            east = east_ref[b, :, chans].astype(F32)
            cos, sin = (east[:32], east[32:])
            weighted = jnp.concatenate([cos * resid_re + sin * resid_im, cos * resid_im - sin * resid_re], axis=0)
            products = products + lax.dot_general(
                weighted.astype(BF16),
                north_ref[b, :, chans],
                (((1,), (1,)), ((), ())),
                preferred_element_type=F32,
            )
        halves = (products[:32, :32] + products[32:, 32:], products[32:, :32] - products[:32, 32:])
        out_ref[pl.ds(b, 16, stride=16), :] = jnp.concatenate(
            [jnp.concatenate([half[8 * p : 8 * p + 8] for p in range(4)], axis=1) for half in halves], axis=0
        )

    for b in range(rows):
        grid(b)
    grid_ref[...] = out_ref[...].astype(BF16)


def regrid_kernel(scale, n_y, n_h, cores, owned, other, subgrid_ref, screen_ref, *refs):
    grids, sum_ref = (refs[:-1], refs[-1])
    blocks = blocks_from(n_y, n_h, -1)
    half = sum_ref.shape[0]
    pixels = screen_ref.shape[1] // 2
    tiles = pixels // 128
    count = screen_ref.shape[0]

    def grid_of(q):
        return jnp.concatenate([ref[16 * q : 16 * q + 16, :] for ref in grids], axis=0).astype(F32)

    subs = lax.broadcasted_iota(jnp.int32, (half, count), 0) + other * half
    target = jnp.concatenate([subgrid_ref[pl.ds(block, 1), :] for block in blocks], axis=1)
    target = slot_of(target, lax.axis_index("c"), cores, owned)
    sums = jnp.where(target == subs, 1.0, 0.0).astype(BF16)
    sums = jnp.concatenate([sums, sums], axis=1)
    for q in range(tiles):
        re, im = pl.ds(128 * q, 128), pl.ds(pixels + 128 * q, 128)
        grid_re, grid_im = (grid_of(q), grid_of(q + tiles))
        screen_re, screen_im = (rows_of_blocks(screen_ref, blocks, re), rows_of_blocks(screen_ref, blocks, im))
        out_re = (screen_re * grid_re + screen_im * grid_im) * scale
        out_im = (screen_re * grid_im - screen_im * grid_re) * scale
        value = jnp.concatenate([out_re, out_im], axis=1)
        high = value.astype(BF16)
        low = (value - high.astype(F32)).astype(BF16)
        both = jnp.dot(sums, jnp.concatenate([high, low], axis=0), preferred_element_type=F32)
        sum_ref[:, re] = both[:, :128]
        sum_ref[:, im] = both[:, 128:]


def shift(value, axis, by):
    size = lax.axis_size(axis)
    return lax.ppermute(value, axis, [(i, (i + by) % size) for i in range(size)])


def far_first(size):
    return sorted(range(1, size), key=lambda by: -min(by, size - by))


def local(
    sectioned_rows,
    reader,
    baseline_coords,
    subgrid_index,
    stations,
    plane_index,
    model_grid,
    beam_screens,
    plane_phase,
    channel_freq,
):
    n_y, n_h, n_x, n_z, n_c = (lax.axis_size(axis) for axis in FACET + TILE)
    n_facet = n_y * n_h
    channels = channel_freq.shape[0]
    pixels = plane_phase.shape[1]
    row_block = sectioned_rows.shape[1]
    count = n_facet * row_block
    owned = model_grid.shape[1]
    subgrid_count = owned * n_x * n_z * n_c
    cell_rows = 2 * pixels // 128 * row_block
    grid_scale = 1.0 / math.sqrt(channels * n_facet * (row_block * n_x * n_z * n_c) / subgrid_count)
    with jax.named_scope("model_gather"):
        copies = jnp.broadcast_to(model_grid, (n_x * n_z, owned, 2 * pixels))
        near = lax.all_to_all(copies, ("x", "z"), split_axis=0, concat_axis=0, tiled=True)

    operands = (stations, plane_index, plane_phase, beam_screens[0])
    screen = pl.pallas_call(
        screen_kernel,
        out_shape=jax.ShapeDtypeStruct((count, 2 * pixels), F32),
        in_specs=[ANY] * len(operands),
        out_specs=VMEM,
        scratch_shapes=[pltpu.VMEM(value.shape, value.dtype) for value in operands]
        + [pltpu.SemaphoreType.DMA((len(operands),))],
        compiler_params=params(44),
        cost_estimate=pl.CostEstimate(flops=10**9, bytes_accessed=4 << 20, transcendentals=1 << 16),
        name="screens",
    )(*operands)

    near, screen = lax.optimization_barrier((near, screen))
    far = shift(near, "c", 1)
    images = pl.pallas_call(
        functools.partial(image_kernel, n_y, n_h, n_c, owned),
        out_shape=[jax.ShapeDtypeStruct((n_h, cell_rows, 128), BF16)] * n_y,
        in_specs=[VMEM] * 4,
        out_specs=[VMEM] * n_y,
        compiler_params=params(8),
        cost_estimate=pl.CostEstimate(flops=10**8, bytes_accessed=2 << 20, transcendentals=0),
        name="images",
    )(subgrid_index, near, far, screen)
    rows, soon, *images = lax.optimization_barrier((sectioned_rows[0], baseline_coords, *images))

    with jax.named_scope("visible_route"):
        other = shift(rows, "h", 1)
        pick, *sent = pl.pallas_call(
            functools.partial(route_kernel, n_y, n_h),
            out_shape=[jax.ShapeDtypeStruct((row_block, 128), jnp.int32)]
            + [jax.ShapeDtypeStruct(rows.shape, BF16)] * (n_y - 1),
            in_specs=[SMEM, VMEM, VMEM],
            out_specs=[VMEM] * n_y,
            compiler_params=params(4),
            cost_estimate=pl.CostEstimate(flops=10**6, bytes_accessed=1 << 18, transcendentals=0),
            name="route",
        )(reader, rows, other)

    def table(kind, coords):
        return pl.pallas_call(
            functools.partial(table_kernel, n_h, kind),
            out_shape=jax.ShapeDtypeStruct((row_block, 64, channels), BF16),
            in_specs=[VMEM] * 2,
            out_specs=VMEM,
            scratch_shapes=[
                pltpu.VMEM((10, row_block, channels), F32),
                pltpu.VMEM((8, row_block, channels), F32),
            ],
            compiler_params=params(16),
            cost_estimate=pl.CostEstimate(flops=10**9, bytes_accessed=4 << 20, transcendentals=1 << 16),
            name=("east", "north")[kind],
        )(coords, channel_freq.reshape(1, channels))

    with jax.named_scope("image_sum"):
        north = table(1, soon)
        images[0], north = lax.optimization_barrier((images[0], north))
        pieces = dict((by, shift(images[by], "y", by)) for by in far_first(n_y))
        pieces = [images[0]] + [pieces[by] for by in range(1, n_y)]
        own_sum, other_sum = pl.pallas_call(
            sum_kernel,
            out_shape=[jax.ShapeDtypeStruct((cell_rows, 128), F32)] * 2,
            in_specs=[VMEM] * n_y,
            out_specs=[VMEM] * 2,
            compiler_params=params(4),
            cost_estimate=pl.CostEstimate(flops=10**6, bytes_accessed=1 << 20, transcendentals=0),
            name="image_sums",
        )(*pieces)
        later, own_sum = lax.optimization_barrier((baseline_coords, own_sum))
        beside_sum = shift(other_sum, "h", 1)

    east = table(0, later)
    came = dict((by, shift(sent[by - 1], "y", by)) for by in far_first(n_y))
    came = [came[by] for by in range(1, n_y)]

    predicted = pl.pallas_call(
        degrid_kernel,
        out_shape=jax.ShapeDtypeStruct((row_block, 2 * channels), F32),
        in_specs=[VMEM] * 4,
        out_specs=VMEM,
        scratch_shapes=[pltpu.VMEM((cell_rows, 128), F32)],
        compiler_params=params(16),
        cost_estimate=pl.CostEstimate(flops=10**9, bytes_accessed=5 << 20, transcendentals=0),
        name="degrid",
    )(own_sum, beside_sum, east, north)

    operands = (pick, rows, other, *came, predicted)
    gridded = pl.pallas_call(
        grid_kernel,
        out_shape=jax.ShapeDtypeStruct((cell_rows, 128), BF16),
        in_specs=[VMEM] * 9,
        out_specs=VMEM,
        scratch_shapes=[pltpu.VMEM((cell_rows, 128), F32), pltpu.VMEM(predicted.shape, F32)],
        compiler_params=params(16),
        cost_estimate=pl.CostEstimate(flops=10**9, bytes_accessed=5 << 20, transcendentals=0),
        name="grid",
    )(*operands, east, north)

    with jax.named_scope("grid_gather"):
        beside = shift(gridded, "h", 1)
        moved = dict((by, (shift(gridded, "y", by), shift(beside, "y", by))) for by in reversed(far_first(n_y)))
        grids = [gridded, beside]
        for by in range(1, n_y):
            grids += moved[by]

    first, *operands = operands
    first, grids[1] = lax.optimization_barrier((first, grids[1]))
    residual = pl.pallas_call(
        residual_kernel,
        out_shape=jax.ShapeDtypeStruct(predicted.shape, F32),
        in_specs=[VMEM] * 7,
        out_specs=VMEM,
        compiler_params=params(4),
        cost_estimate=pl.CostEstimate(flops=10**6, bytes_accessed=1 << 19, transcendentals=0),
        name="residual",
    )(first, *operands)

    half = subgrid_count // n_c

    def regrid(other, subgrids):
        return pl.pallas_call(
            functools.partial(regrid_kernel, grid_scale, n_y, n_h, n_c, owned, other),
            out_shape=jax.ShapeDtypeStruct((half, 2 * pixels), F32),
            in_specs=[VMEM] * (2 + n_facet),
            out_specs=VMEM,
            compiler_params=params(8),
            cost_estimate=pl.CostEstimate(flops=10**8, bytes_accessed=3 << 20, transcendentals=0),
            name=("regrid_near", "regrid_far")[other],
        )(subgrids, screen, *grids)

    subgrids, residual = lax.optimization_barrier((subgrid_index, residual))
    far_sum = regrid(1, subgrids)
    subgrids, far_sum = lax.optimization_barrier((subgrid_index, far_sum))
    near_sum = regrid(0, subgrids)

    with jax.named_scope("dirty_scatter"):
        chip_sum = (near_sum + shift(far_sum, "c", 1)).astype(BF16).reshape(n_x * n_z, owned, 2 * pixels)
        chips = lax.all_to_all(chip_sum, ("x", "z"), split_axis=0, concat_axis=0, tiled=True)
        dirty = jnp.sum(chips.astype(F32), axis=0)
    return (residual[None], dirty[None])


def solution(mesh):
    split = Mesh(mesh.devices.reshape(4, 2, 4, 4, 2), FACET + TILE)
    return jax.shard_map(
        local,
        mesh=split,
        in_specs=(
            P(FACET, TILE, None),
            P(TILE, None),
            P(None, None, TILE),
            P(None, TILE),
            P(None, None, TILE),
            P(None, TILE),
            P(FACET, TILE, None),
            P(FACET, None, None),
            P(),
            P(),
        ),
        out_specs=(P(FACET, TILE, None), P(FACET, TILE, None)),
        check_vma=False,
    )
```

```python
import functools
import math

import jax
import jax.numpy as jnp
from jax import lax
from jax.experimental import pallas as pl
from jax.experimental.pallas import tpu as pltpu
from jax.sharding import Mesh
from jax.sharding import PartitionSpec as P

TWO_PI = 2.0 * math.pi
F32 = jnp.float32
BF16 = jnp.bfloat16
FACET = ("y", "h")
TILE = ("x", "z", "c")
VMEM = pl.BlockSpec(memory_space=pltpu.VMEM)
SMEM = pl.BlockSpec(memory_space=pltpu.SMEM)
ANY = pl.BlockSpec(memory_space=pl.ANY)


def params(mib):
    return pltpu.CompilerParams(vmem_limit_bytes=mib << 20)


def cmul(a, b):
    return (a[0] * b[0] - a[1] * b[1], a[0] * b[1] + a[1] * b[0])


def conj(a):
    return (a[0], -a[1])


def row_of_blocks(values):
    return jnp.concatenate([values[at : at + 1, :] for at in range(values.shape[0])], axis=1)


def down(row):
    return jnp.broadcast_to(row, (128, 128)).T


def onehot(column, first, count):
    lanes = lax.broadcasted_iota(jnp.int32, (128, 128), 1)
    width = min(count, 128)
    parts = [
        jnp.where(column == lanes + (first + at), 1.0, 0.0).astype(BF16)[:, :width] for at in range(0, count, 128)
    ]
    return parts[0] if len(parts) == 1 else jnp.concatenate(parts, axis=1)


def slot_of(subgrid, core, cores, owned):
    held = lax.rem(lax.div(subgrid, owned) + (cores - core), cores)
    return (held * (128 // cores)) + lax.div(subgrid, owned * cores) * owned + lax.rem(subgrid, owned)


def table_kernel(n_h, kind, coords_ref, freq_ref, table_ref, powers, groups):
    rows = coords_ref.shape[2]
    coords = coords_ref[lax.axis_index("y") * n_h + lax.axis_index("h")]
    row = jnp.concatenate([coords[kind : kind + 1], jnp.zeros((1, 128 - rows), F32)], axis=1)
    column = (TWO_PI * down(row)[:rows]) * (1.0 / 32.0)
    angle = jnp.concatenate([column] * (freq_ref.shape[1] // 128), axis=1) * freq_ref[...]
    z1 = (jnp.cos(angle), jnp.sin(angle))
    z2 = cmul(z1, z1)
    z4 = cmul(z2, z2)
    z8 = cmul(z4, z4)
    z16 = cmul(z8, z8)
    low16 = conj(z16)
    for at, value in enumerate((z1, z2, z4, z8, z16)):
        powers[2 * at] = value[0]
        powers[2 * at + 1] = value[1]
    for at, value in enumerate((low16, cmul(low16, z1), cmul(low16, z2), cmul(low16, cmul(z1, z2)))):
        groups[2 * at] = value[0]
        groups[2 * at + 1] = value[1]
    sub = lax.broadcasted_iota(jnp.int32, (8, angle.shape[1]), 0)

    def row_of(ref, at, row):
        return (ref[2 * at, pl.ds(row, 1), :], ref[2 * at + 1, pl.ds(row, 1), :])

    def picked(factor, bit):
        on = (sub & bit) != 0
        return (jnp.where(on, factor[0], 1.0), jnp.where(on, factor[1], 0.0))

    def bits(factors):
        return cmul(cmul(picked(factors[0], 1), picked(factors[1], 2)), picked(factors[2], 4))

    def stacked(parts):
        return jnp.concatenate([part[0] for part in parts] + [part[1] for part in parts], axis=0).astype(BF16)

    def body(b):
        base = bits([row_of(powers, at, b) for at in ((2, 3, 4), (0, 1, 2))[kind]])
        if kind == 0:
            table_ref[b] = stacked([cmul(base, row_of(groups, at, b)) for at in range(4)])
        else:
            up8 = row_of(powers, 3, b)
            table_ref[b] = stacked([cmul(base, row_of(groups, 0, b)), cmul(base, conj(up8)), base, cmul(base, up8)])

    for b in range(rows):
        body(b)


def screen_kernel(stations_from, plane_from, phase_from, beam_from, screen_ref, *refs):
    sources, held, sems = ((stations_from, plane_from, phase_from, beam_from), refs[:4], refs[4])
    copies = [pltpu.make_async_copy(src, dst, sems.at[at]) for at, (src, dst) in enumerate(zip(sources, held))]
    for copy in copies:
        copy.start()
    stations_ref, plane_ref, phase_ref, beam_ref = held
    for copy in copies:
        copy.wait()
    stations = beam_ref.shape[0]
    planes, pixels = phase_ref.shape
    one = onehot(down(row_of_blocks(stations_ref[:, 0, :])), 0, stations)
    two = onehot(down(row_of_blocks(stations_ref[:, 1, :])), 0, stations)
    plane = onehot(down(row_of_blocks(plane_ref[...])), 0, planes).astype(F32)
    width = 256
    for at in range(0, pixels, width):
        re, im = pl.ds(at, width), pl.ds(pixels + at, width)
        one_re = jnp.dot(one, beam_ref[:, re], preferred_element_type=F32)
        one_im = jnp.dot(one, beam_ref[:, im], preferred_element_type=F32)
        two_re = jnp.dot(two, beam_ref[:, re], preferred_element_type=F32)
        two_im = jnp.dot(two, beam_ref[:, im], preferred_element_type=F32)
        pair_re = one_re * two_re + one_im * two_im
        pair_im = one_im * two_re - one_re * two_im
        phase = phase_ref[:, re]
        exact = lax.Precision.HIGHEST
        wave_re = jnp.dot(plane, jnp.cos(phase), precision=exact, preferred_element_type=F32)
        wave_im = jnp.dot(plane, jnp.sin(phase), precision=exact, preferred_element_type=F32)
        screen_ref[:, re] = pair_re * wave_re - pair_im * wave_im
        screen_ref[:, im] = pair_re * wave_im + pair_im * wave_re


def blocks_from(n_y, n_h, sign):
    at_y, at_h = (lax.axis_index("y"), lax.axis_index("h"))
    return [
        lax.rem(at_y + (n_y + sign * by) % n_y, n_y) * n_h + lax.rem(at_h + flip, n_h)
        for by in range(n_y)
        for flip in range(n_h)
    ]


def rows_of_blocks(ref, blocks, cells):
    return jnp.concatenate([ref[pl.ds(pl.multiple_of(block * 16, 16), 16), cells] for block in blocks], axis=0)


def image_kernel(n_y, n_h, cores, owned, subgrid_ref, near_ref, far_ref, screen_ref, *image_refs):
    half = near_ref.shape[0] * near_ref.shape[1]
    pixels = screen_ref.shape[1] // 2
    blocks = blocks_from(n_y, n_h, 1)
    subgrids = jnp.concatenate([subgrid_ref[pl.ds(block, 1), :] for block in blocks], axis=1)
    slots = down(slot_of(subgrids, lax.axis_index("c"), cores, owned))
    near, far = (onehot(slots, 0, half), onehot(slots, half, half))
    tiles = pixels // 128
    width = 256

    def rows_of(cells):
        held = (near_ref[:, :, cells].reshape(half, width), far_ref[:, :, cells].reshape(half, width))
        return jnp.dot(near, held[0], preferred_element_type=F32) + jnp.dot(far, held[1], preferred_element_type=F32)

    for at in range(0, pixels, width):
        re, im = pl.ds(at, width), pl.ds(pixels + at, width)
        model_re, model_im = (rows_of(re), rows_of(im))
        screen_re, screen_im = (rows_of_blocks(screen_ref, blocks, re), rows_of_blocks(screen_ref, blocks, im))
        image_re = (screen_re * model_re - screen_im * model_im).astype(BF16)
        image_im = (screen_re * model_im + screen_im * model_re).astype(BF16)
        for off in range(0, width, 128):
            for image, q in ((image_re, (at + off) // 128), (image_im, (at + off) // 128 + tiles)):
                for j in range(len(blocks)):
                    image_refs[j // n_h][j % n_h, 16 * q : 16 * q + 16, :] = image[
                        16 * j : 16 * j + 16, off : off + 128
                    ]


def sum_kernel(*refs):
    pieces, sums = (refs[:-2], refs[-2:])
    for flip, sum_ref in enumerate(sums):
        total = pieces[0][flip].astype(F32)
        for piece in pieces[1:]:
            total = total + piece[flip].astype(F32)
        sum_ref[...] = total


def route_kernel(n_y, n_h, reader_ref, rows_ref, other_ref, pick_ref, *out_refs):
    at_y, at_h = (lax.axis_index("y"), lax.axis_index("h"))
    own = at_y * n_h + at_h
    source = reader_ref[0, own]
    steps = lax.rem(at_y + n_y - lax.div(source, n_h), n_y)
    here = jnp.where(lax.rem(source, n_h) == at_h, 0, 1)
    pick_ref[...] = jnp.full(pick_ref.shape, jnp.where(steps == 0, here, steps + 1), jnp.int32)
    block = jnp.int32(0)
    for at in range(n_y * n_h):
        block = jnp.where(reader_ref[0, at] == own, at, block)
    for by, out_ref in enumerate(out_refs, 1):
        to = lax.rem(at_y + by, n_y) * n_h + at_h

        @pl.when(block == to)
        def _():
            out_ref[...] = rows_ref[...]

        @pl.when(block != to)
        def _():
            out_ref[...] = other_ref[...]


def degrid_kernel(near_ref, far_ref, east_ref, north_ref, predicted_ref, cells_ref):
    rows, channels = (predicted_ref.shape[0], predicted_ref.shape[1] // 2)
    cells_ref[...] = near_ref[...] + far_ref[...]
    width = 256

    def degrid(b):
        cells = cells_ref[pl.ds(b, 16, stride=16), :]

        def spread(first, second):
            return jnp.concatenate(
                [
                    jnp.concatenate([first[:, 32 * p : 32 * p + 32], second[:, 32 * p : 32 * p + 32]], axis=1)
                    for p in range(4)
                ],
                axis=0,
            )

        image = jnp.concatenate([spread(cells[0:8], -cells[8:16]), spread(cells[8:16], cells[0:8])], axis=0)
        high = image.astype(BF16)
        low = (image - high.astype(F32)).astype(BF16)
        for at in range(0, channels, width):
            chans = pl.ds(at, width)
            north = north_ref[b, :, chans]
            inner = jnp.dot(high, north, preferred_element_type=F32) + jnp.dot(low, north, preferred_element_type=F32)
            inner_re, inner_im = (inner[:32], inner[32:])
            east = east_ref[b, :, chans].astype(F32)
            cos, sin = (east[:32], east[32:])
            vis_re = jnp.sum(cos * inner_re - sin * inner_im, axis=0, keepdims=True)
            vis_im = jnp.sum(cos * inner_im + sin * inner_re, axis=0, keepdims=True)
            row = pl.ds(b, 1)
            late = pl.ds(channels + at, width)
            predicted_ref[row, chans] = vis_re
            predicted_ref[row, late] = vis_im

    for b in range(rows):
        degrid(b)


def residual_kernel(pick_ref, *refs):
    found, (predicted_ref, resid_ref) = (refs[:-2], refs[-2:])
    for at in range(0, resid_ref.shape[1], 128):
        chans = pl.ds(at, 128)
        visible = found[0][:, chans].astype(F32)
        for which, ref in enumerate(found[1:], 1):
            visible = jnp.where(pick_ref[...] == which, ref[:, chans].astype(F32), visible)
        resid_ref[:, chans] = visible - predicted_ref[:, chans]


def grid_kernel(
    pick_ref,
    rows_ref,
    other_ref,
    came_1_ref,
    came_2_ref,
    came_3_ref,
    predicted_ref,
    east_ref,
    north_ref,
    grid_ref,
    out_ref,
    resid_ref,
):
    rows, channels = (resid_ref.shape[0], resid_ref.shape[1] // 2)
    residual_kernel(
        pick_ref, rows_ref, other_ref, came_1_ref, came_2_ref, came_3_ref, predicted_ref, resid_ref
    )
    width = 512

    def grid(b):
        products = jnp.zeros((64, 64), F32)
        for at in range(0, channels, width):
            chans, late = (pl.ds(at, width), pl.ds(channels + at, width))
            resid_re, resid_im = (resid_ref[pl.ds(b, 1), chans], resid_ref[pl.ds(b, 1), late])
            east = east_ref[b, :, chans].astype(F32)
            cos, sin = (east[:32], east[32:])
            weighted = jnp.concatenate([cos * resid_re + sin * resid_im, cos * resid_im - sin * resid_re], axis=0)
            products = products + lax.dot_general(
                weighted.astype(BF16),
                north_ref[b, :, chans],
                (((1,), (1,)), ((), ())),
                preferred_element_type=F32,
            )
        halves = (products[:32, :32] + products[32:, 32:], products[32:, :32] - products[:32, 32:])
        out_ref[pl.ds(b, 16, stride=16), :] = jnp.concatenate(
            [jnp.concatenate([half[8 * p : 8 * p + 8] for p in range(4)], axis=1) for half in halves], axis=0
        )

    for b in range(rows):
        grid(b)
    grid_ref[...] = out_ref[...].astype(BF16)


def regrid_kernel(scale, n_y, n_h, cores, owned, other, subgrid_ref, screen_ref, *refs):
    grids, sum_ref = (refs[:-1], refs[-1])
    blocks = blocks_from(n_y, n_h, -1)
    half = sum_ref.shape[0]
    pixels = screen_ref.shape[1] // 2
    tiles = pixels // 128
    count = screen_ref.shape[0]

    def grid_of(q):
        return jnp.concatenate([ref[16 * q : 16 * q + 16, :] for ref in grids], axis=0).astype(F32)

    subs = lax.broadcasted_iota(jnp.int32, (half, count), 0) + other * half
    target = jnp.concatenate([subgrid_ref[pl.ds(block, 1), :] for block in blocks], axis=1)
    target = slot_of(target, lax.axis_index("c"), cores, owned)
    sums = jnp.where(target == subs, 1.0, 0.0).astype(BF16)
    sums = jnp.concatenate([sums, sums], axis=1)
    for q in range(tiles):
        re, im = pl.ds(128 * q, 128), pl.ds(pixels + 128 * q, 128)
        grid_re, grid_im = (grid_of(q), grid_of(q + tiles))
        screen_re, screen_im = (rows_of_blocks(screen_ref, blocks, re), rows_of_blocks(screen_ref, blocks, im))
        out_re = (screen_re * grid_re + screen_im * grid_im) * scale
        out_im = (screen_re * grid_im - screen_im * grid_re) * scale
        value = jnp.concatenate([out_re, out_im], axis=1)
        high = value.astype(BF16)
        low = (value - high.astype(F32)).astype(BF16)
        both = jnp.dot(sums, jnp.concatenate([high, low], axis=0), preferred_element_type=F32)
        sum_ref[:, re] = both[:, :128].astype(sum_ref.dtype)
        sum_ref[:, im] = both[:, 128:].astype(sum_ref.dtype)


def shift(value, axis, by):
    size = lax.axis_size(axis)
    return lax.ppermute(value, axis, [(i, (i + by) % size) for i in range(size)])


def far_first(size):
    return sorted(range(1, size), key=lambda by: -min(by, size - by))


def local(
    sectioned_rows,
    reader,
    baseline_coords,
    subgrid_index,
    stations,
    plane_index,
    model_grid,
    beam_screens,
    plane_phase,
    channel_freq,
):
    n_y, n_h, n_x, n_z, n_c = (lax.axis_size(axis) for axis in FACET + TILE)
    n_facet = n_y * n_h
    channels = channel_freq.shape[0]
    pixels = plane_phase.shape[1]
    row_block = sectioned_rows.shape[1]
    count = n_facet * row_block
    owned = model_grid.shape[1]
    subgrid_count = owned * n_x * n_z * n_c
    cell_rows = 2 * pixels // 128 * row_block
    grid_scale = 1.0 / math.sqrt(channels * n_facet * (row_block * n_x * n_z * n_c) / subgrid_count)
    with jax.named_scope("model_gather"):
        copies = jnp.broadcast_to(model_grid, (n_x * n_z, owned, 2 * pixels))
        near = lax.all_to_all(copies, ("x", "z"), split_axis=0, concat_axis=0, tiled=True)

    operands = (stations, plane_index, plane_phase, beam_screens[0])
    screen = pl.pallas_call(
        screen_kernel,
        out_shape=jax.ShapeDtypeStruct((count, 2 * pixels), F32),
        in_specs=[ANY] * len(operands),
        out_specs=VMEM,
        scratch_shapes=[pltpu.VMEM(value.shape, value.dtype) for value in operands]
        + [pltpu.SemaphoreType.DMA((len(operands),))],
        compiler_params=params(44),
        cost_estimate=pl.CostEstimate(flops=10**9, bytes_accessed=4 << 20, transcendentals=1 << 16),
        name="screens",
    )(*operands)

    near, screen = lax.optimization_barrier((near, screen))
    far = shift(near, "c", 1)
    images = pl.pallas_call(
        functools.partial(image_kernel, n_y, n_h, n_c, owned),
        out_shape=[jax.ShapeDtypeStruct((n_h, cell_rows, 128), BF16)] * n_y,
        in_specs=[VMEM] * 4,
        out_specs=[VMEM] * n_y,
        compiler_params=params(8),
        cost_estimate=pl.CostEstimate(flops=10**8, bytes_accessed=2 << 20, transcendentals=0),
        name="images",
    )(subgrid_index, near, far, screen)
    rows, soon, *images = lax.optimization_barrier((sectioned_rows[0], baseline_coords, *images))

    with jax.named_scope("visible_route"):
        other = shift(rows, "h", 1)
        pick, *sent = pl.pallas_call(
            functools.partial(route_kernel, n_y, n_h),
            out_shape=[jax.ShapeDtypeStruct((row_block, 128), jnp.int32)]
            + [jax.ShapeDtypeStruct(rows.shape, BF16)] * (n_y - 1),
            in_specs=[SMEM, VMEM, VMEM],
            out_specs=[VMEM] * n_y,
            compiler_params=params(4),
            cost_estimate=pl.CostEstimate(flops=10**6, bytes_accessed=1 << 18, transcendentals=0),
            name="route",
        )(reader, rows, other)

    def table(kind, coords):
        return pl.pallas_call(
            functools.partial(table_kernel, n_h, kind),
            out_shape=jax.ShapeDtypeStruct((row_block, 64, channels), BF16),
            in_specs=[VMEM] * 2,
            out_specs=VMEM,
            scratch_shapes=[
                pltpu.VMEM((10, row_block, channels), F32),
                pltpu.VMEM((8, row_block, channels), F32),
            ],
            compiler_params=params(16),
            cost_estimate=pl.CostEstimate(flops=10**9, bytes_accessed=4 << 20, transcendentals=1 << 16),
            name=("east", "north")[kind],
        )(coords, channel_freq.reshape(1, channels))

    with jax.named_scope("image_sum"):
        north = table(1, soon)
        images[0], north = lax.optimization_barrier((images[0], north))
        pieces = dict((by, shift(images[by], "y", by)) for by in far_first(n_y))
        pieces = [images[0]] + [pieces[by] for by in range(1, n_y)]
        own_sum, other_sum = pl.pallas_call(
            sum_kernel,
            out_shape=[jax.ShapeDtypeStruct((cell_rows, 128), F32)] * 2,
            in_specs=[VMEM] * n_y,
            out_specs=[VMEM] * 2,
            compiler_params=params(4),
            cost_estimate=pl.CostEstimate(flops=10**6, bytes_accessed=1 << 20, transcendentals=0),
            name="image_sums",
        )(*pieces)
        later, own_sum = lax.optimization_barrier((baseline_coords, own_sum))
        beside_sum = shift(other_sum, "h", 1)

    east = table(0, later)
    came = dict((by, shift(sent[by - 1], "y", by)) for by in far_first(n_y))
    came = [came[by] for by in range(1, n_y)]

    predicted = pl.pallas_call(
        degrid_kernel,
        out_shape=jax.ShapeDtypeStruct((row_block, 2 * channels), F32),
        in_specs=[VMEM] * 4,
        out_specs=VMEM,
        scratch_shapes=[pltpu.VMEM((cell_rows, 128), F32)],
        compiler_params=params(16),
        cost_estimate=pl.CostEstimate(flops=10**9, bytes_accessed=5 << 20, transcendentals=0),
        name="degrid",
    )(own_sum, beside_sum, east, north)

    operands = (pick, rows, other, *came, predicted)
    gridded = pl.pallas_call(
        grid_kernel,
        out_shape=jax.ShapeDtypeStruct((cell_rows, 128), BF16),
        in_specs=[VMEM] * 9,
        out_specs=VMEM,
        scratch_shapes=[pltpu.VMEM((cell_rows, 128), F32), pltpu.VMEM(predicted.shape, F32)],
        compiler_params=params(16),
        cost_estimate=pl.CostEstimate(flops=10**9, bytes_accessed=5 << 20, transcendentals=0),
        name="grid",
    )(*operands, east, north)

    with jax.named_scope("grid_gather"):
        beside = shift(gridded, "h", 1)
        moved = dict((by, (shift(gridded, "y", by), shift(beside, "y", by))) for by in reversed(far_first(n_y)))
        grids = [gridded, beside]
        for by in range(1, n_y):
            grids += moved[by]

    first, *operands = operands
    first, grids[1] = lax.optimization_barrier((first, grids[1]))
    residual = pl.pallas_call(
        residual_kernel,
        out_shape=jax.ShapeDtypeStruct(predicted.shape, F32),
        in_specs=[VMEM] * 7,
        out_specs=VMEM,
        compiler_params=params(4),
        cost_estimate=pl.CostEstimate(flops=10**6, bytes_accessed=1 << 19, transcendentals=0),
        name="residual",
    )(first, *operands)

    half = subgrid_count // n_c

    def regrid(other, subgrids):
        return pl.pallas_call(
            functools.partial(regrid_kernel, grid_scale, n_y, n_h, n_c, owned, other),
            out_shape=jax.ShapeDtypeStruct((half, 2 * pixels), (F32, BF16)[other]),
            in_specs=[VMEM] * (2 + n_facet),
            out_specs=VMEM,
            compiler_params=params(8),
            cost_estimate=pl.CostEstimate(flops=10**8, bytes_accessed=3 << 20, transcendentals=0),
            name=("regrid_near", "regrid_far")[other],
        )(subgrids, screen, *grids)

    subgrids, residual = lax.optimization_barrier((subgrid_index, residual))
    far_sum = regrid(1, subgrids)
    subgrids, far_sum = lax.optimization_barrier((subgrid_index, far_sum))
    near_sum = regrid(0, subgrids)

    with jax.named_scope("dirty_scatter"):
        chip_sum = (near_sum + shift(far_sum, "c", 1).astype(F32)).astype(BF16).reshape(n_x * n_z, owned, 2 * pixels)
        chips = lax.all_to_all(chip_sum, ("x", "z"), split_axis=0, concat_axis=0, tiled=True)
        dirty = jnp.sum(chips.astype(F32), axis=0)
    return (residual[None], dirty[None])


def solution(mesh):
    split = Mesh(mesh.devices.reshape(4, 2, 4, 4, 2), FACET + TILE)
    return jax.shard_map(
        local,
        mesh=split,
        in_specs=(
            P(FACET, TILE, None),
            P(TILE, None),
            P(None, None, TILE),
            P(None, TILE),
            P(None, None, TILE),
            P(None, TILE),
            P(FACET, TILE, None),
            P(FACET, None, None),
            P(),
            P(),
        ),
        out_specs=(P(FACET, TILE, None), P(FACET, TILE, None)),
        check_vma=False,
    )
```

```python
import functools
import math

import jax
import jax.numpy as jnp
from jax import lax
from jax.experimental import pallas as pl
from jax.experimental.pallas import tpu as pltpu
from jax.sharding import Mesh
from jax.sharding import PartitionSpec as P

TWO_PI = 2.0 * math.pi
F32 = jnp.float32
BF16 = jnp.bfloat16
FACET = ("y", "h")
TILE = ("x", "z", "c")
VMEM = pl.BlockSpec(memory_space=pltpu.VMEM)
SMEM = pl.BlockSpec(memory_space=pltpu.SMEM)
ANY = pl.BlockSpec(memory_space=pl.ANY)


def params(mib):
    return pltpu.CompilerParams(vmem_limit_bytes=mib << 20)


def cmul(a, b):
    return (a[0] * b[0] - a[1] * b[1], a[0] * b[1] + a[1] * b[0])


def conj(a):
    return (a[0], -a[1])


def row_of_blocks(values):
    return jnp.concatenate([values[at : at + 1, :] for at in range(values.shape[0])], axis=1)


def down(row):
    return jnp.broadcast_to(row, (128, 128)).T


def onehot(column, first, count):
    lanes = lax.broadcasted_iota(jnp.int32, (128, 128), 1)
    width = min(count, 128)
    parts = [
        jnp.where(column == lanes + (first + at), 1.0, 0.0).astype(BF16)[:, :width] for at in range(0, count, 128)
    ]
    return parts[0] if len(parts) == 1 else jnp.concatenate(parts, axis=1)


def slot_of(subgrid, core, cores, owned):
    held = lax.rem(lax.div(subgrid, owned) + (cores - core), cores)
    return (held * (128 // cores)) + lax.div(subgrid, owned * cores) * owned + lax.rem(subgrid, owned)


def table_kernel(n_h, kind, coords_ref, freq_ref, table_ref, powers, groups):
    rows = coords_ref.shape[2]
    coords = coords_ref[lax.axis_index("y") * n_h + lax.axis_index("h")]
    row = jnp.concatenate([coords[kind : kind + 1], jnp.zeros((1, 128 - rows), F32)], axis=1)
    column = (TWO_PI * down(row)[:rows]) * (1.0 / 32.0)
    angle = jnp.concatenate([column] * (freq_ref.shape[1] // 128), axis=1) * freq_ref[...]
    z1 = (jnp.cos(angle), jnp.sin(angle))
    z2 = cmul(z1, z1)
    z4 = cmul(z2, z2)
    z8 = cmul(z4, z4)
    z16 = cmul(z8, z8)
    low16 = conj(z16)
    for at, value in enumerate((z1, z2, z4, z8, z16)):
        powers[2 * at] = value[0]
        powers[2 * at + 1] = value[1]
    for at, value in enumerate((low16, cmul(low16, z1), cmul(low16, z2), cmul(low16, cmul(z1, z2)))):
        groups[2 * at] = value[0]
        groups[2 * at + 1] = value[1]
    sub = lax.broadcasted_iota(jnp.int32, (8, angle.shape[1]), 0)

    def row_of(ref, at, row):
        return (ref[2 * at, pl.ds(row, 1), :], ref[2 * at + 1, pl.ds(row, 1), :])

    def picked(factor, bit):
        on = (sub & bit) != 0
        return (jnp.where(on, factor[0], 1.0), jnp.where(on, factor[1], 0.0))

    def bits(factors):
        return cmul(cmul(picked(factors[0], 1), picked(factors[1], 2)), picked(factors[2], 4))

    def stacked(parts):
        return jnp.concatenate([part[0] for part in parts] + [part[1] for part in parts], axis=0).astype(BF16)

    def body(b):
        base = bits([row_of(powers, at, b) for at in ((2, 3, 4), (0, 1, 2))[kind]])
        if kind == 0:
            table_ref[b] = stacked([cmul(base, row_of(groups, at, b)) for at in range(4)])
        else:
            up8 = row_of(powers, 3, b)
            table_ref[b] = stacked([cmul(base, row_of(groups, 0, b)), cmul(base, conj(up8)), base, cmul(base, up8)])

    for b in range(rows):
        body(b)


def screen_kernel(stations_from, plane_from, phase_from, beam_from, screen_ref, *refs):
    sources, held, sems = ((stations_from, plane_from, phase_from, beam_from), refs[:4], refs[4])
    copies = [pltpu.make_async_copy(src, dst, sems.at[at]) for at, (src, dst) in enumerate(zip(sources, held))]
    for copy in copies:
        copy.start()
    stations_ref, plane_ref, phase_ref, beam_ref = held
    for copy in copies:
        copy.wait()
    stations = beam_ref.shape[0]
    planes, pixels = phase_ref.shape
    one = onehot(down(row_of_blocks(stations_ref[:, 0, :])), 0, stations)
    two = onehot(down(row_of_blocks(stations_ref[:, 1, :])), 0, stations)
    plane = onehot(down(row_of_blocks(plane_ref[...])), 0, planes).astype(F32)
    width = 256
    for at in range(0, pixels, width):
        re, im = pl.ds(at, width), pl.ds(pixels + at, width)
        one_re = jnp.dot(one, beam_ref[:, re], preferred_element_type=F32)
        one_im = jnp.dot(one, beam_ref[:, im], preferred_element_type=F32)
        two_re = jnp.dot(two, beam_ref[:, re], preferred_element_type=F32)
        two_im = jnp.dot(two, beam_ref[:, im], preferred_element_type=F32)
        pair_re = one_re * two_re + one_im * two_im
        pair_im = one_im * two_re - one_re * two_im
        phase = phase_ref[:, re]
        exact = lax.Precision.HIGHEST
        wave_re = jnp.dot(plane, jnp.cos(phase), precision=exact, preferred_element_type=F32)
        wave_im = jnp.dot(plane, jnp.sin(phase), precision=exact, preferred_element_type=F32)
        screen_ref[:, re] = pair_re * wave_re - pair_im * wave_im
        screen_ref[:, im] = pair_re * wave_im + pair_im * wave_re


def blocks_from(n_y, n_h, sign):
    at_y, at_h = (lax.axis_index("y"), lax.axis_index("h"))
    return [
        lax.rem(at_y + (n_y + sign * by) % n_y, n_y) * n_h + lax.rem(at_h + flip, n_h)
        for by in range(n_y)
        for flip in range(n_h)
    ]


def rows_of_blocks(ref, blocks, cells):
    return jnp.concatenate([ref[pl.ds(pl.multiple_of(block * 16, 16), 16), cells] for block in blocks], axis=0)


def image_kernel(n_y, n_h, cores, owned, subgrid_ref, near_ref, far_ref, screen_ref, *image_refs):
    half = near_ref.shape[0] * near_ref.shape[1]
    pixels = screen_ref.shape[1] // 2
    blocks = blocks_from(n_y, n_h, 1)
    subgrids = jnp.concatenate([subgrid_ref[pl.ds(block, 1), :] for block in blocks], axis=1)
    slots = down(slot_of(subgrids, lax.axis_index("c"), cores, owned))
    near, far = (onehot(slots, 0, half), onehot(slots, half, half))
    tiles = pixels // 128
    width = 256

    def rows_of(cells):
        held = (near_ref[:, :, cells].reshape(half, width), far_ref[:, :, cells].reshape(half, width))
        return jnp.dot(near, held[0], preferred_element_type=F32) + jnp.dot(far, held[1], preferred_element_type=F32)

    for at in range(0, pixels, width):
        re, im = pl.ds(at, width), pl.ds(pixels + at, width)
        model_re, model_im = (rows_of(re), rows_of(im))
        screen_re, screen_im = (rows_of_blocks(screen_ref, blocks, re), rows_of_blocks(screen_ref, blocks, im))
        image_re = (screen_re * model_re - screen_im * model_im).astype(BF16)
        image_im = (screen_re * model_im + screen_im * model_re).astype(BF16)
        for off in range(0, width, 128):
            for image, q in ((image_re, (at + off) // 128), (image_im, (at + off) // 128 + tiles)):
                for j in range(len(blocks)):
                    image_refs[j // n_h][j % n_h, 16 * q : 16 * q + 16, :] = image[
                        16 * j : 16 * j + 16, off : off + 128
                    ]


def sum_kernel(*refs):
    pieces, sums = (refs[:-2], refs[-2:])
    for flip, sum_ref in enumerate(sums):
        total = pieces[0][flip].astype(F32)
        for piece in pieces[1:]:
            total = total + piece[flip].astype(F32)
        sum_ref[...] = total


def route_kernel(n_y, n_h, reader_ref, rows_ref, other_ref, pick_ref, *out_refs):
    at_y, at_h = (lax.axis_index("y"), lax.axis_index("h"))
    own = at_y * n_h + at_h
    source = reader_ref[0, own]
    steps = lax.rem(at_y + n_y - lax.div(source, n_h), n_y)
    here = jnp.where(lax.rem(source, n_h) == at_h, 0, 1)
    pick_ref[...] = jnp.full(pick_ref.shape, jnp.where(steps == 0, here, steps + 1), jnp.int32)
    block = jnp.int32(0)
    for at in range(n_y * n_h):
        block = jnp.where(reader_ref[0, at] == own, at, block)
    for by, out_ref in enumerate(out_refs, 1):
        to = lax.rem(at_y + by, n_y) * n_h + at_h

        @pl.when(block == to)
        def _():
            out_ref[...] = rows_ref[...]

        @pl.when(block != to)
        def _():
            out_ref[...] = other_ref[...]


def degrid_kernel(near_ref, far_ref, east_ref, north_ref, predicted_ref, cells_ref):
    rows, channels = (predicted_ref.shape[0], predicted_ref.shape[1] // 2)
    cells_ref[...] = near_ref[...] + far_ref[...]
    width = 256

    def degrid(b):
        cells = cells_ref[pl.ds(b, 16, stride=16), :]

        def spread(first, second):
            return jnp.concatenate(
                [
                    jnp.concatenate([first[:, 32 * p : 32 * p + 32], second[:, 32 * p : 32 * p + 32]], axis=1)
                    for p in range(4)
                ],
                axis=0,
            )

        image = jnp.concatenate([spread(cells[0:8], -cells[8:16]), spread(cells[8:16], cells[0:8])], axis=0)
        high = image.astype(BF16)
        low = (image - high.astype(F32)).astype(BF16)
        for at in range(0, channels, width):
            chans = pl.ds(at, width)
            north = north_ref[b, :, chans]
            inner = jnp.dot(high, north, preferred_element_type=F32) + jnp.dot(low, north, preferred_element_type=F32)
            inner_re, inner_im = (inner[:32], inner[32:])
            east = east_ref[b, :, chans].astype(F32)
            cos, sin = (east[:32], east[32:])
            vis_re = jnp.sum(cos * inner_re - sin * inner_im, axis=0, keepdims=True)
            vis_im = jnp.sum(cos * inner_im + sin * inner_re, axis=0, keepdims=True)
            row = pl.ds(b, 1)
            late = pl.ds(channels + at, width)
            predicted_ref[row, chans] = vis_re
            predicted_ref[row, late] = vis_im

    for b in range(rows):
        degrid(b)


def residual_kernel(pick_ref, *refs):
    found, (predicted_ref, resid_ref) = (refs[:-2], refs[-2:])
    for at in range(0, resid_ref.shape[1], 128):
        chans = pl.ds(at, 128)
        visible = found[0][:, chans].astype(F32)
        for which, ref in enumerate(found[1:], 1):
            visible = jnp.where(pick_ref[...] == which, ref[:, chans].astype(F32), visible)
        resid_ref[:, chans] = visible - predicted_ref[:, chans]


def grid_kernel(
    pick_ref,
    rows_ref,
    other_ref,
    came_1_ref,
    came_2_ref,
    came_3_ref,
    predicted_ref,
    east_ref,
    north_ref,
    grid_ref,
    out_ref,
    resid_ref,
):
    rows, channels = (resid_ref.shape[0], resid_ref.shape[1] // 2)
    residual_kernel(
        pick_ref, rows_ref, other_ref, came_1_ref, came_2_ref, came_3_ref, predicted_ref, resid_ref
    )
    width = 512

    def grid(b):
        products = jnp.zeros((64, 64), F32)
        for at in range(0, channels, width):
            chans, late = (pl.ds(at, width), pl.ds(channels + at, width))
            resid_re, resid_im = (resid_ref[pl.ds(b, 1), chans], resid_ref[pl.ds(b, 1), late])
            east = east_ref[b, :, chans].astype(F32)
            cos, sin = (east[:32], east[32:])
            weighted = jnp.concatenate([cos * resid_re + sin * resid_im, cos * resid_im - sin * resid_re], axis=0)
            products = products + lax.dot_general(
                weighted.astype(BF16),
                north_ref[b, :, chans],
                (((1,), (1,)), ((), ())),
                preferred_element_type=F32,
            )
        halves = (products[:32, :32] + products[32:, 32:], products[32:, :32] - products[:32, 32:])
        out_ref[pl.ds(b, 16, stride=16), :] = jnp.concatenate(
            [jnp.concatenate([half[8 * p : 8 * p + 8] for p in range(4)], axis=1) for half in halves], axis=0
        )

    for b in range(rows):
        grid(b)
    grid_ref[...] = out_ref[...].astype(BF16)


def regrid_kernel(scale, n_y, n_h, cores, owned, other, subgrid_ref, screen_ref, *refs):
    grids, sum_ref = (refs[:-1], refs[-1])
    blocks = blocks_from(n_y, n_h, -1)
    half = sum_ref.shape[0]
    pixels = screen_ref.shape[1] // 2
    tiles = pixels // 128
    count = screen_ref.shape[0]

    def grid_of(q):
        return jnp.concatenate([ref[16 * q : 16 * q + 16, :] for ref in grids], axis=0).astype(F32)

    subs = lax.broadcasted_iota(jnp.int32, (half, count), 0) + other * half
    target = jnp.concatenate([subgrid_ref[pl.ds(block, 1), :] for block in blocks], axis=1)
    target = slot_of(target, lax.axis_index("c"), cores, owned)
    sums = jnp.where(target == subs, 1.0, 0.0).astype(BF16)
    sums = jnp.concatenate([sums, sums], axis=1)
    for q in range(tiles):
        re, im = pl.ds(128 * q, 128), pl.ds(pixels + 128 * q, 128)
        grid_re, grid_im = (grid_of(q), grid_of(q + tiles))
        screen_re, screen_im = (rows_of_blocks(screen_ref, blocks, re), rows_of_blocks(screen_ref, blocks, im))
        out_re = (screen_re * grid_re + screen_im * grid_im) * scale
        out_im = (screen_re * grid_im - screen_im * grid_re) * scale
        value = jnp.concatenate([out_re, out_im], axis=1)
        high = value.astype(BF16)
        low = (value - high.astype(F32)).astype(BF16)
        both = jnp.dot(sums, jnp.concatenate([high, low], axis=0), preferred_element_type=F32)
        sum_ref[:, re] = both[:, :128].astype(sum_ref.dtype)
        sum_ref[:, im] = both[:, 128:].astype(sum_ref.dtype)


def shift(value, axis, by):
    size = lax.axis_size(axis)
    return lax.ppermute(value, axis, [(i, (i + by) % size) for i in range(size)])


def far_first(size):
    return sorted(range(1, size), key=lambda by: -min(by, size - by))


def local(
    sectioned_rows,
    reader,
    baseline_coords,
    subgrid_index,
    stations,
    plane_index,
    model_grid,
    beam_screens,
    plane_phase,
    channel_freq,
):
    n_y, n_h, n_x, n_z, n_c = (lax.axis_size(axis) for axis in FACET + TILE)
    n_facet = n_y * n_h
    channels = channel_freq.shape[0]
    pixels = plane_phase.shape[1]
    row_block = sectioned_rows.shape[1]
    count = n_facet * row_block
    owned = model_grid.shape[1]
    subgrid_count = owned * n_x * n_z * n_c
    cell_rows = 2 * pixels // 128 * row_block
    grid_scale = 1.0 / math.sqrt(channels * n_facet * (row_block * n_x * n_z * n_c) / subgrid_count)
    with jax.named_scope("model_gather"):
        copies = jnp.broadcast_to(model_grid, (n_x * n_z, owned, 2 * pixels))
        near = lax.all_to_all(copies, ("x", "z"), split_axis=0, concat_axis=0, tiled=True)

    operands = (stations, plane_index, plane_phase, beam_screens[0])
    screen = pl.pallas_call(
        screen_kernel,
        out_shape=jax.ShapeDtypeStruct((count, 2 * pixels), F32),
        in_specs=[ANY] * len(operands),
        out_specs=VMEM,
        scratch_shapes=[pltpu.VMEM(value.shape, value.dtype) for value in operands]
        + [pltpu.SemaphoreType.DMA((len(operands),))],
        compiler_params=params(44),
        cost_estimate=pl.CostEstimate(flops=10**9, bytes_accessed=4 << 20, transcendentals=1 << 16),
        name="screens",
    )(*operands)

    def table(kind, coords):
        return pl.pallas_call(
            functools.partial(table_kernel, n_h, kind),
            out_shape=jax.ShapeDtypeStruct((row_block, 64, channels), BF16),
            in_specs=[VMEM] * 2,
            out_specs=VMEM,
            scratch_shapes=[
                pltpu.VMEM((10, row_block, channels), F32),
                pltpu.VMEM((8, row_block, channels), F32),
            ],
            compiler_params=params(16),
            cost_estimate=pl.CostEstimate(flops=10**9, bytes_accessed=4 << 20, transcendentals=1 << 16),
            name=("east", "north")[kind],
        )(coords, channel_freq.reshape(1, channels))

    north = table(1, baseline_coords)
    near, screen, north = lax.optimization_barrier((near, screen, north))
    far = shift(near, "c", 1)
    images = pl.pallas_call(
        functools.partial(image_kernel, n_y, n_h, n_c, owned),
        out_shape=[jax.ShapeDtypeStruct((n_h, cell_rows, 128), BF16)] * n_y,
        in_specs=[VMEM] * 4,
        out_specs=[VMEM] * n_y,
        compiler_params=params(8),
        cost_estimate=pl.CostEstimate(flops=10**8, bytes_accessed=2 << 20, transcendentals=0),
        name="images",
    )(subgrid_index, near, far, screen)
    rows, *images = lax.optimization_barrier((sectioned_rows[0], *images))

    with jax.named_scope("visible_route"):
        other = shift(rows, "h", 1)
        pick, *sent = pl.pallas_call(
            functools.partial(route_kernel, n_y, n_h),
            out_shape=[jax.ShapeDtypeStruct((row_block, 128), jnp.int32)]
            + [jax.ShapeDtypeStruct(rows.shape, BF16)] * (n_y - 1),
            in_specs=[SMEM, VMEM, VMEM],
            out_specs=[VMEM] * n_y,
            compiler_params=params(4),
            cost_estimate=pl.CostEstimate(flops=10**6, bytes_accessed=1 << 18, transcendentals=0),
            name="route",
        )(reader, rows, other)

    with jax.named_scope("image_sum"):
        pieces = [images[0]] + [shift(images[by], "y", by) for by in far_first(n_y)]
        own_sum, other_sum = pl.pallas_call(
            sum_kernel,
            out_shape=[jax.ShapeDtypeStruct((cell_rows, 128), F32)] * 2,
            in_specs=[VMEM] * n_y,
            out_specs=[VMEM] * 2,
            compiler_params=params(4),
            cost_estimate=pl.CostEstimate(flops=10**6, bytes_accessed=1 << 20, transcendentals=0),
            name="image_sums",
        )(*pieces)
        later, own_sum = lax.optimization_barrier((baseline_coords, own_sum))
        beside_sum = shift(other_sum, "h", 1)

    east = table(0, later)
    came = dict((by, shift(sent[by - 1], "y", by)) for by in far_first(n_y))
    came = [came[by] for by in range(1, n_y)]

    predicted = pl.pallas_call(
        degrid_kernel,
        out_shape=jax.ShapeDtypeStruct((row_block, 2 * channels), F32),
        in_specs=[VMEM] * 4,
        out_specs=VMEM,
        scratch_shapes=[pltpu.VMEM((cell_rows, 128), F32)],
        compiler_params=params(16),
        cost_estimate=pl.CostEstimate(flops=10**9, bytes_accessed=5 << 20, transcendentals=0),
        name="degrid",
    )(own_sum, beside_sum, east, north)

    operands = (pick, rows, other, *came, predicted)
    gridded = pl.pallas_call(
        grid_kernel,
        out_shape=jax.ShapeDtypeStruct((cell_rows, 128), BF16),
        in_specs=[VMEM] * 9,
        out_specs=VMEM,
        scratch_shapes=[pltpu.VMEM((cell_rows, 128), F32), pltpu.VMEM(predicted.shape, F32)],
        compiler_params=params(16),
        cost_estimate=pl.CostEstimate(flops=10**9, bytes_accessed=5 << 20, transcendentals=0),
        name="grid",
    )(*operands, east, north)

    with jax.named_scope("grid_gather"):
        beside = shift(gridded, "h", 1)
        moved = dict((by, (shift(gridded, "y", by), shift(beside, "y", by))) for by in reversed(far_first(n_y)))
        grids = [gridded, beside]
        for by in range(1, n_y):
            grids += moved[by]

    first, *operands = operands
    first, grids[1] = lax.optimization_barrier((first, grids[1]))
    residual = pl.pallas_call(
        residual_kernel,
        out_shape=jax.ShapeDtypeStruct(predicted.shape, F32),
        in_specs=[VMEM] * 7,
        out_specs=VMEM,
        compiler_params=params(4),
        cost_estimate=pl.CostEstimate(flops=10**6, bytes_accessed=1 << 19, transcendentals=0),
        name="residual",
    )(first, *operands)

    half = subgrid_count // n_c

    def regrid(other, subgrids):
        return pl.pallas_call(
            functools.partial(regrid_kernel, grid_scale, n_y, n_h, n_c, owned, other),
            out_shape=jax.ShapeDtypeStruct((half, 2 * pixels), (F32, BF16)[other]),
            in_specs=[VMEM] * (2 + n_facet),
            out_specs=VMEM,
            compiler_params=params(8),
            cost_estimate=pl.CostEstimate(flops=10**8, bytes_accessed=3 << 20, transcendentals=0),
            name=("regrid_near", "regrid_far")[other],
        )(subgrids, screen, *grids)

    subgrids, residual = lax.optimization_barrier((subgrid_index, residual))
    far_sum = regrid(1, subgrids)
    subgrids, far_sum = lax.optimization_barrier((subgrid_index, far_sum))
    near_sum = regrid(0, subgrids)

    with jax.named_scope("dirty_scatter"):
        chip_sum = (near_sum + shift(far_sum, "c", 1).astype(F32)).astype(BF16).reshape(n_x * n_z, owned, 2 * pixels)
        chips = lax.all_to_all(chip_sum, ("x", "z"), split_axis=0, concat_axis=0, tiled=True)
        dirty = jnp.sum(chips.astype(F32), axis=0)
    return (residual[None], dirty[None])


def solution(mesh):
    split = Mesh(mesh.devices.reshape(4, 2, 4, 4, 2), FACET + TILE)
    return jax.shard_map(
        local,
        mesh=split,
        in_specs=(
            P(FACET, TILE, None),
            P(TILE, None),
            P(None, None, TILE),
            P(None, TILE),
            P(None, None, TILE),
            P(None, TILE),
            P(FACET, TILE, None),
            P(FACET, None, None),
            P(),
            P(),
        ),
        out_specs=(P(FACET, TILE, None), P(FACET, TILE, None)),
        check_vma=False,
    )
```

```python
import functools
import math

import jax
import jax.numpy as jnp
from jax import lax
from jax.experimental import pallas as pl
from jax.experimental.pallas import tpu as pltpu
from jax.sharding import Mesh
from jax.sharding import PartitionSpec as P

TWO_PI = 2.0 * math.pi
F32 = jnp.float32
BF16 = jnp.bfloat16
FACET = ("y", "h")
TILE = ("x", "z", "c")
VMEM = pl.BlockSpec(memory_space=pltpu.VMEM)
SMEM = pl.BlockSpec(memory_space=pltpu.SMEM)
ANY = pl.BlockSpec(memory_space=pl.ANY)


def params(mib):
    return pltpu.CompilerParams(vmem_limit_bytes=mib << 20)


def cmul(a, b):
    return (a[0] * b[0] - a[1] * b[1], a[0] * b[1] + a[1] * b[0])


def conj(a):
    return (a[0], -a[1])


def repeat_kernel(rows_ref, copies_ref):
    for at in range(copies_ref.shape[0]):
        copies_ref[at] = rows_ref[0]


def row_of_blocks(values):
    return jnp.concatenate([values[at : at + 1, :] for at in range(values.shape[0])], axis=1)


def down(row):
    return jnp.broadcast_to(row, (128, 128)).T


def onehot(column, first, count):
    lanes = lax.broadcasted_iota(jnp.int32, (128, 128), 1)
    width = min(count, 128)
    parts = [
        jnp.where(column == lanes + (first + at), 1.0, 0.0).astype(BF16)[:, :width] for at in range(0, count, 128)
    ]
    return parts[0] if len(parts) == 1 else jnp.concatenate(parts, axis=1)


def slot_of(subgrid, core, cores, owned):
    held = lax.rem(lax.div(subgrid, owned) + (cores - core), cores)
    return (held * (128 // cores)) + lax.div(subgrid, owned * cores) * owned + lax.rem(subgrid, owned)


def table_kernel(n_h, kind, coords_ref, freq_ref, table_ref, powers, groups):
    rows = coords_ref.shape[2]
    coords = coords_ref[lax.axis_index("y") * n_h + lax.axis_index("h")]
    row = jnp.concatenate([coords[kind : kind + 1], jnp.zeros((1, 128 - rows), F32)], axis=1)
    column = (TWO_PI * down(row)[:rows]) * (1.0 / 32.0)
    angle = jnp.concatenate([column] * (freq_ref.shape[1] // 128), axis=1) * freq_ref[...]
    z1 = (jnp.cos(angle), jnp.sin(angle))
    z2 = cmul(z1, z1)
    z4 = cmul(z2, z2)
    z8 = cmul(z4, z4)
    z16 = cmul(z8, z8)
    low16 = conj(z16)
    for at, value in enumerate((z1, z2, z4, z8, z16)):
        powers[2 * at] = value[0]
        powers[2 * at + 1] = value[1]
    for at, value in enumerate((low16, cmul(low16, z1), cmul(low16, z2), cmul(low16, cmul(z1, z2)))):
        groups[2 * at] = value[0]
        groups[2 * at + 1] = value[1]
    sub = lax.broadcasted_iota(jnp.int32, (8, angle.shape[1]), 0)

    def row_of(ref, at, row):
        return (ref[2 * at, pl.ds(row, 1), :], ref[2 * at + 1, pl.ds(row, 1), :])

    def picked(factor, bit):
        on = (sub & bit) != 0
        return (jnp.where(on, factor[0], 1.0), jnp.where(on, factor[1], 0.0))

    def bits(factors):
        return cmul(cmul(picked(factors[0], 1), picked(factors[1], 2)), picked(factors[2], 4))

    def stacked(parts):
        return jnp.concatenate([part[0] for part in parts] + [part[1] for part in parts], axis=0).astype(BF16)

    def body(b):
        base = bits([row_of(powers, at, b) for at in ((2, 3, 4), (0, 1, 2))[kind]])
        if kind == 0:
            table_ref[b] = stacked([cmul(base, row_of(groups, at, b)) for at in range(4)])
        else:
            up8 = row_of(powers, 3, b)
            table_ref[b] = stacked([cmul(base, row_of(groups, 0, b)), cmul(base, conj(up8)), base, cmul(base, up8)])

    for b in range(rows):
        body(b)


def target_of(subgrid, sizes, owned):
    n_x, n_z, n_c = sizes
    row, rest = (lax.rem(subgrid, owned), lax.div(subgrid, owned))
    core, rest = (lax.rem(rest, n_c), lax.div(rest, n_c))
    x = lax.rem(lax.div(rest, n_z) + n_x - lax.axis_index("x"), n_x)
    z = lax.rem(lax.rem(rest, n_z) + n_z - lax.axis_index("z"), n_z)
    core = lax.rem(core + n_c - lax.axis_index("c"), n_c)
    return ((core * n_x + x) * n_z + z) * owned + row


def chip_kernel(near_ref, far_ref, own_ref, *send_refs):
    rows = own_ref.shape[0]
    own_ref[...] = near_ref[:rows] + far_ref[:rows].astype(F32)
    for at, ref in enumerate(send_refs, 1):
        part = pl.ds(at * rows, rows)
        ref[...] = (near_ref[part] + far_ref[part].astype(F32)).astype(BF16)


def column_kernel(own_ref, *refs):
    came, outs = (refs[:3], refs[3:])
    total = own_ref[...]
    for ref in came:
        total = total + ref[...].astype(F32)
    rows = outs[0].shape[0]
    for at, ref in enumerate(outs):
        ref[...] = total[at * rows : at * rows + rows]


def total_kernel(*refs):
    total = refs[0][...]
    for ref in refs[1:-1]:
        total = total + ref[...]
    refs[-1][...] = total


def screen_kernel(stations_from, plane_from, phase_from, beam_from, screen_ref, *refs):
    sources, held, sems = ((stations_from, plane_from, phase_from, beam_from), refs[:4], refs[4])
    copies = [pltpu.make_async_copy(src, dst, sems.at[at]) for at, (src, dst) in enumerate(zip(sources, held))]
    for copy in copies:
        copy.start()
    stations_ref, plane_ref, phase_ref, beam_ref = held
    for copy in copies:
        copy.wait()
    stations = beam_ref.shape[0]
    planes, pixels = phase_ref.shape
    one = onehot(down(row_of_blocks(stations_ref[:, 0, :])), 0, stations)
    two = onehot(down(row_of_blocks(stations_ref[:, 1, :])), 0, stations)
    plane = onehot(down(row_of_blocks(plane_ref[...])), 0, planes).astype(F32)
    width = 256
    for at in range(0, pixels, width):
        re, im = pl.ds(at, width), pl.ds(pixels + at, width)
        one_re = jnp.dot(one, beam_ref[:, re], preferred_element_type=F32)
        one_im = jnp.dot(one, beam_ref[:, im], preferred_element_type=F32)
        two_re = jnp.dot(two, beam_ref[:, re], preferred_element_type=F32)
        two_im = jnp.dot(two, beam_ref[:, im], preferred_element_type=F32)
        pair_re = one_re * two_re + one_im * two_im
        pair_im = one_im * two_re - one_re * two_im
        phase = phase_ref[:, re]
        exact = lax.Precision.HIGHEST
        wave_re = jnp.dot(plane, jnp.cos(phase), precision=exact, preferred_element_type=F32)
        wave_im = jnp.dot(plane, jnp.sin(phase), precision=exact, preferred_element_type=F32)
        screen_ref[:, re] = pair_re * wave_re - pair_im * wave_im
        screen_ref[:, im] = pair_re * wave_im + pair_im * wave_re


def blocks_from(n_y, n_h, sign):
    at_y, at_h = (lax.axis_index("y"), lax.axis_index("h"))
    return [
        lax.rem(at_y + (n_y + sign * by) % n_y, n_y) * n_h + lax.rem(at_h + flip, n_h)
        for by in range(n_y)
        for flip in range(n_h)
    ]


def rows_of_blocks(ref, blocks, cells):
    return jnp.concatenate([ref[pl.ds(pl.multiple_of(block * 16, 16), 16), cells] for block in blocks], axis=0)


def image_kernel(n_y, n_h, cores, owned, subgrid_ref, near_ref, far_ref, screen_ref, *image_refs):
    half = near_ref.shape[0] * near_ref.shape[1]
    pixels = screen_ref.shape[1] // 2
    blocks = blocks_from(n_y, n_h, 1)
    subgrids = jnp.concatenate([subgrid_ref[pl.ds(block, 1), :] for block in blocks], axis=1)
    slots = down(slot_of(subgrids, lax.axis_index("c"), cores, owned))
    near, far = (onehot(slots, 0, half), onehot(slots, half, half))
    tiles = pixels // 128
    width = 256

    def rows_of(cells):
        held = (near_ref[:, :, cells].reshape(half, width), far_ref[:, :, cells].reshape(half, width))
        return jnp.dot(near, held[0], preferred_element_type=F32) + jnp.dot(far, held[1], preferred_element_type=F32)

    for at in range(0, pixels, width):
        re, im = pl.ds(at, width), pl.ds(pixels + at, width)
        model_re, model_im = (rows_of(re), rows_of(im))
        screen_re, screen_im = (rows_of_blocks(screen_ref, blocks, re), rows_of_blocks(screen_ref, blocks, im))
        image_re = (screen_re * model_re - screen_im * model_im).astype(BF16)
        image_im = (screen_re * model_im + screen_im * model_re).astype(BF16)
        for off in range(0, width, 128):
            for image, q in ((image_re, (at + off) // 128), (image_im, (at + off) // 128 + tiles)):
                for j in range(len(blocks)):
                    image_refs[j // n_h][j % n_h, 16 * q : 16 * q + 16, :] = image[
                        16 * j : 16 * j + 16, off : off + 128
                    ]


def sum_kernel(*refs):
    pieces, sums = (refs[:-2], refs[-2:])
    for flip, sum_ref in enumerate(sums):
        total = pieces[0][flip].astype(F32)
        for piece in pieces[1:]:
            total = total + piece[flip].astype(F32)
        sum_ref[...] = total


def route_kernel(n_y, n_h, reader_ref, rows_ref, other_ref, pick_ref, *out_refs):
    at_y, at_h = (lax.axis_index("y"), lax.axis_index("h"))
    own = at_y * n_h + at_h
    source = reader_ref[0, own]
    steps = lax.rem(at_y + n_y - lax.div(source, n_h), n_y)
    here = jnp.where(lax.rem(source, n_h) == at_h, 0, 1)
    pick_ref[...] = jnp.full(pick_ref.shape, jnp.where(steps == 0, here, steps + 1), jnp.int32)
    block = jnp.int32(0)
    for at in range(n_y * n_h):
        block = jnp.where(reader_ref[0, at] == own, at, block)
    for by, out_ref in enumerate(out_refs, 1):
        to = lax.rem(at_y + by, n_y) * n_h + at_h

        @pl.when(block == to)
        def _():
            out_ref[...] = rows_ref[...]

        @pl.when(block != to)
        def _():
            out_ref[...] = other_ref[...]


def degrid_kernel(near_ref, far_ref, east_ref, north_ref, predicted_ref, cells_ref):
    rows, channels = (predicted_ref.shape[0], predicted_ref.shape[1] // 2)
    cells_ref[...] = near_ref[...] + far_ref[...]
    width = 256

    def degrid(b):
        cells = cells_ref[pl.ds(b, 16, stride=16), :]

        def spread(first, second):
            return jnp.concatenate(
                [
                    jnp.concatenate([first[:, 32 * p : 32 * p + 32], second[:, 32 * p : 32 * p + 32]], axis=1)
                    for p in range(4)
                ],
                axis=0,
            )

        image = jnp.concatenate([spread(cells[0:8], -cells[8:16]), spread(cells[8:16], cells[0:8])], axis=0)
        high = image.astype(BF16)
        low = (image - high.astype(F32)).astype(BF16)
        for at in range(0, channels, width):
            chans = pl.ds(at, width)
            north = north_ref[b, :, chans]
            inner = jnp.dot(high, north, preferred_element_type=F32) + jnp.dot(low, north, preferred_element_type=F32)
            inner_re, inner_im = (inner[:32], inner[32:])
            east = east_ref[b, :, chans].astype(F32)
            cos, sin = (east[:32], east[32:])
            vis_re = jnp.sum(cos * inner_re - sin * inner_im, axis=0, keepdims=True)
            vis_im = jnp.sum(cos * inner_im + sin * inner_re, axis=0, keepdims=True)
            row = pl.ds(b, 1)
            late = pl.ds(channels + at, width)
            predicted_ref[row, chans] = vis_re
            predicted_ref[row, late] = vis_im

    for b in range(rows):
        degrid(b)


def residual_kernel(pick_ref, *refs):
    found, (predicted_ref, resid_ref) = (refs[:-2], refs[-2:])
    for at in range(0, resid_ref.shape[1], 128):
        chans = pl.ds(at, 128)
        visible = found[0][:, chans].astype(F32)
        for which, ref in enumerate(found[1:], 1):
            visible = jnp.where(pick_ref[...] == which, ref[:, chans].astype(F32), visible)
        resid_ref[:, chans] = visible - predicted_ref[:, chans]


def grid_kernel(
    pick_ref,
    rows_ref,
    other_ref,
    came_1_ref,
    came_2_ref,
    came_3_ref,
    predicted_ref,
    east_ref,
    north_ref,
    grid_ref,
    out_ref,
    resid_ref,
):
    rows, channels = (resid_ref.shape[0], resid_ref.shape[1] // 2)
    residual_kernel(
        pick_ref, rows_ref, other_ref, came_1_ref, came_2_ref, came_3_ref, predicted_ref, resid_ref
    )
    width = 512

    def grid(b):
        products = jnp.zeros((64, 64), F32)
        for at in range(0, channels, width):
            chans, late = (pl.ds(at, width), pl.ds(channels + at, width))
            resid_re, resid_im = (resid_ref[pl.ds(b, 1), chans], resid_ref[pl.ds(b, 1), late])
            east = east_ref[b, :, chans].astype(F32)
            cos, sin = (east[:32], east[32:])
            weighted = jnp.concatenate([cos * resid_re + sin * resid_im, cos * resid_im - sin * resid_re], axis=0)
            products = products + lax.dot_general(
                weighted.astype(BF16),
                north_ref[b, :, chans],
                (((1,), (1,)), ((), ())),
                preferred_element_type=F32,
            )
        halves = (products[:32, :32] + products[32:, 32:], products[32:, :32] - products[:32, 32:])
        out_ref[pl.ds(b, 16, stride=16), :] = jnp.concatenate(
            [jnp.concatenate([half[8 * p : 8 * p + 8] for p in range(4)], axis=1) for half in halves], axis=0
        )

    for b in range(rows):
        grid(b)
    grid_ref[...] = out_ref[...].astype(BF16)


def regrid_kernel(scale, n_y, n_h, sizes, owned, other, subgrid_ref, screen_ref, *refs):
    grids, sum_ref = (refs[:-1], refs[-1])
    blocks = blocks_from(n_y, n_h, -1)
    half = sum_ref.shape[0]
    pixels = screen_ref.shape[1] // 2
    tiles = pixels // 128
    count = screen_ref.shape[0]

    def grid_of(q):
        return jnp.concatenate([ref[16 * q : 16 * q + 16, :] for ref in grids], axis=0).astype(F32)

    subs = lax.broadcasted_iota(jnp.int32, (half, count), 0) + other * half
    target = jnp.concatenate([subgrid_ref[pl.ds(block, 1), :] for block in blocks], axis=1)
    target = target_of(target, sizes, owned)
    sums = jnp.where(target == subs, 1.0, 0.0).astype(BF16)
    sums = jnp.concatenate([sums, sums], axis=1)
    for q in range(tiles):
        re, im = pl.ds(128 * q, 128), pl.ds(pixels + 128 * q, 128)
        grid_re, grid_im = (grid_of(q), grid_of(q + tiles))
        screen_re, screen_im = (rows_of_blocks(screen_ref, blocks, re), rows_of_blocks(screen_ref, blocks, im))
        out_re = (screen_re * grid_re + screen_im * grid_im) * scale
        out_im = (screen_re * grid_im - screen_im * grid_re) * scale
        value = jnp.concatenate([out_re, out_im], axis=1)
        high = value.astype(BF16)
        low = (value - high.astype(F32)).astype(BF16)
        both = jnp.dot(sums, jnp.concatenate([high, low], axis=0), preferred_element_type=F32)
        sum_ref[:, re] = both[:, :128].astype(sum_ref.dtype)
        sum_ref[:, im] = both[:, 128:].astype(sum_ref.dtype)


def shift(value, axis, by):
    size = lax.axis_size(axis)
    return lax.ppermute(value, axis, [(i, (i + by) % size) for i in range(size)])


def far_first(size):
    return sorted(range(1, size), key=lambda by: -min(by, size - by))


def local(
    sectioned_rows,
    reader,
    baseline_coords,
    subgrid_index,
    stations,
    plane_index,
    model_grid,
    beam_screens,
    plane_phase,
    channel_freq,
):
    n_y, n_h, n_x, n_z, n_c = (lax.axis_size(axis) for axis in FACET + TILE)
    n_facet = n_y * n_h
    channels = channel_freq.shape[0]
    pixels = plane_phase.shape[1]
    row_block = sectioned_rows.shape[1]
    count = n_facet * row_block
    owned = model_grid.shape[1]
    subgrid_count = owned * n_x * n_z * n_c
    cell_rows = 2 * pixels // 128 * row_block
    grid_scale = 1.0 / math.sqrt(channels * n_facet * (row_block * n_x * n_z * n_c) / subgrid_count)
    with jax.named_scope("model_gather"):
        copies = pl.pallas_call(
            repeat_kernel,
            out_shape=jax.ShapeDtypeStruct((n_x * n_z, owned, 2 * pixels), BF16),
            in_specs=[VMEM],
            out_specs=VMEM,
            compiler_params=params(61),
            cost_estimate=pl.CostEstimate(flops=0, bytes_accessed=1 << 18, transcendentals=0),
            name="repeat",
        )(model_grid)
        near = lax.all_to_all(copies, ("x", "z"), split_axis=0, concat_axis=0, tiled=True)

    operands = (stations, plane_index, plane_phase, beam_screens[0])
    screen = pl.pallas_call(
        screen_kernel,
        out_shape=jax.ShapeDtypeStruct((count, 2 * pixels), F32),
        in_specs=[ANY] * len(operands),
        out_specs=VMEM,
        scratch_shapes=[pltpu.VMEM(value.shape, value.dtype) for value in operands]
        + [pltpu.SemaphoreType.DMA((len(operands),))],
        compiler_params=params(44),
        cost_estimate=pl.CostEstimate(flops=10**9, bytes_accessed=4 << 20, transcendentals=1 << 16),
        name="screens",
    )(*operands)

    def table(kind, coords):
        return pl.pallas_call(
            functools.partial(table_kernel, n_h, kind),
            out_shape=jax.ShapeDtypeStruct((row_block, 64, channels), BF16),
            in_specs=[VMEM] * 2,
            out_specs=VMEM,
            scratch_shapes=[
                pltpu.VMEM((10, row_block, channels), F32),
                pltpu.VMEM((8, row_block, channels), F32),
            ],
            compiler_params=params(16),
            cost_estimate=pl.CostEstimate(flops=10**9, bytes_accessed=4 << 20, transcendentals=1 << 16),
            name=("east", "north")[kind],
        )(coords, channel_freq.reshape(1, channels))

    north = table(1, baseline_coords)
    near, screen, north = lax.optimization_barrier((near, screen, north))
    far = shift(near, "c", 1)
    images = pl.pallas_call(
        functools.partial(image_kernel, n_y, n_h, n_c, owned),
        out_shape=[jax.ShapeDtypeStruct((n_h, cell_rows, 128), BF16)] * n_y,
        in_specs=[VMEM] * 4,
        out_specs=[VMEM] * n_y,
        compiler_params=params(8),
        cost_estimate=pl.CostEstimate(flops=10**8, bytes_accessed=2 << 20, transcendentals=0),
        name="images",
    )(subgrid_index, near, far, screen)
    rows, *images = lax.optimization_barrier((sectioned_rows[0], *images))

    with jax.named_scope("visible_route"):
        other = shift(rows, "h", 1)
        pick, *sent = pl.pallas_call(
            functools.partial(route_kernel, n_y, n_h),
            out_shape=[jax.ShapeDtypeStruct((row_block, 128), jnp.int32)]
            + [jax.ShapeDtypeStruct(rows.shape, BF16)] * (n_y - 1),
            in_specs=[SMEM, VMEM, VMEM],
            out_specs=[VMEM] * n_y,
            compiler_params=params(4),
            cost_estimate=pl.CostEstimate(flops=10**6, bytes_accessed=1 << 18, transcendentals=0),
            name="route",
        )(reader, rows, other)

    with jax.named_scope("image_sum"):
        pieces = [images[0]] + [shift(images[by], "y", by) for by in far_first(n_y)]
        own_sum, other_sum = pl.pallas_call(
            sum_kernel,
            out_shape=[jax.ShapeDtypeStruct((cell_rows, 128), F32)] * 2,
            in_specs=[VMEM] * n_y,
            out_specs=[VMEM] * 2,
            compiler_params=params(4),
            cost_estimate=pl.CostEstimate(flops=10**6, bytes_accessed=1 << 20, transcendentals=0),
            name="image_sums",
        )(*pieces)
        later, own_sum = lax.optimization_barrier((baseline_coords, own_sum))
        beside_sum = shift(other_sum, "h", 1)

    east = table(0, later)
    came = dict((by, shift(sent[by - 1], "y", by)) for by in far_first(n_y))
    came = [came[by] for by in range(1, n_y)]

    predicted = pl.pallas_call(
        degrid_kernel,
        out_shape=jax.ShapeDtypeStruct((row_block, 2 * channels), F32),
        in_specs=[VMEM] * 4,
        out_specs=VMEM,
        scratch_shapes=[pltpu.VMEM((cell_rows, 128), F32)],
        compiler_params=params(16),
        cost_estimate=pl.CostEstimate(flops=10**9, bytes_accessed=5 << 20, transcendentals=0),
        name="degrid",
    )(own_sum, beside_sum, east, north)

    operands = (pick, rows, other, *came, predicted)
    gridded = pl.pallas_call(
        grid_kernel,
        out_shape=jax.ShapeDtypeStruct((cell_rows, 128), BF16),
        in_specs=[VMEM] * 9,
        out_specs=VMEM,
        scratch_shapes=[pltpu.VMEM((cell_rows, 128), F32), pltpu.VMEM(predicted.shape, F32)],
        compiler_params=params(16),
        cost_estimate=pl.CostEstimate(flops=10**9, bytes_accessed=5 << 20, transcendentals=0),
        name="grid",
    )(*operands, east, north)

    with jax.named_scope("grid_gather"):
        beside = shift(gridded, "h", 1)
        moved = dict((by, (shift(gridded, "y", by), shift(beside, "y", by))) for by in reversed(far_first(n_y)))
        grids = [gridded, beside]
        for by in range(1, n_y):
            grids += moved[by]

    first, *operands = operands
    first, grids[1] = lax.optimization_barrier((first, grids[1]))
    residual = pl.pallas_call(
        residual_kernel,
        out_shape=jax.ShapeDtypeStruct(predicted.shape, F32),
        in_specs=[VMEM] * 7,
        out_specs=VMEM,
        compiler_params=params(4),
        cost_estimate=pl.CostEstimate(flops=10**6, bytes_accessed=1 << 19, transcendentals=0),
        name="residual",
    )(first, *operands)

    half = subgrid_count // n_c

    def regrid(other, subgrids):
        return pl.pallas_call(
            functools.partial(regrid_kernel, grid_scale, n_y, n_h, (n_x, n_z, n_c), owned, other),
            out_shape=jax.ShapeDtypeStruct((half, 2 * pixels), (F32, BF16)[other]),
            in_specs=[VMEM] * (2 + n_facet),
            out_specs=VMEM,
            compiler_params=params(8),
            cost_estimate=pl.CostEstimate(flops=10**8, bytes_accessed=3 << 20, transcendentals=0),
            name=("regrid_near", "regrid_far")[other],
        )(subgrids, screen, *grids)

    subgrids, residual = lax.optimization_barrier((subgrid_index, residual))
    far_sum = regrid(1, subgrids)
    subgrids, far_sum = lax.optimization_barrier((subgrid_index, far_sum))
    near_sum = regrid(0, subgrids)

    with jax.named_scope("dirty_scatter"):
        far_sum = shift(far_sum, "c", 1)

        def call(kernel, name, shapes, *operands):
            return pl.pallas_call(
                kernel,
                out_shape=shapes,
                in_specs=[VMEM] * len(operands),
                out_specs=[VMEM] * len(shapes),
                compiler_params=params(4),
                cost_estimate=pl.CostEstimate(flops=10**6, bytes_accessed=1 << 20, transcendentals=0),
                name=name,
            )(*operands)

        column = (n_z * owned, 2 * pixels)
        own, *sent = call(
            chip_kernel,
            "chip_sums",
            [jax.ShapeDtypeStruct(column, F32)] + [jax.ShapeDtypeStruct(column, BF16)] * (n_x - 1),
            near_sum,
            far_sum,
        )
        sent = [shift(sent[by - 1], "x", by) for by in far_first(n_x)]
        own, *sent = call(
            column_kernel, "column_sums", [jax.ShapeDtypeStruct((owned, 2 * pixels), F32)] * n_z, own, *sent
        )
        sent = [shift(value, "z", by) for by, value in enumerate(sent, 1)]
        (dirty,) = call(total_kernel, "total", [jax.ShapeDtypeStruct(own.shape, F32)], own, *sent)
    return (residual[None], dirty[None])


def solution(mesh):
    split = Mesh(mesh.devices.reshape(4, 2, 4, 4, 2), FACET + TILE)
    return jax.shard_map(
        local,
        mesh=split,
        in_specs=(
            P(FACET, TILE, None),
            P(TILE, None),
            P(None, None, TILE),
            P(None, TILE),
            P(None, None, TILE),
            P(None, TILE),
            P(FACET, TILE, None),
            P(FACET, None, None),
            P(),
            P(),
        ),
        out_specs=(P(FACET, TILE, None), P(FACET, TILE, None)),
        check_vma=False,
    )
```

```python
import functools
import math

import jax
import jax.numpy as jnp
from jax import lax
from jax.experimental import pallas as pl
from jax.experimental.pallas import tpu as pltpu
from jax.sharding import Mesh
from jax.sharding import PartitionSpec as P

TWO_PI = 2.0 * math.pi
F32 = jnp.float32
BF16 = jnp.bfloat16
FACET = ("y", "h")
TILE = ("x", "z", "c")
VMEM = pl.BlockSpec(memory_space=pltpu.VMEM)
SMEM = pl.BlockSpec(memory_space=pltpu.SMEM)
ANY = pl.BlockSpec(memory_space=pl.ANY)


def params(mib):
    return pltpu.CompilerParams(vmem_limit_bytes=mib << 20)


def cmul(a, b):
    return (a[0] * b[0] - a[1] * b[1], a[0] * b[1] + a[1] * b[0])


def conj(a):
    return (a[0], -a[1])


def repeat_kernel(rows_ref, copies_ref):
    for at in range(copies_ref.shape[0]):
        copies_ref[at] = rows_ref[0]


def row_of_blocks(values):
    return jnp.concatenate([values[at : at + 1, :] for at in range(values.shape[0])], axis=1)


def down(row):
    return jnp.broadcast_to(row, (128, 128)).T


def onehot(column, first, count):
    lanes = lax.broadcasted_iota(jnp.int32, (128, 128), 1)
    width = min(count, 128)
    parts = [
        jnp.where(column == lanes + (first + at), 1.0, 0.0).astype(BF16)[:, :width] for at in range(0, count, 128)
    ]
    return parts[0] if len(parts) == 1 else jnp.concatenate(parts, axis=1)


def slot_of(subgrid, core, cores, owned):
    held = lax.rem(lax.div(subgrid, owned) + (cores - core), cores)
    return (held * (128 // cores)) + lax.div(subgrid, owned * cores) * owned + lax.rem(subgrid, owned)


def table_kernel(n_h, kind, coords_ref, freq_ref, table_ref, powers, groups):
    rows = coords_ref.shape[2]
    coords = coords_ref[lax.axis_index("y") * n_h + lax.axis_index("h")]
    row = jnp.concatenate([coords[kind : kind + 1], jnp.zeros((1, 128 - rows), F32)], axis=1)
    column = (TWO_PI * down(row)[:rows]) * (1.0 / 32.0)
    angle = jnp.concatenate([column] * (freq_ref.shape[1] // 128), axis=1) * freq_ref[...]
    z1 = (jnp.cos(angle), jnp.sin(angle))
    z2 = cmul(z1, z1)
    z4 = cmul(z2, z2)
    z8 = cmul(z4, z4)
    z16 = cmul(z8, z8)
    low16 = conj(z16)
    for at, value in enumerate((z1, z2, z4, z8, z16)):
        powers[2 * at] = value[0]
        powers[2 * at + 1] = value[1]
    for at, value in enumerate((low16, cmul(low16, z1), cmul(low16, z2), cmul(low16, cmul(z1, z2)))):
        groups[2 * at] = value[0]
        groups[2 * at + 1] = value[1]
    sub = lax.broadcasted_iota(jnp.int32, (8, angle.shape[1]), 0)

    def row_of(ref, at, row):
        return (ref[2 * at, pl.ds(row, 1), :], ref[2 * at + 1, pl.ds(row, 1), :])

    def picked(factor, bit):
        on = (sub & bit) != 0
        return (jnp.where(on, factor[0], 1.0), jnp.where(on, factor[1], 0.0))

    def bits(factors):
        return cmul(cmul(picked(factors[0], 1), picked(factors[1], 2)), picked(factors[2], 4))

    def stacked(parts):
        return jnp.concatenate([part[0] for part in parts] + [part[1] for part in parts], axis=0).astype(BF16)

    def body(b):
        base = bits([row_of(powers, at, b) for at in ((2, 3, 4), (0, 1, 2))[kind]])
        if kind == 0:
            table_ref[b] = stacked([cmul(base, row_of(groups, at, b)) for at in range(4)])
        else:
            up8 = row_of(powers, 3, b)
            table_ref[b] = stacked([cmul(base, row_of(groups, 0, b)), cmul(base, conj(up8)), base, cmul(base, up8)])

    for b in range(rows):
        body(b)


def target_of(subgrid, sizes, owned):
    n_x, n_z, n_c = sizes
    row, rest = (lax.rem(subgrid, owned), lax.div(subgrid, owned))
    core, rest = (lax.rem(rest, n_c), lax.div(rest, n_c))
    x = lax.rem(lax.div(rest, n_z) + n_x - lax.axis_index("x"), n_x)
    z = lax.bitwise_xor(lax.rem(rest, n_z), jnp.full_like(rest, lax.axis_index("z")))
    core = lax.rem(core + n_c - lax.axis_index("c"), n_c)
    return ((core * n_x + x) * n_z + z) * owned + row


def chip_kernel(near_ref, far_ref, own_ref, *send_refs):
    rows = own_ref.shape[0]
    own_ref[...] = near_ref[:rows] + far_ref[:rows].astype(F32)
    for at, ref in enumerate(send_refs, 1):
        part = pl.ds(at * rows, rows)
        ref[...] = (near_ref[part] + far_ref[part].astype(F32)).astype(BF16)


def column_kernel(own_ref, *refs):
    came, outs = (refs[:3], refs[3:])
    total = own_ref[...]
    for ref in came:
        total = total + ref[...].astype(F32)
    rows = outs[0].shape[0]
    for at, ref in enumerate(outs):
        ref[...] = total[at * rows : at * rows + rows]


def total_kernel(*refs):
    total = refs[0][...]
    for ref in refs[1:-1]:
        total = total + ref[...]
    refs[-1][...] = total


def screen_kernel(stations_from, plane_from, phase_from, beam_from, screen_ref, *refs):
    sources, held, sems = ((stations_from, plane_from, phase_from, beam_from), refs[:4], refs[4])
    copies = [pltpu.make_async_copy(src, dst, sems.at[at]) for at, (src, dst) in enumerate(zip(sources, held))]
    for copy in copies:
        copy.start()
    stations_ref, plane_ref, phase_ref, beam_ref = held
    for copy in copies:
        copy.wait()
    stations = beam_ref.shape[0]
    planes, pixels = phase_ref.shape
    one = onehot(down(row_of_blocks(stations_ref[:, 0, :])), 0, stations)
    two = onehot(down(row_of_blocks(stations_ref[:, 1, :])), 0, stations)
    plane = onehot(down(row_of_blocks(plane_ref[...])), 0, planes).astype(F32)
    width = 256
    for at in range(0, pixels, width):
        re, im = pl.ds(at, width), pl.ds(pixels + at, width)
        one_re = jnp.dot(one, beam_ref[:, re], preferred_element_type=F32)
        one_im = jnp.dot(one, beam_ref[:, im], preferred_element_type=F32)
        two_re = jnp.dot(two, beam_ref[:, re], preferred_element_type=F32)
        two_im = jnp.dot(two, beam_ref[:, im], preferred_element_type=F32)
        pair_re = one_re * two_re + one_im * two_im
        pair_im = one_im * two_re - one_re * two_im
        phase = phase_ref[:, re]
        exact = lax.Precision.HIGHEST
        wave_re = jnp.dot(plane, jnp.cos(phase), precision=exact, preferred_element_type=F32)
        wave_im = jnp.dot(plane, jnp.sin(phase), precision=exact, preferred_element_type=F32)
        screen_ref[:, re] = pair_re * wave_re - pair_im * wave_im
        screen_ref[:, im] = pair_re * wave_im + pair_im * wave_re


def blocks_from(n_y, n_h, sign):
    at_y, at_h = (lax.axis_index("y"), lax.axis_index("h"))
    return [
        lax.rem(at_y + (n_y + sign * by) % n_y, n_y) * n_h + lax.rem(at_h + flip, n_h)
        for by in range(n_y)
        for flip in range(n_h)
    ]


def rows_of_blocks(ref, blocks, cells):
    return jnp.concatenate([ref[pl.ds(pl.multiple_of(block * 16, 16), 16), cells] for block in blocks], axis=0)


def image_kernel(n_y, n_h, cores, owned, subgrid_ref, near_ref, far_ref, screen_ref, *image_refs):
    half = near_ref.shape[0] * near_ref.shape[1]
    pixels = screen_ref.shape[1] // 2
    blocks = blocks_from(n_y, n_h, 1)
    subgrids = jnp.concatenate([subgrid_ref[pl.ds(block, 1), :] for block in blocks], axis=1)
    slots = down(slot_of(subgrids, lax.axis_index("c"), cores, owned))
    near, far = (onehot(slots, 0, half), onehot(slots, half, half))
    tiles = pixels // 128
    width = 256

    def rows_of(cells):
        held = (near_ref[:, :, cells].reshape(half, width), far_ref[:, :, cells].reshape(half, width))
        return jnp.dot(near, held[0], preferred_element_type=F32) + jnp.dot(far, held[1], preferred_element_type=F32)

    for at in range(0, pixels, width):
        re, im = pl.ds(at, width), pl.ds(pixels + at, width)
        model_re, model_im = (rows_of(re), rows_of(im))
        screen_re, screen_im = (rows_of_blocks(screen_ref, blocks, re), rows_of_blocks(screen_ref, blocks, im))
        image_re = (screen_re * model_re - screen_im * model_im).astype(BF16)
        image_im = (screen_re * model_im + screen_im * model_re).astype(BF16)
        for off in range(0, width, 128):
            for image, q in ((image_re, (at + off) // 128), (image_im, (at + off) // 128 + tiles)):
                for j in range(len(blocks)):
                    image_refs[j // n_h][j % n_h, 16 * q : 16 * q + 16, :] = image[
                        16 * j : 16 * j + 16, off : off + 128
                    ]


def sum_kernel(*refs):
    pieces, sums = (refs[:-2], refs[-2:])
    for flip, sum_ref in enumerate(sums):
        total = pieces[0][flip].astype(F32)
        for piece in pieces[1:]:
            total = total + piece[flip].astype(F32)
        sum_ref[...] = total


def route_kernel(n_y, n_h, reader_ref, rows_ref, other_ref, pick_ref, *out_refs):
    at_y, at_h = (lax.axis_index("y"), lax.axis_index("h"))
    own = at_y * n_h + at_h
    source = reader_ref[0, own]
    steps = lax.rem(at_y + n_y - lax.div(source, n_h), n_y)
    here = jnp.where(lax.rem(source, n_h) == at_h, 0, 1)
    pick_ref[...] = jnp.full(pick_ref.shape, jnp.where(steps == 0, here, steps + 1), jnp.int32)
    block = jnp.int32(0)
    for at in range(n_y * n_h):
        block = jnp.where(reader_ref[0, at] == own, at, block)
    for by, out_ref in enumerate(out_refs, 1):
        to = lax.rem(at_y + by, n_y) * n_h + at_h

        @pl.when(block == to)
        def _():
            out_ref[...] = rows_ref[...]

        @pl.when(block != to)
        def _():
            out_ref[...] = other_ref[...]


def degrid_kernel(near_ref, far_ref, east_ref, north_ref, predicted_ref, cells_ref):
    rows, channels = (predicted_ref.shape[0], predicted_ref.shape[1] // 2)
    cells_ref[...] = near_ref[...] + far_ref[...]
    width = 256

    def degrid(b):
        cells = cells_ref[pl.ds(b, 16, stride=16), :]

        def spread(first, second):
            return jnp.concatenate(
                [
                    jnp.concatenate([first[:, 32 * p : 32 * p + 32], second[:, 32 * p : 32 * p + 32]], axis=1)
                    for p in range(4)
                ],
                axis=0,
            )

        image = jnp.concatenate([spread(cells[0:8], -cells[8:16]), spread(cells[8:16], cells[0:8])], axis=0)
        high = image.astype(BF16)
        low = (image - high.astype(F32)).astype(BF16)
        for at in range(0, channels, width):
            chans = pl.ds(at, width)
            north = north_ref[b, :, chans]
            inner = jnp.dot(high, north, preferred_element_type=F32) + jnp.dot(low, north, preferred_element_type=F32)
            inner_re, inner_im = (inner[:32], inner[32:])
            east = east_ref[b, :, chans].astype(F32)
            cos, sin = (east[:32], east[32:])
            vis_re = jnp.sum(cos * inner_re - sin * inner_im, axis=0, keepdims=True)
            vis_im = jnp.sum(cos * inner_im + sin * inner_re, axis=0, keepdims=True)
            row = pl.ds(b, 1)
            late = pl.ds(channels + at, width)
            predicted_ref[row, chans] = vis_re
            predicted_ref[row, late] = vis_im

    for b in range(rows):
        degrid(b)


def residual_kernel(pick_ref, *refs):
    found, (predicted_ref, resid_ref) = (refs[:-2], refs[-2:])
    for at in range(0, resid_ref.shape[1], 128):
        chans = pl.ds(at, 128)
        visible = found[0][:, chans].astype(F32)
        for which, ref in enumerate(found[1:], 1):
            visible = jnp.where(pick_ref[...] == which, ref[:, chans].astype(F32), visible)
        resid_ref[:, chans] = visible - predicted_ref[:, chans]


def grid_kernel(
    pick_ref,
    rows_ref,
    other_ref,
    came_1_ref,
    came_2_ref,
    came_3_ref,
    predicted_ref,
    east_ref,
    north_ref,
    grid_ref,
    out_ref,
    resid_ref,
):
    rows, channels = (resid_ref.shape[0], resid_ref.shape[1] // 2)
    residual_kernel(
        pick_ref, rows_ref, other_ref, came_1_ref, came_2_ref, came_3_ref, predicted_ref, resid_ref
    )
    width = 512

    def grid(b):
        products = jnp.zeros((64, 64), F32)
        for at in range(0, channels, width):
            chans, late = (pl.ds(at, width), pl.ds(channels + at, width))
            resid_re, resid_im = (resid_ref[pl.ds(b, 1), chans], resid_ref[pl.ds(b, 1), late])
            east = east_ref[b, :, chans].astype(F32)
            cos, sin = (east[:32], east[32:])
            weighted = jnp.concatenate([cos * resid_re + sin * resid_im, cos * resid_im - sin * resid_re], axis=0)
            products = products + lax.dot_general(
                weighted.astype(BF16),
                north_ref[b, :, chans],
                (((1,), (1,)), ((), ())),
                preferred_element_type=F32,
            )
        halves = (products[:32, :32] + products[32:, 32:], products[32:, :32] - products[:32, 32:])
        out_ref[pl.ds(b, 16, stride=16), :] = jnp.concatenate(
            [jnp.concatenate([half[8 * p : 8 * p + 8] for p in range(4)], axis=1) for half in halves], axis=0
        )

    for b in range(rows):
        grid(b)
    grid_ref[...] = out_ref[...].astype(BF16)


def regrid_kernel(scale, n_y, n_h, sizes, owned, other, subgrid_ref, screen_ref, *refs):
    grids, sum_ref = (refs[:-1], refs[-1])
    blocks = blocks_from(n_y, n_h, -1)
    half = sum_ref.shape[0]
    pixels = screen_ref.shape[1] // 2
    tiles = pixels // 128
    count = screen_ref.shape[0]

    def grid_of(q):
        return jnp.concatenate([ref[16 * q : 16 * q + 16, :] for ref in grids], axis=0).astype(F32)

    subs = lax.broadcasted_iota(jnp.int32, (half, count), 0) + other * half
    target = jnp.concatenate([subgrid_ref[pl.ds(block, 1), :] for block in blocks], axis=1)
    target = target_of(target, sizes, owned)
    sums = jnp.where(target == subs, 1.0, 0.0).astype(BF16)
    sums = jnp.concatenate([sums, sums], axis=1)
    for q in range(tiles):
        re, im = pl.ds(128 * q, 128), pl.ds(pixels + 128 * q, 128)
        grid_re, grid_im = (grid_of(q), grid_of(q + tiles))
        screen_re, screen_im = (rows_of_blocks(screen_ref, blocks, re), rows_of_blocks(screen_ref, blocks, im))
        out_re = (screen_re * grid_re + screen_im * grid_im) * scale
        out_im = (screen_re * grid_im - screen_im * grid_re) * scale
        value = jnp.concatenate([out_re, out_im], axis=1)
        high = value.astype(BF16)
        low = (value - high.astype(F32)).astype(BF16)
        both = jnp.dot(sums, jnp.concatenate([high, low], axis=0), preferred_element_type=F32)
        sum_ref[:, re] = both[:, :128].astype(sum_ref.dtype)
        sum_ref[:, im] = both[:, 128:].astype(sum_ref.dtype)


def pair(value, axis, by):
    return lax.ppermute(value, axis, [(i, i ^ by) for i in range(lax.axis_size(axis))])


def shift(value, axis, by):
    size = lax.axis_size(axis)
    return lax.ppermute(value, axis, [(i, (i + by) % size) for i in range(size)])


def far_first(size):
    return sorted(range(1, size), key=lambda by: -min(by, size - by))


def local(
    sectioned_rows,
    reader,
    baseline_coords,
    subgrid_index,
    stations,
    plane_index,
    model_grid,
    beam_screens,
    plane_phase,
    channel_freq,
):
    n_y, n_h, n_x, n_z, n_c = (lax.axis_size(axis) for axis in FACET + TILE)
    n_facet = n_y * n_h
    channels = channel_freq.shape[0]
    pixels = plane_phase.shape[1]
    row_block = sectioned_rows.shape[1]
    count = n_facet * row_block
    owned = model_grid.shape[1]
    subgrid_count = owned * n_x * n_z * n_c
    cell_rows = 2 * pixels // 128 * row_block
    grid_scale = 1.0 / math.sqrt(channels * n_facet * (row_block * n_x * n_z * n_c) / subgrid_count)
    with jax.named_scope("model_gather"):
        copies = pl.pallas_call(
            repeat_kernel,
            out_shape=jax.ShapeDtypeStruct((n_x * n_z, owned, 2 * pixels), BF16),
            in_specs=[VMEM],
            out_specs=VMEM,
            compiler_params=params(61),
            cost_estimate=pl.CostEstimate(flops=0, bytes_accessed=1 << 18, transcendentals=0),
            name="repeat",
        )(model_grid)
        near = lax.all_to_all(copies, ("x", "z"), split_axis=0, concat_axis=0, tiled=True)

    operands = (stations, plane_index, plane_phase, beam_screens[0])
    screen = pl.pallas_call(
        screen_kernel,
        out_shape=jax.ShapeDtypeStruct((count, 2 * pixels), F32),
        in_specs=[ANY] * len(operands),
        out_specs=VMEM,
        scratch_shapes=[pltpu.VMEM(value.shape, value.dtype) for value in operands]
        + [pltpu.SemaphoreType.DMA((len(operands),))],
        compiler_params=params(44),
        cost_estimate=pl.CostEstimate(flops=10**9, bytes_accessed=4 << 20, transcendentals=1 << 16),
        name="screens",
    )(*operands)

    def table(kind, coords):
        return pl.pallas_call(
            functools.partial(table_kernel, n_h, kind),
            out_shape=jax.ShapeDtypeStruct((row_block, 64, channels), BF16),
            in_specs=[VMEM] * 2,
            out_specs=VMEM,
            scratch_shapes=[
                pltpu.VMEM((10, row_block, channels), F32),
                pltpu.VMEM((8, row_block, channels), F32),
            ],
            compiler_params=params(16),
            cost_estimate=pl.CostEstimate(flops=10**9, bytes_accessed=4 << 20, transcendentals=1 << 16),
            name=("east", "north")[kind],
        )(coords, channel_freq.reshape(1, channels))

    north = table(1, baseline_coords)
    near, screen, north = lax.optimization_barrier((near, screen, north))
    far = shift(near, "c", 1)
    images = pl.pallas_call(
        functools.partial(image_kernel, n_y, n_h, n_c, owned),
        out_shape=[jax.ShapeDtypeStruct((n_h, cell_rows, 128), BF16)] * n_y,
        in_specs=[VMEM] * 4,
        out_specs=[VMEM] * n_y,
        compiler_params=params(8),
        cost_estimate=pl.CostEstimate(flops=10**8, bytes_accessed=2 << 20, transcendentals=0),
        name="images",
    )(subgrid_index, near, far, screen)
    rows, *images = lax.optimization_barrier((sectioned_rows[0], *images))

    with jax.named_scope("visible_route"):
        other = shift(rows, "h", 1)
        pick, *sent = pl.pallas_call(
            functools.partial(route_kernel, n_y, n_h),
            out_shape=[jax.ShapeDtypeStruct((row_block, 128), jnp.int32)]
            + [jax.ShapeDtypeStruct(rows.shape, BF16)] * (n_y - 1),
            in_specs=[SMEM, VMEM, VMEM],
            out_specs=[VMEM] * n_y,
            compiler_params=params(4),
            cost_estimate=pl.CostEstimate(flops=10**6, bytes_accessed=1 << 18, transcendentals=0),
            name="route",
        )(reader, rows, other)

    with jax.named_scope("image_sum"):
        pieces = [images[0]] + [shift(images[by], "y", by) for by in far_first(n_y)]
        own_sum, other_sum = pl.pallas_call(
            sum_kernel,
            out_shape=[jax.ShapeDtypeStruct((cell_rows, 128), F32)] * 2,
            in_specs=[VMEM] * n_y,
            out_specs=[VMEM] * 2,
            compiler_params=params(4),
            cost_estimate=pl.CostEstimate(flops=10**6, bytes_accessed=1 << 20, transcendentals=0),
            name="image_sums",
        )(*pieces)
        later, own_sum = lax.optimization_barrier((baseline_coords, own_sum))
        beside_sum = shift(other_sum, "h", 1)

    east = table(0, later)
    came = dict((by, shift(sent[by - 1], "y", by)) for by in far_first(n_y))
    came = [came[by] for by in range(1, n_y)]

    predicted = pl.pallas_call(
        degrid_kernel,
        out_shape=jax.ShapeDtypeStruct((row_block, 2 * channels), F32),
        in_specs=[VMEM] * 4,
        out_specs=VMEM,
        scratch_shapes=[pltpu.VMEM((cell_rows, 128), F32)],
        compiler_params=params(16),
        cost_estimate=pl.CostEstimate(flops=10**9, bytes_accessed=5 << 20, transcendentals=0),
        name="degrid",
    )(own_sum, beside_sum, east, north)

    operands = (pick, rows, other, *came, predicted)
    gridded = pl.pallas_call(
        grid_kernel,
        out_shape=jax.ShapeDtypeStruct((cell_rows, 128), BF16),
        in_specs=[VMEM] * 9,
        out_specs=VMEM,
        scratch_shapes=[pltpu.VMEM((cell_rows, 128), F32), pltpu.VMEM(predicted.shape, F32)],
        compiler_params=params(16),
        cost_estimate=pl.CostEstimate(flops=10**9, bytes_accessed=5 << 20, transcendentals=0),
        name="grid",
    )(*operands, east, north)

    with jax.named_scope("grid_gather"):
        beside = shift(gridded, "h", 1)
        moved = dict((by, (shift(gridded, "y", by), shift(beside, "y", by))) for by in reversed(far_first(n_y)))
        grids = [gridded, beside]
        for by in range(1, n_y):
            grids += moved[by]

    first, *operands = operands
    first, grids[1] = lax.optimization_barrier((first, grids[1]))
    residual = pl.pallas_call(
        residual_kernel,
        out_shape=jax.ShapeDtypeStruct(predicted.shape, F32),
        in_specs=[VMEM] * 7,
        out_specs=VMEM,
        compiler_params=params(4),
        cost_estimate=pl.CostEstimate(flops=10**6, bytes_accessed=1 << 19, transcendentals=0),
        name="residual",
    )(first, *operands)

    half = subgrid_count // n_c

    def regrid(other, subgrids):
        return pl.pallas_call(
            functools.partial(regrid_kernel, grid_scale, n_y, n_h, (n_x, n_z, n_c), owned, other),
            out_shape=jax.ShapeDtypeStruct((half, 2 * pixels), (F32, BF16)[other]),
            in_specs=[VMEM] * (2 + n_facet),
            out_specs=VMEM,
            compiler_params=params(8),
            cost_estimate=pl.CostEstimate(flops=10**8, bytes_accessed=3 << 20, transcendentals=0),
            name=("regrid_near", "regrid_far")[other],
        )(subgrids, screen, *grids)

    subgrids, residual = lax.optimization_barrier((subgrid_index, residual))
    far_sum = regrid(1, subgrids)
    subgrids, far_sum = lax.optimization_barrier((subgrid_index, far_sum))
    near_sum = regrid(0, subgrids)

    with jax.named_scope("dirty_scatter"):
        far_sum = shift(far_sum, "c", 1)

        def call(kernel, name, shapes, *operands):
            return pl.pallas_call(
                kernel,
                out_shape=shapes,
                in_specs=[VMEM] * len(operands),
                out_specs=[VMEM] * len(shapes),
                compiler_params=params(4),
                cost_estimate=pl.CostEstimate(flops=10**6, bytes_accessed=1 << 20, transcendentals=0),
                name=name,
            )(*operands)

        column = (n_z * owned, 2 * pixels)
        own, *sent = call(
            chip_kernel,
            "chip_sums",
            [jax.ShapeDtypeStruct(column, F32)] + [jax.ShapeDtypeStruct(column, BF16)] * (n_x - 1),
            near_sum,
            far_sum,
        )
        sent = [shift(sent[by - 1], "x", by) for by in far_first(n_x)]
        own, *sent = call(
            column_kernel, "column_sums", [jax.ShapeDtypeStruct((owned, 2 * pixels), F32)] * n_z, own, *sent
        )
        sent = [pair(sent[by - 1], "z", by) for by in reversed(range(1, n_z))]
        (dirty,) = call(total_kernel, "total", [jax.ShapeDtypeStruct(own.shape, F32)], own, *sent)
    return (residual[None], dirty[None])


def solution(mesh):
    split = Mesh(mesh.devices.reshape(4, 2, 4, 4, 2), FACET + TILE)
    return jax.shard_map(
        local,
        mesh=split,
        in_specs=(
            P(FACET, TILE, None),
            P(TILE, None),
            P(None, None, TILE),
            P(None, TILE),
            P(None, None, TILE),
            P(None, TILE),
            P(FACET, TILE, None),
            P(FACET, None, None),
            P(),
            P(),
        ),
        out_specs=(P(FACET, TILE, None), P(FACET, TILE, None)),
        check_vma=False,
    )
```

```python
import functools
import math

import jax
import jax.numpy as jnp
from jax import lax
from jax.experimental import pallas as pl
from jax.experimental.pallas import tpu as pltpu
from jax.sharding import Mesh
from jax.sharding import PartitionSpec as P

TWO_PI = 2.0 * math.pi
F32 = jnp.float32
BF16 = jnp.bfloat16
FACET = ("y", "h")
TILE = ("x", "z", "c")
VMEM = pl.BlockSpec(memory_space=pltpu.VMEM)
SMEM = pl.BlockSpec(memory_space=pltpu.SMEM)
ANY = pl.BlockSpec(memory_space=pl.ANY)


def params(mib):
    return pltpu.CompilerParams(vmem_limit_bytes=mib << 20)


def cmul(a, b):
    return (a[0] * b[0] - a[1] * b[1], a[0] * b[1] + a[1] * b[0])


def conj(a):
    return (a[0], -a[1])


def repeat_kernel(rows_ref, copies_ref):
    for at in range(copies_ref.shape[0]):
        copies_ref[at] = rows_ref[0]


def row_of_blocks(values):
    return jnp.concatenate([values[at : at + 1, :] for at in range(values.shape[0])], axis=1)


def down(row):
    return jnp.broadcast_to(row, (128, 128)).T


def onehot(column, first, count):
    lanes = lax.broadcasted_iota(jnp.int32, (128, 128), 1)
    width = min(count, 128)
    parts = [
        jnp.where(column == lanes + (first + at), 1.0, 0.0).astype(BF16)[:, :width] for at in range(0, count, 128)
    ]
    return parts[0] if len(parts) == 1 else jnp.concatenate(parts, axis=1)


def slot_of(subgrid, core, cores, owned):
    held = lax.rem(lax.div(subgrid, owned) + (cores - core), cores)
    return (held * (128 // cores)) + lax.div(subgrid, owned * cores) * owned + lax.rem(subgrid, owned)


def table_kernel(n_h, kind, coords_ref, freq_ref, table_ref, powers, groups):
    rows = coords_ref.shape[2]
    coords = coords_ref[lax.axis_index("y") * n_h + lax.axis_index("h")]
    row = jnp.concatenate([coords[kind : kind + 1], jnp.zeros((1, 128 - rows), F32)], axis=1)
    column = (TWO_PI * down(row)[:rows]) * (1.0 / 32.0)
    angle = jnp.concatenate([column] * (freq_ref.shape[1] // 128), axis=1) * freq_ref[...]
    z1 = (jnp.cos(angle), jnp.sin(angle))
    z2 = cmul(z1, z1)
    z4 = cmul(z2, z2)
    z8 = cmul(z4, z4)
    z16 = cmul(z8, z8)
    low16 = conj(z16)
    for at, value in enumerate((z1, z2, z4, z8, z16)):
        powers[2 * at] = value[0]
        powers[2 * at + 1] = value[1]
    for at, value in enumerate((low16, cmul(low16, z1), cmul(low16, z2), cmul(low16, cmul(z1, z2)))):
        groups[2 * at] = value[0]
        groups[2 * at + 1] = value[1]
    sub = lax.broadcasted_iota(jnp.int32, (8, angle.shape[1]), 0)

    def row_of(ref, at, row):
        return (ref[2 * at, pl.ds(row, 1), :], ref[2 * at + 1, pl.ds(row, 1), :])

    def picked(factor, bit):
        on = (sub & bit) != 0
        return (jnp.where(on, factor[0], 1.0), jnp.where(on, factor[1], 0.0))

    def bits(factors):
        return cmul(cmul(picked(factors[0], 1), picked(factors[1], 2)), picked(factors[2], 4))

    def stacked(parts):
        return jnp.concatenate([part[0] for part in parts] + [part[1] for part in parts], axis=0).astype(BF16)

    def body(b):
        base = bits([row_of(powers, at, b) for at in ((2, 3, 4), (0, 1, 2))[kind]])
        if kind == 0:
            table_ref[b] = stacked([cmul(base, row_of(groups, at, b)) for at in range(4)])
        else:
            up8 = row_of(powers, 3, b)
            table_ref[b] = stacked([cmul(base, row_of(groups, 0, b)), cmul(base, conj(up8)), base, cmul(base, up8)])

    for b in range(rows):
        body(b)


def target_of(subgrid, sizes, owned):
    n_x, n_z, n_c = sizes
    row, rest = (lax.rem(subgrid, owned), lax.div(subgrid, owned))
    core, rest = (lax.rem(rest, n_c), lax.div(rest, n_c))
    x = lax.bitwise_xor(lax.div(rest, n_z), jnp.full_like(rest, lax.axis_index("x")))
    z = lax.bitwise_xor(lax.rem(rest, n_z), jnp.full_like(rest, lax.axis_index("z")))
    core = lax.rem(core + n_c - lax.axis_index("c"), n_c)
    return ((core * n_x + x) * n_z + z) * owned + row


def chip_kernel(near_ref, far_ref, own_ref, *send_refs):
    rows = own_ref.shape[0]
    own_ref[...] = near_ref[:rows] + far_ref[:rows].astype(F32)
    for at, ref in enumerate(send_refs, 1):
        part = pl.ds(at * rows, rows)
        ref[...] = (near_ref[part] + far_ref[part].astype(F32)).astype(BF16)


def column_kernel(own_ref, *refs):
    came, outs = (refs[:3], refs[3:])
    total = own_ref[...]
    for ref in came:
        total = total + ref[...].astype(F32)
    rows = outs[0].shape[0]
    for at, ref in enumerate(outs):
        ref[...] = total[at * rows : at * rows + rows]


def total_kernel(*refs):
    total = refs[0][...]
    for ref in refs[1:-1]:
        total = total + ref[...]
    refs[-1][...] = total


def screen_kernel(stations_from, plane_from, phase_from, beam_from, screen_ref, *refs):
    sources, held, sems = ((stations_from, plane_from, phase_from, beam_from), refs[:4], refs[4])
    copies = [pltpu.make_async_copy(src, dst, sems.at[at]) for at, (src, dst) in enumerate(zip(sources, held))]
    for copy in copies:
        copy.start()
    stations_ref, plane_ref, phase_ref, beam_ref = held
    for copy in copies:
        copy.wait()
    stations = beam_ref.shape[0]
    planes, pixels = phase_ref.shape
    one = onehot(down(row_of_blocks(stations_ref[:, 0, :])), 0, stations)
    two = onehot(down(row_of_blocks(stations_ref[:, 1, :])), 0, stations)
    plane = onehot(down(row_of_blocks(plane_ref[...])), 0, planes).astype(F32)
    width = 256
    for at in range(0, pixels, width):
        re, im = pl.ds(at, width), pl.ds(pixels + at, width)
        one_re = jnp.dot(one, beam_ref[:, re], preferred_element_type=F32)
        one_im = jnp.dot(one, beam_ref[:, im], preferred_element_type=F32)
        two_re = jnp.dot(two, beam_ref[:, re], preferred_element_type=F32)
        two_im = jnp.dot(two, beam_ref[:, im], preferred_element_type=F32)
        pair_re = one_re * two_re + one_im * two_im
        pair_im = one_im * two_re - one_re * two_im
        phase = phase_ref[:, re]
        exact = lax.Precision.HIGHEST
        wave_re = jnp.dot(plane, jnp.cos(phase), precision=exact, preferred_element_type=F32)
        wave_im = jnp.dot(plane, jnp.sin(phase), precision=exact, preferred_element_type=F32)
        screen_ref[:, re] = pair_re * wave_re - pair_im * wave_im
        screen_ref[:, im] = pair_re * wave_im + pair_im * wave_re


def blocks_from(n_y, n_h, sign):
    at_y, at_h = (lax.axis_index("y"), lax.axis_index("h"))
    return [
        lax.bitwise_xor(at_y, jnp.int32(by)) * n_h + lax.rem(at_h + flip, n_h)
        for by in range(n_y)
        for flip in range(n_h)
    ]


def rows_of_blocks(ref, blocks, cells):
    return jnp.concatenate([ref[pl.ds(pl.multiple_of(block * 16, 16), 16), cells] for block in blocks], axis=0)


def image_kernel(n_y, n_h, cores, owned, subgrid_ref, near_ref, far_ref, screen_ref, *image_refs):
    half = near_ref.shape[0] * near_ref.shape[1]
    pixels = screen_ref.shape[1] // 2
    blocks = blocks_from(n_y, n_h, 1)
    subgrids = jnp.concatenate([subgrid_ref[pl.ds(block, 1), :] for block in blocks], axis=1)
    slots = down(slot_of(subgrids, lax.axis_index("c"), cores, owned))
    near, far = (onehot(slots, 0, half), onehot(slots, half, half))
    tiles = pixels // 128
    width = 256

    def rows_of(cells):
        held = (near_ref[:, :, cells].reshape(half, width), far_ref[:, :, cells].reshape(half, width))
        return jnp.dot(near, held[0], preferred_element_type=F32) + jnp.dot(far, held[1], preferred_element_type=F32)

    for at in range(0, pixels, width):
        re, im = pl.ds(at, width), pl.ds(pixels + at, width)
        model_re, model_im = (rows_of(re), rows_of(im))
        screen_re, screen_im = (rows_of_blocks(screen_ref, blocks, re), rows_of_blocks(screen_ref, blocks, im))
        image_re = (screen_re * model_re - screen_im * model_im).astype(BF16)
        image_im = (screen_re * model_im + screen_im * model_re).astype(BF16)
        for off in range(0, width, 128):
            for image, q in ((image_re, (at + off) // 128), (image_im, (at + off) // 128 + tiles)):
                for j in range(len(blocks)):
                    image_refs[j // n_h][j % n_h, 16 * q : 16 * q + 16, :] = image[
                        16 * j : 16 * j + 16, off : off + 128
                    ]


def sum_kernel(*refs):
    pieces, sums = (refs[:-2], refs[-2:])
    for flip, sum_ref in enumerate(sums):
        total = pieces[0][flip].astype(F32)
        for piece in pieces[1:]:
            total = total + piece[flip].astype(F32)
        sum_ref[...] = total


def route_kernel(n_y, n_h, reader_ref, rows_ref, other_ref, pick_ref, *out_refs):
    at_y, at_h = (lax.axis_index("y"), lax.axis_index("h"))
    own = at_y * n_h + at_h
    source = reader_ref[0, own]
    steps = lax.bitwise_xor(at_y, lax.div(source, n_h))
    here = jnp.where(lax.rem(source, n_h) == at_h, 0, 1)
    pick_ref[...] = jnp.full(pick_ref.shape, jnp.where(steps == 0, here, steps + 1), jnp.int32)
    block = jnp.int32(0)
    for at in range(n_y * n_h):
        block = jnp.where(reader_ref[0, at] == own, at, block)
    for by, out_ref in enumerate(out_refs, 1):
        to = lax.bitwise_xor(at_y, jnp.int32(by)) * n_h + at_h

        @pl.when(block == to)
        def _():
            out_ref[...] = rows_ref[...]

        @pl.when(block != to)
        def _():
            out_ref[...] = other_ref[...]


def degrid_kernel(near_ref, far_ref, east_ref, north_ref, predicted_ref, cells_ref):
    rows, channels = (predicted_ref.shape[0], predicted_ref.shape[1] // 2)
    cells_ref[...] = near_ref[...] + far_ref[...]
    width = 256

    def degrid(b):
        cells = cells_ref[pl.ds(b, 16, stride=16), :]

        def spread(first, second):
            return jnp.concatenate(
                [
                    jnp.concatenate([first[:, 32 * p : 32 * p + 32], second[:, 32 * p : 32 * p + 32]], axis=1)
                    for p in range(4)
                ],
                axis=0,
            )

        image = jnp.concatenate([spread(cells[0:8], -cells[8:16]), spread(cells[8:16], cells[0:8])], axis=0)
        high = image.astype(BF16)
        low = (image - high.astype(F32)).astype(BF16)
        for at in range(0, channels, width):
            chans = pl.ds(at, width)
            north = north_ref[b, :, chans]
            inner = jnp.dot(high, north, preferred_element_type=F32) + jnp.dot(low, north, preferred_element_type=F32)
            inner_re, inner_im = (inner[:32], inner[32:])
            east = east_ref[b, :, chans].astype(F32)
            cos, sin = (east[:32], east[32:])
            vis_re = jnp.sum(cos * inner_re - sin * inner_im, axis=0, keepdims=True)
            vis_im = jnp.sum(cos * inner_im + sin * inner_re, axis=0, keepdims=True)
            row = pl.ds(b, 1)
            late = pl.ds(channels + at, width)
            predicted_ref[row, chans] = vis_re
            predicted_ref[row, late] = vis_im

    for b in range(rows):
        degrid(b)


def residual_kernel(pick_ref, *refs):
    found, (predicted_ref, resid_ref) = (refs[:-2], refs[-2:])
    for at in range(0, resid_ref.shape[1], 128):
        chans = pl.ds(at, 128)
        visible = found[0][:, chans].astype(F32)
        for which, ref in enumerate(found[1:], 1):
            visible = jnp.where(pick_ref[...] == which, ref[:, chans].astype(F32), visible)
        resid_ref[:, chans] = visible - predicted_ref[:, chans]


def grid_kernel(
    pick_ref,
    rows_ref,
    other_ref,
    came_1_ref,
    came_2_ref,
    came_3_ref,
    predicted_ref,
    east_ref,
    north_ref,
    grid_ref,
    out_ref,
    resid_ref,
):
    rows, channels = (resid_ref.shape[0], resid_ref.shape[1] // 2)
    residual_kernel(
        pick_ref, rows_ref, other_ref, came_1_ref, came_2_ref, came_3_ref, predicted_ref, resid_ref
    )
    width = 512

    def grid(b):
        products = jnp.zeros((64, 64), F32)
        for at in range(0, channels, width):
            chans, late = (pl.ds(at, width), pl.ds(channels + at, width))
            resid_re, resid_im = (resid_ref[pl.ds(b, 1), chans], resid_ref[pl.ds(b, 1), late])
            east = east_ref[b, :, chans].astype(F32)
            cos, sin = (east[:32], east[32:])
            weighted = jnp.concatenate([cos * resid_re + sin * resid_im, cos * resid_im - sin * resid_re], axis=0)
            products = products + lax.dot_general(
                weighted.astype(BF16),
                north_ref[b, :, chans],
                (((1,), (1,)), ((), ())),
                preferred_element_type=F32,
            )
        halves = (products[:32, :32] + products[32:, 32:], products[32:, :32] - products[:32, 32:])
        out_ref[pl.ds(b, 16, stride=16), :] = jnp.concatenate(
            [jnp.concatenate([half[8 * p : 8 * p + 8] for p in range(4)], axis=1) for half in halves], axis=0
        )

    for b in range(rows):
        grid(b)
    grid_ref[...] = out_ref[...].astype(BF16)


def regrid_kernel(scale, n_y, n_h, sizes, owned, other, subgrid_ref, screen_ref, *refs):
    grids, sum_ref = (refs[:-1], refs[-1])
    blocks = blocks_from(n_y, n_h, -1)
    half = sum_ref.shape[0]
    pixels = screen_ref.shape[1] // 2
    tiles = pixels // 128
    count = screen_ref.shape[0]

    def grid_of(q):
        return jnp.concatenate([ref[16 * q : 16 * q + 16, :] for ref in grids], axis=0).astype(F32)

    subs = lax.broadcasted_iota(jnp.int32, (half, count), 0) + other * half
    target = jnp.concatenate([subgrid_ref[pl.ds(block, 1), :] for block in blocks], axis=1)
    target = target_of(target, sizes, owned)
    sums = jnp.where(target == subs, 1.0, 0.0).astype(BF16)
    sums = jnp.concatenate([sums, sums], axis=1)
    for q in range(tiles):
        re, im = pl.ds(128 * q, 128), pl.ds(pixels + 128 * q, 128)
        grid_re, grid_im = (grid_of(q), grid_of(q + tiles))
        screen_re, screen_im = (rows_of_blocks(screen_ref, blocks, re), rows_of_blocks(screen_ref, blocks, im))
        out_re = (screen_re * grid_re + screen_im * grid_im) * scale
        out_im = (screen_re * grid_im - screen_im * grid_re) * scale
        value = jnp.concatenate([out_re, out_im], axis=1)
        high = value.astype(BF16)
        low = (value - high.astype(F32)).astype(BF16)
        both = jnp.dot(sums, jnp.concatenate([high, low], axis=0), preferred_element_type=F32)
        sum_ref[:, re] = both[:, :128].astype(sum_ref.dtype)
        sum_ref[:, im] = both[:, 128:].astype(sum_ref.dtype)


def pair(value, axis, by):
    return lax.ppermute(value, axis, [(i, i ^ by) for i in range(lax.axis_size(axis))])


def shift(value, axis, by):
    size = lax.axis_size(axis)
    return lax.ppermute(value, axis, [(i, (i + by) % size) for i in range(size)])


def far_first(size):
    return sorted(range(1, size), key=lambda by: -min(by, size - by))


def local(
    sectioned_rows,
    reader,
    baseline_coords,
    subgrid_index,
    stations,
    plane_index,
    model_grid,
    beam_screens,
    plane_phase,
    channel_freq,
):
    n_y, n_h, n_x, n_z, n_c = (lax.axis_size(axis) for axis in FACET + TILE)
    n_facet = n_y * n_h
    channels = channel_freq.shape[0]
    pixels = plane_phase.shape[1]
    row_block = sectioned_rows.shape[1]
    count = n_facet * row_block
    owned = model_grid.shape[1]
    subgrid_count = owned * n_x * n_z * n_c
    cell_rows = 2 * pixels // 128 * row_block
    grid_scale = 1.0 / math.sqrt(channels * n_facet * (row_block * n_x * n_z * n_c) / subgrid_count)
    with jax.named_scope("model_gather"):
        copies = pl.pallas_call(
            repeat_kernel,
            out_shape=jax.ShapeDtypeStruct((n_x * n_z, owned, 2 * pixels), BF16),
            in_specs=[VMEM],
            out_specs=VMEM,
            compiler_params=params(61),
            cost_estimate=pl.CostEstimate(flops=0, bytes_accessed=1 << 18, transcendentals=0),
            name="repeat",
        )(model_grid)
        near = lax.all_to_all(copies, ("x", "z"), split_axis=0, concat_axis=0, tiled=True)

    operands = (stations, plane_index, plane_phase, beam_screens[0])
    screen = pl.pallas_call(
        screen_kernel,
        out_shape=jax.ShapeDtypeStruct((count, 2 * pixels), F32),
        in_specs=[ANY] * len(operands),
        out_specs=VMEM,
        scratch_shapes=[pltpu.VMEM(value.shape, value.dtype) for value in operands]
        + [pltpu.SemaphoreType.DMA((len(operands),))],
        compiler_params=params(44),
        cost_estimate=pl.CostEstimate(flops=10**9, bytes_accessed=4 << 20, transcendentals=1 << 16),
        name="screens",
    )(*operands)

    def table(kind, coords):
        return pl.pallas_call(
            functools.partial(table_kernel, n_h, kind),
            out_shape=jax.ShapeDtypeStruct((row_block, 64, channels), BF16),
            in_specs=[VMEM] * 2,
            out_specs=VMEM,
            scratch_shapes=[
                pltpu.VMEM((10, row_block, channels), F32),
                pltpu.VMEM((8, row_block, channels), F32),
            ],
            compiler_params=params(16),
            cost_estimate=pl.CostEstimate(flops=10**9, bytes_accessed=4 << 20, transcendentals=1 << 16),
            name=("east", "north")[kind],
        )(coords, channel_freq.reshape(1, channels))

    north = table(1, baseline_coords)
    near, screen, north = lax.optimization_barrier((near, screen, north))
    far = shift(near, "c", 1)
    images = pl.pallas_call(
        functools.partial(image_kernel, n_y, n_h, n_c, owned),
        out_shape=[jax.ShapeDtypeStruct((n_h, cell_rows, 128), BF16)] * n_y,
        in_specs=[VMEM] * 4,
        out_specs=[VMEM] * n_y,
        compiler_params=params(8),
        cost_estimate=pl.CostEstimate(flops=10**8, bytes_accessed=2 << 20, transcendentals=0),
        name="images",
    )(subgrid_index, near, far, screen)
    rows, *images = lax.optimization_barrier((sectioned_rows[0], *images))

    with jax.named_scope("visible_route"):
        other = shift(rows, "h", 1)
        pick, *sent = pl.pallas_call(
            functools.partial(route_kernel, n_y, n_h),
            out_shape=[jax.ShapeDtypeStruct((row_block, 128), jnp.int32)]
            + [jax.ShapeDtypeStruct(rows.shape, BF16)] * (n_y - 1),
            in_specs=[SMEM, VMEM, VMEM],
            out_specs=[VMEM] * n_y,
            compiler_params=params(4),
            cost_estimate=pl.CostEstimate(flops=10**6, bytes_accessed=1 << 18, transcendentals=0),
            name="route",
        )(reader, rows, other)

    with jax.named_scope("image_sum"):
        pieces = [images[0]] + [pair(images[by], "y", by) for by in far_first(n_y)]
        own_sum, other_sum = pl.pallas_call(
            sum_kernel,
            out_shape=[jax.ShapeDtypeStruct((cell_rows, 128), F32)] * 2,
            in_specs=[VMEM] * n_y,
            out_specs=[VMEM] * 2,
            compiler_params=params(4),
            cost_estimate=pl.CostEstimate(flops=10**6, bytes_accessed=1 << 20, transcendentals=0),
            name="image_sums",
        )(*pieces)
        later, own_sum = lax.optimization_barrier((baseline_coords, own_sum))
        beside_sum = shift(other_sum, "h", 1)

    east = table(0, later)
    came = dict((by, pair(sent[by - 1], "y", by)) for by in far_first(n_y))
    came = [came[by] for by in range(1, n_y)]

    predicted = pl.pallas_call(
        degrid_kernel,
        out_shape=jax.ShapeDtypeStruct((row_block, 2 * channels), F32),
        in_specs=[VMEM] * 4,
        out_specs=VMEM,
        scratch_shapes=[pltpu.VMEM((cell_rows, 128), F32)],
        compiler_params=params(16),
        cost_estimate=pl.CostEstimate(flops=10**9, bytes_accessed=5 << 20, transcendentals=0),
        name="degrid",
    )(own_sum, beside_sum, east, north)

    operands = (pick, rows, other, *came, predicted)
    gridded = pl.pallas_call(
        grid_kernel,
        out_shape=jax.ShapeDtypeStruct((cell_rows, 128), BF16),
        in_specs=[VMEM] * 9,
        out_specs=VMEM,
        scratch_shapes=[pltpu.VMEM((cell_rows, 128), F32), pltpu.VMEM(predicted.shape, F32)],
        compiler_params=params(16),
        cost_estimate=pl.CostEstimate(flops=10**9, bytes_accessed=5 << 20, transcendentals=0),
        name="grid",
    )(*operands, east, north)

    with jax.named_scope("grid_gather"):
        beside = shift(gridded, "h", 1)
        moved = dict((by, (pair(gridded, "y", by), pair(beside, "y", by))) for by in reversed(far_first(n_y)))
        grids = [gridded, beside]
        for by in range(1, n_y):
            grids += moved[by]

    first, *operands = operands
    first, grids[1] = lax.optimization_barrier((first, grids[1]))
    residual = pl.pallas_call(
        residual_kernel,
        out_shape=jax.ShapeDtypeStruct(predicted.shape, F32),
        in_specs=[VMEM] * 7,
        out_specs=VMEM,
        compiler_params=params(4),
        cost_estimate=pl.CostEstimate(flops=10**6, bytes_accessed=1 << 19, transcendentals=0),
        name="residual",
    )(first, *operands)

    half = subgrid_count // n_c

    def regrid(other, subgrids):
        return pl.pallas_call(
            functools.partial(regrid_kernel, grid_scale, n_y, n_h, (n_x, n_z, n_c), owned, other),
            out_shape=jax.ShapeDtypeStruct((half, 2 * pixels), (F32, BF16)[other]),
            in_specs=[VMEM] * (2 + n_facet),
            out_specs=VMEM,
            compiler_params=params(8),
            cost_estimate=pl.CostEstimate(flops=10**8, bytes_accessed=3 << 20, transcendentals=0),
            name=("regrid_near", "regrid_far")[other],
        )(subgrids, screen, *grids)

    subgrids, residual = lax.optimization_barrier((subgrid_index, residual))
    far_sum = regrid(1, subgrids)
    subgrids, far_sum = lax.optimization_barrier((subgrid_index, far_sum))
    near_sum = regrid(0, subgrids)

    with jax.named_scope("dirty_scatter"):
        far_sum = shift(far_sum, "c", 1)

        def call(kernel, name, shapes, *operands):
            return pl.pallas_call(
                kernel,
                out_shape=shapes,
                in_specs=[VMEM] * len(operands),
                out_specs=[VMEM] * len(shapes),
                compiler_params=params(4),
                cost_estimate=pl.CostEstimate(flops=10**6, bytes_accessed=1 << 20, transcendentals=0),
                name=name,
            )(*operands)

        column = (n_z * owned, 2 * pixels)
        own, *sent = call(
            chip_kernel,
            "chip_sums",
            [jax.ShapeDtypeStruct(column, F32)] + [jax.ShapeDtypeStruct(column, BF16)] * (n_x - 1),
            near_sum,
            far_sum,
        )
        sent = [pair(sent[by - 1], "x", by) for by in far_first(n_x)]
        own, *sent = call(
            column_kernel, "column_sums", [jax.ShapeDtypeStruct((owned, 2 * pixels), F32)] * n_z, own, *sent
        )
        sent = [pair(sent[by - 1], "z", by) for by in reversed(range(1, n_z))]
        (dirty,) = call(total_kernel, "total", [jax.ShapeDtypeStruct(own.shape, F32)], own, *sent)
    return (residual[None], dirty[None])


def solution(mesh):
    split = Mesh(mesh.devices.reshape(4, 2, 4, 4, 2), FACET + TILE)
    return jax.shard_map(
        local,
        mesh=split,
        in_specs=(
            P(FACET, TILE, None),
            P(TILE, None),
            P(None, None, TILE),
            P(None, TILE),
            P(None, None, TILE),
            P(None, TILE),
            P(FACET, TILE, None),
            P(FACET, None, None),
            P(),
            P(),
        ),
        out_specs=(P(FACET, TILE, None), P(FACET, TILE, None)),
        check_vma=False,
    )
```
